32 devices in a mesh: grp: 2 (over x), rows: 16 (over z, y, core).
Axes of the slice: x: 2, y: 2, z: 4, core: 2. Of those that a mesh axis runs over, the one named last changes fastest.
Arguments:
- pixels: bfloat16 [4, 12, 3, 128, 128], P('grp', None, None, 'rows'), may hold values from -6 to 6
- cotangent: bfloat16 [4, 12, 3, 128, 128], P('grp', None, None, 'rows'), may hold values from -6 to 6
- embed_single: bfloat16 [300, 512], replicated, may hold values from -0.375 to 0.375
- embed_pair: bfloat16 [600, 512], replicated, may hold values from -0.25 to 0.25
- spatial_gain: bfloat16 [512], replicated, may hold values from 0.5 to 1.5
- spatial_heads: bfloat16 [512, 1536], replicated, may hold values from -0.25 to 0.25
- spatial_output: bfloat16 [512, 512], replicated, may hold values from -1.5 to 1.5
- spatial_scale: bfloat16 [512], replicated, may hold values from 0.5 to 1.5
- spatial_upward: bfloat16 [512, 2048], replicated, may hold values from -0.25 to 0.25
- spatial_down: bfloat16 [2048, 512], replicated, may hold values from -0.125 to 0.125
- temporal_gain: bfloat16 [512], replicated, may hold values from 0.5 to 1.5
- temporal_heads: bfloat16 [512, 1536], replicated, may hold values from -0.25 to 0.25
- temporal_output: bfloat16 [512, 512], replicated, may hold values from -0.375 to 0.375
- temporal_scale: bfloat16 [512], replicated, may hold values from 0.5 to 1.5
- temporal_upward: bfloat16 [512, 2048], replicated, may hold values from -0.25 to 0.25
- temporal_down: bfloat16 [2048, 512], replicated, may hold values from -0.125 to 0.125
- unpatch_single: bfloat16 [512, 300], replicated, may hold values from -0.25 to 0.25
- unpatch_pair: bfloat16 [512, 600], replicated, may hold values from -0.25 to 0.25
Outputs:
- rebuilt: float32 [4, 12, 3, 128, 128], P('grp', None, None, 'rows')
- pixel_gradient: float32 [4, 12, 3, 128, 128], P('grp', None, None, 'rows')
- embed_single_gradient: float32 [300, 512], P(None, 'grp')
- embed_pair_gradient: float32 [600, 512], P(None, 'grp')
- spatial_gain_gradient: float32 [512], P('grp')
- spatial_heads_gradient: float32 [512, 1536], P('grp')
- spatial_output_gradient: float32 [512, 512], P('grp')
- spatial_scale_gradient: float32 [512], P('grp')
- spatial_upward_gradient: float32 [512, 2048], P('grp')
- spatial_down_gradient: float32 [2048, 512], P(None, 'grp')
- temporal_gain_gradient: float32 [512], P('grp')
- temporal_heads_gradient: float32 [512, 1536], P('grp')
- temporal_output_gradient: float32 [512, 512], P('grp')
- temporal_scale_gradient: float32 [512], P('grp')
- temporal_upward_gradient: float32 [512, 2048], P('grp')
- temporal_down_gradient: float32 [2048, 512], P(None, 'grp')
- unpatch_single_gradient: float32 [512, 300], P('grp')
- unpatch_pair_gradient: float32 [512, 600], P('grp')
The draws below stay inside these ranges and needn't reach their ends.
All inputs are finite; a program needn't handle non-finite values.
Results may differ from the reference program's by a relative error of at most 0.025.
Values may be sent and summed in bfloat16 or wider, within the bound.
No kernel may reach another device: no remote copies, remote signals or barrier semaphores. Data moves between devices by JAX's collectives and lax.ppermute only.
A program may use at most 192 MiB of HBM per device.

```python
import jax
import jax.numpy as jnp
from jax import lax

D = 512
HEADS = 8
FF = 2048
CHAN = 3
STRIDE = 8
KERN = 10
GRID = 16
IMG = 128
FRAMES = 12
VSTEPS = 5
GROUPS = 4


def steps_of(key, shape, cuts, smallest, largest):
    level = 1.0
    for axis_at, parts in cuts:
        draws = jax.random.uniform(jax.random.fold_in(jax.random.fold_in(key, 6), axis_at), (parts,), jnp.float32, smallest / len(cuts), largest / len(cuts))
        level = level * jnp.repeat(jnp.exp(draws), shape[axis_at] // parts).reshape((-1,) + (1,) * (len(shape) - 1 - axis_at))
    return level


def noise(stream_key, dims, scale, reach, pieces=(), kind=jnp.bfloat16):
    drawn = jax.random.normal(stream_key, dims, jnp.float32) * scale
    if len(pieces) > 0:
        drawn = steps_of(stream_key, dims, pieces, -0.22, 0.18) * drawn
    return jnp.clip(drawn, min=-reach, max=reach).astype(kind)


def setup_inputs(seed: int = 0) -> dict:
    key_list = jax.random.split(jax.random.key(seed), 19)
    return {
        "pixels": noise(key_list[0], (GROUPS, FRAMES, CHAN, IMG, IMG), 1.0, 6.0, ((0, 2), (3, 16))),
        "cotangent": noise(key_list[1], (GROUPS, FRAMES, CHAN, IMG, IMG), 1.0, 6.0, ((0, 2), (3, 16))),
        "embed_single": noise(key_list[2], (CHAN * KERN * KERN, D), (CHAN * KERN * KERN) ** -0.5, 0.375),
        "embed_pair": noise(key_list[3], (2 * CHAN * KERN * KERN, D), (2 * CHAN * KERN * KERN) ** -0.5, 0.25),
        "spatial_gain": jnp.clip(1.0 + 0.1 * jax.random.normal(key_list[4], (D,), jnp.float32), 0.5, 1.5).astype(jnp.bfloat16),
        "spatial_heads": noise(key_list[5], (D, 3 * D), D ** -0.5, 0.25),
        "spatial_output": noise(key_list[6], (D, D), (D // 32) ** -0.5, 1.5),
        "spatial_scale": jnp.clip(1.0 + 0.1 * jax.random.normal(key_list[7], (D,), jnp.float32), 0.5, 1.5).astype(jnp.bfloat16),
        "spatial_upward": noise(key_list[8], (D, FF), D ** -0.5, 0.25),
        "spatial_down": noise(key_list[9], (FF, D), FF ** -0.5, 0.125),
        "temporal_gain": jnp.clip(1.0 + 0.1 * jax.random.normal(key_list[10], (D,), jnp.float32), 0.5, 1.5).astype(jnp.bfloat16),
        "temporal_heads": noise(key_list[11], (D, 3 * D), D ** -0.5, 0.25),
        "temporal_output": noise(key_list[12], (D, D), (D // 2) ** -0.5, 0.375),
        "temporal_scale": jnp.clip(1.0 + 0.1 * jax.random.normal(key_list[13], (D,), jnp.float32), 0.5, 1.5).astype(jnp.bfloat16),
        "temporal_upward": noise(key_list[14], (D, FF), D ** -0.5, 0.25),
        "temporal_down": noise(key_list[15], (FF, D), FF ** -0.5, 0.125),
        "unpatch_single": noise(key_list[16], (D, CHAN * KERN * KERN), D ** -0.5, 0.25),
        "unpatch_pair": noise(key_list[17], (D, 2 * CHAN * KERN * KERN), D ** -0.5, 0.25),
    }


epsilon = 1e-05
gelu_coef = 0.7978845608028654
cubic_coef = 0.044715
masked_score = -1000000000.0
highest = lax.Precision.HIGHEST

@jax.custom_vjp
def low(v):
    return lax.optimization_barrier(v.astype(jnp.bfloat16)).astype(jnp.float32)

@jax.custom_vjp
def low_back(v):
    return v

def low_keep(v):
    return (low(v), None)

def low_pass(kept, grad):
    return (grad,)

def back_keep(v):
    return (v, None)

def back_low(kept, grad):
    return (low(grad),)
low.defvjp(low_keep, low_pass)
low_back.defvjp(back_keep, back_low)

def cut_last(values, count):
    extra = jnp.pad(values, [(0, 0)] * (values.ndim - 1) + [(0, 2 * STRIDE - KERN)])
    main = extra[..., :STRIDE * count].reshape(values.shape[:-1] + (count, STRIDE))
    tail = extra[..., STRIDE:STRIDE * count + STRIDE].reshape(values.shape[:-1] + (count, STRIDE))
    return jnp.concatenate([main, tail[..., :KERN - STRIDE]], axis=-1)

def fold_last(windows, count):
    lead = windows.shape[:-2]
    main = windows[..., :STRIDE].reshape(lead + (count * STRIDE,))
    tail = jnp.pad(windows[..., STRIDE:], [(0, 0)] * (windows.ndim - 1) + [(0, 2 * STRIDE - KERN)])
    tail = tail.reshape(lead + (count * STRIDE,))
    edge = [(0, 0)] * (windows.ndim - 2)
    total = jnp.pad(main, edge + [(0, STRIDE)]) + jnp.pad(tail, edge + [(STRIDE, 0)])
    return total[..., :STRIDE * count + KERN - STRIDE]

def patches(padded, prows):
    wide = cut_last(jnp.pad(padded, [(0, 0)] * 4 + [(1, 1)]), GRID)
    tall = cut_last(jnp.moveaxis(wide, 3, 5), prows)
    tiles = jnp.transpose(tall, (0, 1, 5, 3, 2, 6, 4))
    shape = tiles.shape
    return tiles.reshape(shape[:2] + (prows * GRID, shape[4] * KERN * KERN))

def unpatch(frames, prows):
    shape = frames.shape
    tiles = frames.reshape(shape[:2] + (prows, GRID, shape[3] // (KERN * KERN), KERN, KERN))
    tall = fold_last(jnp.transpose(tiles, (0, 1, 4, 3, 6, 2, 5)), prows)
    wide = fold_last(jnp.moveaxis(tall, 5, 3), GRID)
    return wide[..., 1:-1]

def split_frames(windows):
    single = jnp.concatenate([windows[:, :1], windows[:, 2 * VSTEPS - 1:]], axis=1)
    pair = windows[:, 1:2 * VSTEPS - 1]
    shape = pair.shape
    pair = jnp.swapaxes(pair.reshape((shape[0], VSTEPS - 1, 2) + shape[2:]), 2, 3)
    return (single, pair.reshape((shape[0], VSTEPS - 1, shape[2], 2 * shape[3])))

def join_frames(single, pair):
    shape = pair.shape
    pair = jnp.swapaxes(pair.reshape(shape[:3] + (2, shape[3] // 2)), 2, 3)
    pair = pair.reshape((shape[0], 2 * shape[1], shape[2], shape[3] // 2))
    return jnp.concatenate([single[:, :1], pair, single[:, 1:]], axis=1)

def split_slots(tokens):
    return (jnp.concatenate([tokens[:, :1], tokens[:, VSTEPS:]], axis=1), tokens[:, 1:VSTEPS])

def join_slots(single, pair):
    return jnp.concatenate([single[:, :1], pair, single[:, 1:]], axis=1)

def slot_mask(count):
    slot = jnp.arange(count)
    clip = jnp.where(slot < VSTEPS, 0, slot - VSTEPS + 1)
    return (slot[None, :] <= slot[:, None]) & (clip[None, :] == clip[:, None])

def gelu(inner):
    return 0.5 * inner * (1.0 + jnp.tanh(gelu_coef * (inner + cubic_coef * inner * inner * inner)))

def layer_norm(resid, gain):
    centered = resid - lax.optimization_barrier(jnp.mean(resid, -1, keepdims=True))
    variance = lax.optimization_barrier(jnp.mean(centered * centered, -1, keepdims=True))
    return centered * lax.rsqrt(variance + epsilon) * gain

def mult(left, right):
    return jnp.matmul(left, right, precision=highest)

def split_heads(values):
    return values.reshape(values.shape[:-1] + (HEADS, values.shape[-1] // HEADS))

def softmax_rows(scores):
    top = lax.optimization_barrier(jnp.max(scores, -1, keepdims=True))
    powers = jnp.exp(scores - top)
    return powers / lax.optimization_barrier(jnp.sum(powers, -1, keepdims=True))

def spatial(queries, keys, values):
    scale = queries.shape[-1] ** (-0.5)
    scores = low_back(jnp.einsum('bsqhd,bskhd->bshqk', queries, keys, precision=highest) * scale)
    chance = low(softmax_rows(scores))
    mixed = jnp.einsum('bshqk,bskhd->bsqhd', chance, values, precision=highest)
    return mixed.reshape(mixed.shape[:3] + (-1,))

def temporal(queries, keys, values):
    scale = queries.shape[-1] ** (-0.5)
    scores = low_back(jnp.einsum('bsphd,btphd->bphst', queries, keys, precision=highest) * scale)
    scores = jnp.where(slot_mask(queries.shape[1]), scores, masked_score)
    chance = low(softmax_rows(scores))
    mixed = jnp.einsum('bphst,btphd->bsphd', chance, values, precision=highest)
    return mixed.reshape(mixed.shape[:3] + (-1,))

def block(resid, params, attend):
    gain, heads, output, scale, upward, down = params
    width = resid.shape[-1]
    normed = low(layer_norm(resid, gain))
    projected = low(low_back(mult(normed, heads)))
    mixed = low(low_back(attend(split_heads(projected[..., :width]), split_heads(projected[..., width:2 * width]), split_heads(projected[..., 2 * width:]))))
    resid = resid + low_back(mult(mixed, output))
    second = low(layer_norm(resid, scale))
    inner = low_back(mult(second, upward))
    return resid + low_back(mult(low(gelu(inner)), down))

def forward(image, params):
    padded = jnp.pad(image[None], ((0, 0), (0, 0), (0, 0), (1, 1), (0, 0)))
    single, pair = split_frames(patches(padded, GRID))
    resid = low_back(join_slots(mult(single, params[0]), mult(pair, params[1])))
    resid = block(resid, params[2:8], spatial)
    resid = block(resid, params[8:14], temporal)
    final_single, final_pair = split_slots(low(resid))
    frames = join_frames(mult(final_single, params[14]), mult(final_pair, params[15]))
    return unpatch(frames, GRID)[0, :, :, 1:-1]

def reference(pixels, cotangent, embed_single, embed_pair, spatial_gain, spatial_heads, spatial_output, spatial_scale, spatial_upward, spatial_down, temporal_gain, temporal_heads, temporal_output, temporal_scale, temporal_upward, temporal_down, unpatch_single, unpatch_pair):
    params = tuple((weight.astype(jnp.float32) for weight in (embed_single, embed_pair, spatial_gain, spatial_heads, spatial_output, spatial_scale, spatial_upward, spatial_down, temporal_gain, temporal_heads, temporal_output, temporal_scale, temporal_upward, temporal_down, unpatch_single, unpatch_pair)))

    def one_group(carry, item):
        image, grad_out = item
        rebuilt, pullback = jax.vjp(forward, image.astype(jnp.float32), params)
        grad_image, grad_params = pullback(grad_out.astype(jnp.float32))
        return (jax.tree.map(jnp.add, carry, grad_params), (rebuilt, grad_image))
    zeros = tuple((jnp.zeros(weight.shape, jnp.float32) for weight in params))
    totals, outputs = lax.scan(one_group, zeros, (pixels, cotangent))
    return (outputs[0], outputs[1], totals[0], totals[1], totals[2], totals[3], totals[4], totals[5], totals[6], totals[7], totals[8], totals[9], totals[10], totals[11], totals[12], totals[13], totals[14], totals[15])
```

```python
import functools

import jax
import jax.numpy as jnp
import numpy as np
from jax import lax
from jax.experimental import pallas as pl
from jax.experimental.pallas import tpu as pltpu
from jax.sharding import PartitionSpec as P

HEADS = 8
STRIDE = 8
KERN = 10
GRID = 16
VSTEPS = 5
CHAN = 3
LANES = 128

epsilon = 1e-05
gelu_coef = 0.7978845608028654
cubic_coef = 0.044715
masked_score = -1000000000.0

WIN = CHAN * KERN * KERN
CUTS = KERN * CHAN * STRIDE
SINGLE_FRAMES = (0, 9, 10, 11)
MIB = 1 << 20


def column_picks():
    n = np.arange(256)
    chan, bit = (n % 24) // 8, n % 8
    at = np.arange(CHAN * 128)
    return ((n < CUTS) & (at[:, None] // 128 == chan) & (at[:, None] % 8 == bit)).astype(jnp.bfloat16)


def window_picks(first, width):
    n = np.arange(256)
    row, chan, bit = n // 24, (n % 24) // 8, n % 8
    w = np.arange(width) - first
    hit = (w >= 0) & (w < WIN)
    same = hit & (n < CUTS)[:, None] & (chan[:, None] == w // 100) & (row[:, None] == (w % 100) // 10)
    step = w % 10
    own = same & (step == bit[:, None] + 1)
    before = same & (step == 0) & (bit[:, None] == 7)
    after = same & (step == 9) & (bit[:, None] == 0)
    return np.concatenate([own, before, after], 0).astype(jnp.bfloat16)


def frame_rows():
    order = (SINGLE_FRAMES, (1, 3, 5, 7), (2, 4, 6, 8))
    out = np.zeros((384, 32), np.float32)
    for k in range(3):
        for g in range(2):
            for i in range(4):
                at = ((k * 2 + g) * 4 + i) * 16
                out[at : at + 16, g * 12 + order[k][i]] = 1
    return out.astype(jnp.bfloat16)


def dot(a, b):
    return jnp.dot(a, b, preferred_element_type=jnp.float32)


def dot_nt(a, b):
    return lax.dot_general(a, b, (((1,), (1,)), ((), ())), preferred_element_type=jnp.float32)


def dot_tn(a, b):
    return lax.dot_general(a, b, (((0,), (0,)), ((), ())), preferred_element_type=jnp.float32)


def bf(x):
    return x.astype(jnp.bfloat16)


def f32(x):
    return x.astype(jnp.float32)


def iota(shape, dim):
    return lax.broadcasted_iota(jnp.int32, shape, dim)


def own_columns(rows):
    return ((iota((rows, 384), 1) & 127) >> 3) == (iota((rows, 384), 0) & 15)


def picks_of(picks, i):
    lane = iota((1, 256), 1)
    return picks * bf(jnp.where((lane >= 24 * i) & (lane < 24 * i + 24), 1.0, 0.0))


def shift_up(v):
    return jnp.where((iota(v.shape, 0) & 15) == 15, 0.0, pltpu.roll(v, v.shape[0] - 1, 0))


def shift_down(v):
    return jnp.where((iota(v.shape, 0) & 15) == 0, 0.0, pltpu.roll(v, 1, 0))


def widen(v):
    return bf(jnp.concatenate([v, shift_down(v), shift_up(v)], 1))


def narrow(t):
    return bf(t[:, :256] + shift_up(t[:, 256:512]) + shift_down(t[:, 512:]))


def normalize(x, gain):
    centered = x - jnp.mean(x, -1, keepdims=True)
    inverse = lax.rsqrt(jnp.mean(centered * centered, -1, keepdims=True) + epsilon)
    unit = centered * inverse
    return bf(unit * gain), unit, inverse


def normalize_back(incoming, unit, inverse, gain):
    scaled = incoming * gain
    gain_grad = jnp.sum(incoming * unit, 0, keepdims=True)
    first = jnp.mean(scaled, -1, keepdims=True)
    second = jnp.mean(scaled * unit, -1, keepdims=True)
    return inverse * (scaled - first - unit * second), gain_grad


def halves_mask(width=128):
    lane = iota((1, width), 1)
    return lane < 64


def attention(projected, seen, chance_ref, scale):
    low = halves_mask()
    keep = (bf(jnp.where(low, 1.0, 0.0)), bf(jnp.where(low, 0.0, 1.0)))
    outs = []
    for pair in range(HEADS // 2):
        q = projected[:, pair * 128 : pair * 128 + 128]
        k = projected[:, 512 + pair * 128 : 512 + pair * 128 + 128]
        v = projected[:, 1024 + pair * 128 : 1024 + pair * 128 + 128]
        both = []
        for half in range(2):
            scores = dot_nt(q * keep[half], k) * scale
            if seen is not None:
                scores = jnp.where(seen, scores, masked_score)
            powers = jnp.exp(scores - jnp.max(scores, -1, keepdims=True))
            chance = bf(powers * (1.0 / jnp.sum(powers, -1, keepdims=True)))
            chance_ref[2 * pair + half] = chance
            both.append(dot(chance, v))
        outs.append(jnp.where(low, both[0], both[1]))
    return bf(jnp.concatenate(outs, 1))


def attention_back(grad_mixed, projected, chance_ref, scale):
    low = halves_mask()
    keep = (bf(jnp.where(low, 1.0, 0.0)), bf(jnp.where(low, 0.0, 1.0)))
    grads = ([], [], [])
    for pair in range(HEADS // 2):
        q = projected[:, pair * 128 : pair * 128 + 128]
        k = projected[:, 512 + pair * 128 : 512 + pair * 128 + 128]
        v = projected[:, 1024 + pair * 128 : 1024 + pair * 128 + 128]
        g = grad_mixed[:, pair * 128 : pair * 128 + 128]
        both = ([], [], [])
        for half in range(2):
            chance = chance_ref[2 * pair + half]
            wide = f32(chance)
            grad_chance = dot_nt(g * keep[half], v)
            inner = jnp.sum(wide * grad_chance, -1, keepdims=True)
            grad_scores = bf(wide * (grad_chance - inner))
            both[0].append(dot(grad_scores, k))
            both[1].append(dot_tn(grad_scores, q))
            both[2].append(dot_tn(chance, g))
        for part, factor in zip(range(3), (scale, scale, 1.0)):
            grads[part].append(bf(jnp.where(low, both[part][0], both[part][1]) * factor))
    return jnp.concatenate(grads[0] + grads[1] + grads[2], 1)


def feed_forward(second, quarter, up_ref, down_ref, active_ref, slope_ref):
    total = None
    for rel in range(4):
        at = pl.multiple_of((quarter ^ rel) * 512, 512)
        inner = dot(second, up_ref[:, pl.ds(at, 512)])
        square = inner * inner
        bent = jnp.tanh(gelu_coef * inner * (1.0 + cubic_coef * square))
        half = 0.5 * (1.0 + bent)
        active = bf(inner * half)
        active_ref[:, rel * 512 : rel * 512 + 512] = active
        slope = half + 0.5 * inner * (1.0 - bent * bent) * gelu_coef * (1.0 + 3.0 * cubic_coef * square)
        slope_ref[:, rel * 512 : rel * 512 + 512] = bf(slope)
        part = dot(active, down_ref[pl.ds(at, 512), :])
        total = part if total is None else total + part
    return total


def feed_forward_back(lowered, quarter, up_ref, down_ref, slope_ref, grad_inner_ref):
    total = None
    for rel in range(4):
        at = pl.multiple_of((quarter ^ rel) * 512, 512)
        back = dot_nt(lowered, down_ref[pl.ds(at, 512), :])
        grad_inner = bf(back * f32(slope_ref[:, rel * 512 : rel * 512 + 512]))
        grad_inner_ref[:, rel * 512 : rel * 512 + 512] = grad_inner
        part = dot_nt(grad_inner, up_ref[:, pl.ds(at, 512)])
        total = part if total is None else total + part
    return total


def swap_halves(v, bit):
    half = v.shape[1] // 2
    return jnp.where(bit == 1, jnp.concatenate([v[:, half:], v[:, :half]], 1), v)


def swap_quarters(v, quarter):
    v = swap_halves(v, quarter >> 1)
    half = v.shape[1] // 2
    return jnp.concatenate([swap_halves(v[:, :half], quarter & 1), swap_halves(v[:, half:], quarter & 1)], 1)


def put_columns(outs, x_rel, at, value, count):
    rows, width = value.shape[0], value.shape[1] // 4
    for rel in range(4):
        for j in range(width // LANES):
            block = value[:, rel * width + j * LANES : rel * width + (j + 1) * LANES]
            outs[rel >> 1][x_rel, rel & 1, at + j * rows : at + (j + 1) * rows, :] = bf(block)


def put_rows(outs, x_rel, at, source, row0, rows, quarter):
    size = rows // 4
    blocks = source.shape[1] // LANES
    for rel in range(4):
        first = pl.multiple_of(row0 + (quarter ^ rel) * size, 16)
        for j in range(blocks):
            outs[rel >> 1][x_rel, rel & 1, at + j * size : at + (j + 1) * size, :] = bf(
                source[pl.ds(first, size), j * LANES : (j + 1) * LANES]
            )


def put_feed_forward(outs, second, grad_inner, active, lowered, mx):
    second = swap_halves(second, mx)
    lowered = swap_halves(lowered, mx)
    for rel in range(4):
        up = dot_tn(second, grad_inner[:, rel * 512 : rel * 512 + 512])
        for x_rel in range(2):
            for j in range(4):
                outs[rel >> 1][x_rel, rel & 1, j * 256 : j * 256 + 256, :] = bf(
                    up[x_rel * 256 : x_rel * 256 + 256, j * 128 : j * 128 + 128]
                )
        down = dot_tn(active[:, rel * 512 : rel * 512 + 512], lowered)
        for x_rel in range(2):
            for j in range(2):
                outs[rel >> 1][x_rel, rel & 1, 1024 + j * 512 : 1536 + j * 512, :] = bf(
                    down[:, x_rel * 256 + j * 128 : x_rel * 256 + j * 128 + 128]
                )


def put_attention(outs, normed, grad_projected, mixed, lowered, first_grad, second_grad, mx, quarter):
    heads = dot_tn(swap_halves(normed, mx), swap_quarters(grad_projected, quarter))
    output = dot_tn(swap_halves(mixed, mx), swap_quarters(lowered, quarter))
    gains = (swap_halves(first_grad, mx), swap_halves(second_grad, mx))
    row = iota((16, 128), 0)
    for x_rel in range(2):
        put_columns(outs, x_rel, 0, heads[x_rel * 256 : x_rel * 256 + 256], 3)
        put_columns(outs, x_rel, 768, output[x_rel * 256 : x_rel * 256 + 256], 1)
        block = jnp.zeros((16, 128), jnp.float32)
        for j in range(4):
            at = x_rel * 256 + (j & 1) * 128
            block = jnp.where(row == j, gains[j >> 1][:, at : at + 128], block)
        for rel in range(4):
            outs[rel >> 1][x_rel, rel & 1, 1024:1040, :] = bf(block)


def spatial_forward_kernel(
    me, frames, single_ref, pair_ref, gains, heads_ref, output_ref, up_ref, down_ref, picks_ref, wins_ref,
    windows_out, start_out, projected_out, chance_out, mixed_out, resid_out, active_out, slope_out, middle_out,
    embed,
):
    quarter, is_pair = me[1], me[2]
    embed[...] = jnp.zeros_like(embed)

    @pl.when(is_pair == 1)
    def _():
        embed[0:600, :] = pair_ref[...]

    @pl.when(is_pair == 0)
    def _():
        embed[0:300, :] = single_ref[...]

    own = own_columns(256)
    picks = picks_ref[...]
    windows = None
    for f in range(2):
        frame = jnp.concatenate([frames[(f * 3 + ch) * 128 : (f * 3 + ch) * 128 + 128, :] for ch in range(3)], 1)
        cut = None
        for i in range(KERN):
            lift = bf(jnp.where(iota((256, 128), 1) == 8 * (iota((256, 128), 0) >> 4) + i - 1, 1.0, 0.0))
            spread = bf(jnp.where(own, dot(lift, frame), 0.0))
            part = dot(spread, picks_of(picks, i))
            cut = part if cut is None else cut + part
        part = dot(widen(cut), wins_ref[f])
        windows = part if windows is None else windows + part
    windows = bf(windows)
    windows_out[...] = windows
    start = dot(windows, embed[...])
    start_out[...] = start
    normed, _, _ = normalize(start, gains[0:1, :])
    projected = bf(dot(normed, heads_ref[...]))
    projected_out[...] = projected
    mixed = attention(projected, None, chance_out, 64**-0.5)
    mixed_out[...] = mixed
    resid = start + dot(mixed, output_ref[...])
    resid_out[...] = resid
    second, _, _ = normalize(resid, gains[1:2, :])
    middle_out[...] = bf(resid + feed_forward(second, quarter, up_ref, down_ref, active_out, slope_out))


def spatial_back_one_kernel(
    me, incoming_ref, gains, resid_ref, slope_ref, active_ref, up_ref, down_ref,
    keep_out, send_out, grad_out, gain_out,
    inner_ref,
):
    mx, quarter = me[0], me[1]
    incoming = f32(incoming_ref[...])
    lowered = bf(incoming)
    second, unit, inverse = normalize(resid_ref[...], gains[1:2, :])
    back = feed_forward_back(lowered, quarter, up_ref, down_ref, slope_ref, inner_ref)
    grad, gain_grad = normalize_back(back, unit, inverse, gains[1:2, :])
    grad_out[...] = incoming + grad
    gain_out[...] = jnp.broadcast_to(gain_grad, gain_out.shape)
    put_feed_forward((keep_out, send_out), second, inner_ref, active_ref, lowered, mx)


def spatial_back_two_kernel(
    me, incoming_ref, gain_ref, gains, start_ref, projected_ref, chance_ref, mixed_ref, windows_ref,
    heads_ref, output_ref, single_ref, pair_ref, picks_ref, wins_ref,
    keep_out, send_out, pixel_out,
    embed, grads,
):
    mx, quarter, is_pair = me[0], me[1], me[2]
    outs = (keep_out, send_out)
    embed[...] = jnp.zeros_like(embed)

    @pl.when(is_pair == 1)
    def _():
        embed[0:600, :] = pair_ref[...]

    @pl.when(is_pair == 0)
    def _():
        embed[0:300, :] = single_ref[...]

    incoming = incoming_ref[...]
    lowered = bf(incoming)
    grad_mixed = bf(dot_nt(lowered, output_ref[...]))
    projected = projected_ref[...]
    grad_projected = attention_back(grad_mixed, projected, chance_ref, 64**-0.5)
    normed, unit, inverse = normalize(start_ref[...], gains[0:1, :])
    back, gain_grad = normalize_back(dot_nt(grad_projected, heads_ref[...]), unit, inverse, gains[0:1, :])
    grad_start = bf(incoming + back)
    put_attention(outs, normed, grad_projected, mixed_ref[...], lowered, gain_grad, gain_ref[0:1, :], mx, quarter)
    windows = windows_ref[...]
    grads[...] = dot_tn(windows, swap_halves(grad_start, mx))
    pair_part = jnp.where(is_pair == 1, 1.0, 0.0)
    single_part = 1.0 - pair_part
    for x_rel in range(2):
        for rel in range(4):
            for j in range(2):
                at = x_rel * 256 + j * 128
                first = pl.multiple_of((quarter ^ rel) * 80, 16)
                outs[rel >> 1][x_rel, rel & 1, 1040 + j * 80 : 1120 + j * 80, :] = bf(
                    grads[pl.ds(first, 80), at : at + 128] * single_part
                )
                first = pl.multiple_of((quarter ^ rel) * 160, 16)
                outs[rel >> 1][x_rel, rel & 1, 1200 + j * 160 : 1360 + j * 160, :] = bf(
                    grads[pl.ds(first, 160), at : at + 128] * pair_part
                )
    window_grads = bf(dot_nt(grad_start, embed[...]))
    own = own_columns(256)
    picks = picks_ref[...]
    for f in range(2):
        folded = narrow(dot_nt(window_grads, wins_ref[f]))
        frame = None
        for i in range(KERN):
            spread = bf(jnp.where(own, dot_nt(folded, picks_of(picks, i)), 0.0))
            lift = bf(jnp.where(iota((128, 256), 0) == 8 * (iota((128, 256), 1) >> 4) + i - 1, 1.0, 0.0))
            part = dot(lift, spread)
            frame = part if frame is None else frame + part
        for ch in range(3):
            pixel_out[(f * 3 + ch) * 128 : (f * 3 + ch) * 128 + 128, :] = bf(frame[:, ch * 128 : ch * 128 + 128])


def slots_seen():
    def parts(dim):
        t = iota((256, 256), dim)
        index = (t >> 4) & 3
        slot = jnp.where(t < 128, jnp.where(index == 0, 0, index + 4), index + 1)
        return ((t >> 2) & 16) | (t & 15), slot

    here, query = parts(0)
    there, key = parts(1)
    near = (key <= query) & (((key < VSTEPS) & (query < VSTEPS)) | (key == query))
    return (here == there) & near


def temporal_one_kernel(
    me, middle_ref, cot_ref, edges_ref, gains, heads_ref, output_ref, up_ref, down_ref, single_ref, pair_ref,
    picks_ref, wins_ref, rows_ref, sums_ref,
    keep_out, send_out, grad_out, gain_out, projected_out, chance_out, mixed_out, final_out, cut_out,
    rebuilt_out, rims_out,
    active_ref, slope_ref, inner_ref, unpatch_one, unpatch_two, cot,
):
    mx, quarter = me[0], me[1]
    unpatch_one[...] = jnp.zeros_like(unpatch_one)
    unpatch_two[...] = jnp.zeros_like(unpatch_two)
    unpatch_one[:, 0:300] = single_ref[...]
    unpatch_two[:, 0:600] = pair_ref[...]
    middle = f32(middle_ref[...])
    normed, _, _ = normalize(middle, gains[2:3, :])
    projected = bf(dot(normed, heads_ref[...]))
    projected_out[...] = projected
    mixed = attention(projected, slots_seen(), chance_out, 64**-0.5)
    mixed_out[...] = mixed
    resid = middle + dot(mixed, output_ref[...])
    second, unit, inverse = normalize(resid, gains[3:4, :])
    final = bf(resid + feed_forward(second, quarter, up_ref, down_ref, active_ref, slope_ref))
    final_out[...] = final

    own = own_columns(384)
    picks = picks_ref[...]
    one = bf(dot(final[:128], unpatch_one[...]))
    two = bf(dot(final[128:], unpatch_two[...]))
    folded = jnp.concatenate(
        [
            narrow(dot_nt(one, wins_ref[0, :, 0:384])),
            narrow(dot_nt(two, wins_ref[0])),
            narrow(dot_nt(two, wins_ref[1])),
        ],
        0,
    )
    sums = sums_ref[...]
    for i in range(KERN):
        spread = bf(jnp.where(own, dot_nt(folded, picks_of(picks, i)), 0.0))
        row = dot(sums, spread)
        if i == 0:
            rims_out[0:32, :] = bf(row)
        elif i == KERN - 1:
            rims_out[32:64, :] = bf(row)
        else:
            for ch in range(3):
                rebuilt_out[pl.ds(ch * 8 + i - 1, 24, stride=24), :] = row[:24, ch * 128 : ch * 128 + 128]

    cot[...] = f32(cot_ref[...])
    places = rows_ref[...]
    cut = None
    for i in range(KERN):
        parts = []
        for ch in range(3):
            if i == 0:
                parts.append(edges_ref[pl.ds(ch, 24, stride=3), :])
            elif i == KERN - 1:
                parts.append(edges_ref[pl.ds(72 + ch, 24, stride=3), :])
            else:
                parts.append(cot[pl.ds(ch * 8 + i - 1, 24, stride=24), :])
        row = jnp.concatenate([jnp.concatenate(parts, 1), jnp.zeros((8, 384), jnp.float32)], 0)
        spread = bf(jnp.where(own, dot(places, bf(row)), 0.0))
        part = dot(spread, picks_of(picks, i))
        cut = part if cut is None else cut + part
    wide = widen(cut)
    cut_one = bf(dot(wide[:128], wins_ref[0, :, 0:384]))
    cut_two = bf(dot(wide[128:256], wins_ref[0]) + dot(wide[256:], wins_ref[1]))
    cut_out[:, 0:384] = cut_one
    cut_out[:, 384:1024] = cut_two

    incoming = jnp.concatenate([dot_nt(cut_one, unpatch_one[...]), dot_nt(cut_two, unpatch_two[...])], 0)
    lowered = bf(incoming)
    back = feed_forward_back(lowered, quarter, up_ref, down_ref, slope_ref, inner_ref)
    grad, gain_grad = normalize_back(back, unit, inverse, gains[3:4, :])
    grad_out[...] = incoming + grad
    gain_out[...] = jnp.broadcast_to(gain_grad, gain_out.shape)
    put_feed_forward((keep_out, send_out), second, inner_ref, active_ref, lowered, mx)


def temporal_two_kernel(
    me, incoming_ref, gain_ref, gains, middle_ref, projected_ref, chance_ref, mixed_ref, final_ref, cut_ref,
    heads_ref, output_ref,
    keep_out, send_out, grad_out,
    grads,
):
    mx, quarter = me[0], me[1]
    outs = (keep_out, send_out)
    incoming = incoming_ref[...]
    lowered = bf(incoming)
    grad_mixed = bf(dot_nt(lowered, output_ref[...]))
    grad_projected = attention_back(grad_mixed, projected_ref[...], chance_ref, 64**-0.5)
    normed, unit, inverse = normalize(f32(middle_ref[...]), gains[2:3, :])
    back, gain_grad = normalize_back(dot_nt(grad_projected, heads_ref[...]), unit, inverse, gains[2:3, :])
    grad_out[...] = bf(incoming + back)
    put_attention(outs, normed, grad_projected, mixed_ref[...], lowered, gain_grad, gain_ref[0:1, :], mx, quarter)
    final = swap_halves(final_ref[...], mx)
    grads[:, 0:384] = dot_tn(final[:128], cut_ref[:, 0:384])
    grads[:, 384:1024] = dot_tn(final[128:], cut_ref[:, 384:1024])
    for x_rel in range(2):
        for rel in range(4):
            first = pl.multiple_of(x_rel * 256 + (quarter ^ rel) * 64, 16)
            for j in range(8):
                outs[rel >> 1][x_rel, rel & 1, 1040 + j * 64 : 1104 + j * 64, :] = bf(
                    grads[pl.ds(first, 64), j * 128 : j * 128 + 128]
                )


FEED_ROWS = 2048
TIME_ROWS = 1040 + 512
SPACE_ROWS = 1040 + 480


def unpack_feed_kernel(me, a, b, c, d, up_out, down_out):
    for rel, source in enumerate((a, b, c, d)):
        at = pl.multiple_of((me[1] ^ rel) * 512, 512)
        for j in range(4):
            up_out[:, pl.ds(pl.multiple_of(at + j * 128, 128), 128)] = f32(source[j * 256 : j * 256 + 256, :])
        for j in range(2):
            down_out[pl.ds(at, 512), j * 128 : j * 128 + 128] = f32(source[1024 + j * 512 : 1536 + j * 512, :])


def unpack_attention(me, sources, heads_out, output_out, gains_out):
    for rel, source in enumerate(sources):
        quarter = me[1] ^ rel
        for j in range(3):
            at = pl.multiple_of(quarter * 384 + j * 128, 128)
            heads_out[:, pl.ds(at, 128)] = f32(source[j * 256 : j * 256 + 256, :])
        output_out[:, pl.ds(pl.multiple_of(quarter * 128, 128), 128)] = f32(source[768:1024, :])
    gains_out[...] = f32(sources[0][1024:1040, :])


def unpack_time_kernel(me, a, b, c, d, heads_out, output_out, gains_out, single_out, pair_out):
    sources = (a, b, c, d)
    unpack_attention(me, sources, heads_out, output_out, gains_out)
    for rel, source in enumerate(sources):
        first = pl.ds(pl.multiple_of((me[1] ^ rel) * 64, 16), 64)
        for j in range(8):
            block = f32(source[1040 + j * 64 : 1104 + j * 64, :])
            if j < 3:
                width = min(128, 300 - j * 128)
                single_out[first, j * 128 : j * 128 + width] = block[:, :width]
            else:
                width = min(128, 600 - (j - 3) * 128)
                pair_out[first, (j - 3) * 128 : (j - 3) * 128 + width] = block[:, :width]


def unpack_space_kernel(me, a, b, c, d, heads_out, output_out, gains_out, single_out, pair_out, single, pair):
    sources = (a, b, c, d)
    unpack_attention(me, sources, heads_out, output_out, gains_out)
    for rel, source in enumerate(sources):
        quarter = me[1] ^ rel
        for j in range(2):
            single[pl.ds(pl.multiple_of(quarter * 80, 16), 80), j * 128 : j * 128 + 128] = f32(
                source[1040 + j * 80 : 1120 + j * 80, :]
            )
            pair[pl.ds(pl.multiple_of(quarter * 160, 16), 160), j * 128 : j * 128 + 128] = f32(
                source[1200 + j * 160 : 1360 + j * 160, :]
            )
    single_out[...] = single[0:300, :]
    pair_out[...] = pair[0:600, :]


def call(kernel, name, outs, args, scratch=(), flops=0, smem=1):
    specs = [pl.BlockSpec(memory_space=pltpu.SMEM)] * smem + [pl.BlockSpec(memory_space=pltpu.VMEM)] * (
        len(args) - smem
    )
    return pl.pallas_call(
        kernel,
        name=name,
        out_shape=[jax.ShapeDtypeStruct(s, d) for s, d in outs],
        in_specs=specs,
        out_specs=[pl.BlockSpec(memory_space=pltpu.VMEM)] * len(outs),
        scratch_shapes=[pltpu.VMEM(s, d) for s, d in scratch],
        compiler_params=pltpu.CompilerParams(vmem_limit_bytes=56 * MIB),
        cost_estimate=pl.CostEstimate(
            flops=flops,
            bytes_accessed=sum(int(np.prod(a.shape)) * a.dtype.itemsize for a in args),
            transcendentals=0,
        ),
    )(*args)


def flips(size, bit):
    return [(i, i ^ bit) for i in range(size)]


def add(a, b):
    return bf(f32(a) + f32(b))


def reduce_pieces(keep, send):
    grp, rows = lax.axis_size("grp"), lax.axis_size("rows")
    core, along_y, along_z = flips(rows, 1), flips(rows, 2), rows // 4
    got = lax.ppermute(send, "rows", core)
    near, far = add(keep[0], got[0]), add(keep[1], got[1])
    got = lax.ppermute(far, "grp", flips(grp, grp // 2))
    near, far = add(near[0], got[0]), add(near[1], got[1])
    got = lax.ppermute(far, "rows", along_y)
    total = add(near, got)
    place = lax.axis_index("rows") // 4
    line = [[z * 4 + i for i in range(4)] for z in range(along_z)]
    inward = list(zip(line[0] + line[3], line[1] + line[2]))
    across = list(zip(line[1] + line[2], line[2] + line[1]))
    outward = list(zip(line[1] + line[2], line[0] + line[3]))
    total = add(total, lax.ppermute(total, "rows", inward))
    total = add(total, lax.ppermute(total, "rows", across))
    got = lax.ppermute(total, "rows", outward)
    total = jnp.where((place == 0) | (place == 3), got, total)
    beside = lax.ppermute(total, "rows", along_y)
    other = lax.ppermute(jnp.stack([total, beside]), "rows", core)
    return total, beside, other[0], other[1]


def finish_grp(values, dims):
    grp = lax.axis_size("grp")
    me = lax.axis_index("grp")
    bit = grp // 4
    while bit:
        mine = (me // bit) % 2
        out = []
        for v, dim in zip(values, dims):
            half = v.shape[dim] // 2
            near = lax.dynamic_slice_in_dim(v, mine * half, half, dim)
            far = lax.dynamic_slice_in_dim(v, (1 - mine) * half, half, dim)
            out.append(near + f32(lax.ppermute(bf(far), "grp", flips(grp, bit))))
        values = out
        bit //= 2
    return values


def on_device(
    pixels,
    cotangent,
    embed_single,
    embed_pair,
    spatial_gain,
    spatial_heads,
    spatial_output,
    spatial_scale,
    spatial_upward,
    spatial_down,
    temporal_gain,
    temporal_heads,
    temporal_output,
    temporal_scale,
    temporal_upward,
    temporal_down,
    unpatch_single,
    unpatch_pair,
):
    groups, frames = pixels.shape[:2]
    rows = lax.axis_size("rows")
    assert groups * 8 == rows == GRID and frames == 12 and pixels.shape[3] == STRIDE
    grp = lax.axis_size("grp")
    at = lax.axis_index("rows")
    core, along_y = at & 1, (at >> 1) & 1
    me = jnp.stack(
        [
            lax.axis_index("grp") // (grp // 2),
            core * 2 + along_y,
            jnp.where(at >= 8, 1, 0),
            at,
        ]
    ).astype(jnp.int32)
    picks = jnp.asarray(column_picks())
    wins = jnp.asarray(np.stack([window_picks(0, 640), window_picks(300, 640)]))
    places = frame_rows()
    sums = jnp.asarray(places.T)
    places = jnp.asarray(places)
    gains = f32(jnp.stack([spatial_gain, spatial_scale, temporal_gain, temporal_scale]))

    singles = jnp.concatenate([pixels[:, :1], pixels[:, 9:]], 1).reshape(8, 1, CHAN, STRIDE, 128)
    pairs = pixels[:, 1:9].reshape(8, 2, CHAN, STRIDE, 128)
    sent = jnp.concatenate([jnp.concatenate([singles, singles], 1), pairs], 0)
    got = lax.all_to_all(sent, "rows", 0, 0)
    images = jnp.transpose(got, (1, 2, 0, 3, 4)).reshape(2 * CHAN * 128, 128)

    up = [(i, i + 1) for i in range(rows - 1)]
    down = [(i + 1, i) for i in range(rows - 1)]
    above = lax.ppermute(cotangent[:, :, :, 7, :], "rows", up)
    below = lax.ppermute(cotangent[:, :, :, 0, :], "rows", down)
    edges = f32(jnp.concatenate([above.reshape(72, 128), below.reshape(72, 128)], 0))

    b16, w32 = jnp.bfloat16, jnp.float32
    windows, start, projected, chance, mixed, resid, active, slope, middle = call(
        spatial_forward_kernel,
        "spatial_forward",
        [
            ((256, 640), b16),
            ((256, 512), w32),
            ((256, 1536), b16),
            ((8, 256, 256), b16),
            ((256, 512), b16),
            ((256, 512), w32),
            ((256, 2048), b16),
            ((256, 2048), b16),
            ((256, 512), b16),
        ],
        [me, images, embed_single, embed_pair, gains, spatial_heads, spatial_output, spatial_upward, spatial_down, picks, wins],
        [((640, 512), b16)],
        flops=3_000_000_000,
    )
    middle = lax.all_to_all(middle.reshape(16, 16, 512), "rows", 0, 0).reshape(256, 512)

    (
        t_feed_keep, t_feed_send, t_grad, t_gain, t_projected, t_chance, t_mixed, t_final, t_cut, rebuilt, rims,
    ) = call(
        temporal_one_kernel,
        "temporal_one",
        [
            ((2, 2, FEED_ROWS, 128), b16),
            ((2, 2, FEED_ROWS, 128), b16),
            ((256, 512), w32),
            ((8, 512), w32),
            ((256, 1536), b16),
            ((8, 256, 256), b16),
            ((256, 512), b16),
            ((256, 512), b16),
            ((128, 1024), b16),
            ((576, 128), w32),
            ((64, 384), b16),
        ],
        [
            me, middle, cotangent.reshape(576, 128), edges, gains, temporal_heads, temporal_output, temporal_upward,
            temporal_down, unpatch_single, unpatch_pair, picks, wins, places, sums,
        ],
        [
            ((256, 2048), b16),
            ((256, 2048), b16),
            ((256, 2048), b16),
            ((512, 384), b16),
            ((512, 640), b16),
            ((576, 128), w32),
        ],
        flops=6_000_000_000,
    )
    t_feed = reduce_pieces(t_feed_keep, t_feed_send)

    t_keep, t_send, grad_middle = call(
        temporal_two_kernel,
        "temporal_two",
        [((2, 2, TIME_ROWS, 128), b16), ((2, 2, TIME_ROWS, 128), b16), ((256, 512), b16)],
        [
            me, t_grad, t_gain, gains, middle, t_projected, t_chance, t_mixed, t_final, t_cut, temporal_heads,
            temporal_output,
        ],
        [((512, 1024), w32)],
        flops=2_000_000_000,
    )
    t_rest = reduce_pieces(t_keep, t_send)
    grad_middle = lax.all_to_all(grad_middle.reshape(16, 16, 512), "rows", 0, 0).reshape(256, 512)

    s_feed_keep, s_feed_send, s_grad, s_gain = call(
        spatial_back_one_kernel,
        "spatial_back_one",
        [((2, 2, FEED_ROWS, 128), b16), ((2, 2, FEED_ROWS, 128), b16), ((256, 512), w32), ((8, 512), w32)],
        [me, grad_middle, gains, resid, slope, active, spatial_upward, spatial_down],
        [((256, 2048), b16)],
        flops=2_000_000_000,
    )
    s_feed = reduce_pieces(s_feed_keep, s_feed_send)
    s_keep, s_send, pixel_frames = call(
        spatial_back_two_kernel,
        "spatial_back_two",
        [((2, 2, SPACE_ROWS, 128), b16), ((2, 2, SPACE_ROWS, 128), b16), ((768, 128), b16)],
        [
            me, s_grad, s_gain, gains, start, projected, chance, mixed, windows, spatial_heads, spatial_output,
            embed_single, embed_pair, picks, wins,
        ],
        [((640, 512), b16), ((640, 512), w32)],
        flops=3_000_000_000,
    )
    s_rest = reduce_pieces(s_keep, s_send)

    sent = jnp.transpose(pixel_frames.reshape(2, CHAN, GRID, STRIDE, 128), (2, 0, 1, 3, 4))
    got = f32(lax.all_to_all(sent, "rows", 0, 0))
    singles = got[:8, 0].reshape(2, 4, CHAN, STRIDE, 128)
    pairs = got[8:].reshape(2, 8, CHAN, STRIDE, 128)
    pixel_gradient = jnp.concatenate([singles[:, :1], pairs, singles[:, 1:]], 1)

    top = rims[0:24].reshape(2, 12, CHAN, 1, 128)
    bottom = rims[32:56].reshape(2, 12, CHAN, 1, 128)
    from_below = f32(lax.ppermute(top, "rows", down))
    from_above = f32(lax.ppermute(bottom, "rows", up))
    gap = jnp.zeros(rebuilt.shape[:0] + (2, 12, CHAN, STRIDE - 2, 128), w32)
    rebuilt = rebuilt.reshape(2, 12, CHAN, STRIDE, 128) + jnp.concatenate([from_above, gap, from_below], 3)

    half = 256
    t_up, t_down = call(
        unpack_feed_kernel, "unpack_temporal_feed", [((half, 2048), w32), ((2048, half), w32)], [me, *t_feed]
    )
    t_heads, t_output, t_gains, un_single, un_pair = call(
        unpack_time_kernel,
        "unpack_temporal_rest",
        [((half, 1536), w32), ((half, 512), w32), ((16, 128), w32), ((half, 300), w32), ((half, 600), w32)],
        [me, *t_rest],
    )
    s_up, s_down = call(
        unpack_feed_kernel, "unpack_spatial_feed", [((half, 2048), w32), ((2048, half), w32)], [me, *s_feed]
    )
    s_heads, s_output, s_gains, em_single, em_pair = call(
        unpack_space_kernel,
        "unpack_spatial_rest",
        [((half, 1536), w32), ((half, 512), w32), ((16, 128), w32), ((300, half), w32), ((600, half), w32)],
        [me, *s_rest],
        [((320, half), w32), ((640, half), w32)],
    )
    grads = [
        em_single,
        em_pair,
        s_gains[0:2].reshape(256),
        s_heads,
        s_output,
        s_gains[2:4].reshape(256),
        s_up,
        s_down,
        t_gains[0:2].reshape(256),
        t_heads,
        t_output,
        t_gains[2:4].reshape(256),
        t_up,
        t_down,
        un_single,
        un_pair,
    ]
    dims = [1, 1, 0, 0, 0, 0, 0, 1, 0, 0, 0, 0, 0, 1, 0, 0]
    return (rebuilt, pixel_gradient, *finish_grp(grads, dims))


def solution(mesh):
    in_specs = (
        P("grp", None, None, "rows", None),
        P("grp", None, None, "rows", None),
    ) + (P(),) * 16
    out_specs = (
        P("grp", None, None, "rows", None),
        P("grp", None, None, "rows", None),
        P(None, "grp"),
        P(None, "grp"),
        P("grp"),
        P("grp", None),
        P("grp", None),
        P("grp"),
        P("grp", None),
        P(None, "grp"),
        P("grp"),
        P("grp", None),
        P("grp", None),
        P("grp"),
        P("grp", None),
        P(None, "grp"),
        P("grp", None),
        P("grp", None),
    )
    return jax.shard_map(
        on_device, mesh=mesh, in_specs=in_specs, out_specs=out_specs, check_vma=False
    )
```

```python
import functools

import jax
import jax.numpy as jnp
import numpy as np
from jax import lax
from jax.experimental import pallas as pl
from jax.experimental.pallas import tpu as pltpu
from jax.sharding import PartitionSpec as P

HEADS = 8
STRIDE = 8
KERN = 10
GRID = 16
VSTEPS = 5
CHAN = 3
LANES = 128

epsilon = 1e-05
gelu_coef = 0.7978845608028654
cubic_coef = 0.044715
masked_score = -1000000000.0

WIN = CHAN * KERN * KERN
CUTS = KERN * CHAN * STRIDE
SINGLE_FRAMES = (0, 9, 10, 11)
MIB = 1 << 20
MICRO = 700_000_000


def column_picks():
    n = np.arange(256)
    chan, bit = (n % 24) // 8, n % 8
    at = np.arange(CHAN * 128)
    return ((n < CUTS) & (at[:, None] // 128 == chan) & (at[:, None] % 8 == bit)).astype(jnp.bfloat16)


def window_picks(first, width):
    n = np.arange(256)
    row, chan, bit = n // 24, (n % 24) // 8, n % 8
    w = np.arange(width) - first
    hit = (w >= 0) & (w < WIN)
    same = hit & (n < CUTS)[:, None] & (chan[:, None] == w // 100) & (row[:, None] == (w % 100) // 10)
    step = w % 10
    own = same & (step == bit[:, None] + 1)
    before = same & (step == 0) & (bit[:, None] == 7)
    after = same & (step == 9) & (bit[:, None] == 0)
    return np.concatenate([own, before, after], 0).astype(jnp.bfloat16)


def frame_rows():
    order = (SINGLE_FRAMES, (1, 3, 5, 7), (2, 4, 6, 8))
    out = np.zeros((384, 32), np.float32)
    for k in range(3):
        for g in range(2):
            for i in range(4):
                at = ((k * 2 + g) * 4 + i) * 16
                out[at : at + 16, g * 12 + order[k][i]] = 1
    return out.astype(jnp.bfloat16)


ROUTES = {"a": "y123W", "b": "CXy123W", "c": "y123W", "d": "CXy123W"}
GATES = {}
GROUPS = {}
ORDER = (
    "cut", "A", "T1", "T2", "TG", "bC", "T3", "C1", "bX", "ay", "C3", "dC", "by", "a1", "F", "cy", "b1", "a2", "dX",
    "c1", "b2", "dy", "a3", "P", "c2", "d1", "b3", "aU", "c3", "d2", "bU", "d3", "cU", "dU",
)


def dot(a, b):
    return jnp.dot(a, b, preferred_element_type=jnp.float32)


def dot_nt(a, b):
    return lax.dot_general(a, b, (((1,), (1,)), ((), ())), preferred_element_type=jnp.float32)


def dot_tn(a, b):
    return lax.dot_general(a, b, (((0,), (0,)), ((), ())), preferred_element_type=jnp.float32)


def bf(x):
    return x.astype(jnp.bfloat16)


def f32(x):
    return x.astype(jnp.float32)


def iota(shape, dim):
    return lax.broadcasted_iota(jnp.int32, shape, dim)


def own_columns(rows):
    return ((iota((rows, 384), 1) & 127) >> 3) == (iota((rows, 384), 0) & 15)


def picks_of(picks, i):
    lane = iota((1, 256), 1)
    return picks * bf(jnp.where((lane >= 24 * i) & (lane < 24 * i + 24), 1.0, 0.0))


def shift_up(v):
    return jnp.where((iota(v.shape, 0) & 15) == 15, 0.0, pltpu.roll(v, v.shape[0] - 1, 0))


def shift_down(v):
    return jnp.where((iota(v.shape, 0) & 15) == 0, 0.0, pltpu.roll(v, 1, 0))


def widen(v):
    return bf(jnp.concatenate([v, shift_down(v), shift_up(v)], 1))


def narrow(t):
    return bf(t[:, :256] + shift_up(t[:, 256:512]) + shift_down(t[:, 512:]))


def normalize(x, gain):
    centered = x - jnp.mean(x, -1, keepdims=True)
    inverse = lax.rsqrt(jnp.mean(centered * centered, -1, keepdims=True) + epsilon)
    unit = centered * inverse
    return bf(unit * gain), unit, inverse


def normalize_back(incoming, unit, inverse, gain):
    scaled = incoming * gain
    gain_grad = jnp.sum(incoming * unit, 0, keepdims=True)
    first = jnp.mean(scaled, -1, keepdims=True)
    second = jnp.mean(scaled * unit, -1, keepdims=True)
    return inverse * (scaled - first - unit * second), gain_grad


def halves_mask(width=128):
    lane = iota((1, width), 1)
    return lane < 64


def attention(projected, seen, chance_ref, scale):
    low = halves_mask()
    keep = (bf(jnp.where(low, 1.0, 0.0)), bf(jnp.where(low, 0.0, 1.0)))
    outs = []
    for pair in range(HEADS // 2):
        q = projected[:, pair * 128 : pair * 128 + 128]
        k = projected[:, 512 + pair * 128 : 512 + pair * 128 + 128]
        v = projected[:, 1024 + pair * 128 : 1024 + pair * 128 + 128]
        both = []
        for half in range(2):
            scores = dot_nt(q * keep[half], k) * scale
            if seen is not None:
                scores = jnp.where(seen, scores, masked_score)
            powers = jnp.exp(scores - jnp.max(scores, -1, keepdims=True))
            chance = bf(powers * (1.0 / jnp.sum(powers, -1, keepdims=True)))
            chance_ref[2 * pair + half] = chance
            both.append(dot(chance, v))
        outs.append(jnp.where(low, both[0], both[1]))
    return bf(jnp.concatenate(outs, 1))


def attention_back(grad_mixed, projected, chance_ref, scale):
    low = halves_mask()
    keep = (bf(jnp.where(low, 1.0, 0.0)), bf(jnp.where(low, 0.0, 1.0)))
    grads = ([], [], [])
    for pair in range(HEADS // 2):
        q = projected[:, pair * 128 : pair * 128 + 128]
        k = projected[:, 512 + pair * 128 : 512 + pair * 128 + 128]
        v = projected[:, 1024 + pair * 128 : 1024 + pair * 128 + 128]
        g = grad_mixed[:, pair * 128 : pair * 128 + 128]
        both = ([], [], [])
        for half in range(2):
            chance = chance_ref[2 * pair + half]
            wide = f32(chance)
            grad_chance = dot_nt(g * keep[half], v)
            inner = jnp.sum(wide * grad_chance, -1, keepdims=True)
            grad_scores = bf(wide * (grad_chance - inner))
            both[0].append(dot(grad_scores, k))
            both[1].append(dot_tn(grad_scores, q))
            both[2].append(dot_tn(chance, g))
        for part, factor in zip(range(3), (scale, scale, 1.0)):
            grads[part].append(bf(jnp.where(low, both[part][0], both[part][1]) * factor))
    return jnp.concatenate(grads[0] + grads[1] + grads[2], 1)


def gelu_parts(inner):
    square = inner * inner
    bent = jnp.tanh(gelu_coef * inner * (1.0 + cubic_coef * square))
    half = 0.5 * (1.0 + bent)
    slope = half + 0.5 * inner * (1.0 - bent * bent) * gelu_coef * (1.0 + 3.0 * cubic_coef * square)
    return bf(inner * half), slope


def feed_forward(second, up_ref, down_ref, slope_ref):
    total = None
    for k in range(4):
        columns = slice(k * 512, k * 512 + 512)
        active, slope = gelu_parts(dot(second, up_ref[:, columns]))
        slope_ref[:, columns] = bf(slope)
        part = dot(active, down_ref[columns, :])
        total = part if total is None else total + part
    return total


def feed_forward_back(lowered, up_ref, down_ref, slope_ref):
    total = None
    for k in range(4):
        columns = slice(k * 512, k * 512 + 512)
        grad_inner = bf(dot_nt(lowered, down_ref[columns, :]) * f32(slope_ref[:, columns]))
        part = dot_nt(grad_inner, up_ref[:, columns])
        total = part if total is None else total + part
    return total


def feed_grad_kernel(me, *refs):
    *shares, up_ref, down_ref, near, far, second, incoming, active, grad_inner = refs
    for k in range(4):
        rows = slice(k * 256, k * 256 + 256)
        if len(shares) == 4:
            second[rows, :] = shares[k][0]
            incoming[rows, :] = shares[k][1]
        else:
            second[rows, :] = shares[k][...]
            incoming[rows, :] = shares[4 + k][...]
    half = pl.ds(pl.multiple_of(me[0] * 256, 256), 256)
    for rel, out in enumerate((near, far)):
        at = pl.multiple_of((me[1] ^ rel) * 512, 512)
        up, down = up_ref[:, pl.ds(at, 512)], down_ref[pl.ds(at, 512), :]
        for k in range(4):
            rows = slice(k * 256, k * 256 + 256)
            act, slope = gelu_parts(dot(second[rows, :], up))
            active[rows, :] = act
            grad_inner[rows, :] = bf(dot_nt(incoming[rows, :], down) * slope)
        up_grad = dot_tn(second[:, half], grad_inner[...])
        for j in range(4):
            out[j * 256 : j * 256 + 256, :] = bf(up_grad[:, j * 128 : j * 128 + 128])
        down_grad = dot_tn(active[...], incoming[:, half])
        for j in range(2):
            out[1024 + j * 512 : 1536 + j * 512, :] = bf(down_grad[:, j * 128 : j * 128 + 128])


def swap_halves(v, bit):
    half = v.shape[1] // 2
    return jnp.where(bit == 1, jnp.concatenate([v[:, half:], v[:, :half]], 1), v)


def swap_quarters(v, quarter):
    v = swap_halves(v, quarter >> 1)
    half = v.shape[1] // 2
    return jnp.concatenate([swap_halves(v[:, :half], quarter & 1), swap_halves(v[:, half:], quarter & 1)], 1)


def put(outs, rel, x_rel, first, last, value):
    if rel < 2:
        outs[0][x_rel, rel, first:last, :] = value
    elif len(outs) == 2:
        outs[1][x_rel, rel & 1, first:last, :] = value
    else:
        outs[1 + x_rel][rel & 1, first:last, :] = value


def put_columns(outs, x_rel, at, value, count):
    rows, width = value.shape[0], value.shape[1] // 4
    for rel in range(4):
        for j in range(width // LANES):
            block = value[:, rel * width + j * LANES : rel * width + (j + 1) * LANES]
            put(outs, rel, x_rel, at + j * rows, at + (j + 1) * rows, bf(block))


def put_rows(outs, x_rel, at, source, row0, rows, quarter):
    size = rows // 4
    blocks = source.shape[1] // LANES
    for rel in range(4):
        first = pl.multiple_of(row0 + (quarter ^ rel) * size, 16)
        for j in range(blocks):
            put(outs, rel, x_rel, at + j * size, at + (j + 1) * size, bf(source[pl.ds(first, size), j * LANES : (j + 1) * LANES]))


def put_attention(outs, normed, grad_projected, mixed, lowered, first_grad, second_grad, mx, quarter):
    heads = dot_tn(swap_halves(normed, mx), swap_quarters(grad_projected, quarter))
    output = dot_tn(swap_halves(mixed, mx), swap_quarters(lowered, quarter))
    gains = (swap_halves(first_grad, mx), swap_halves(second_grad, mx))
    row = iota((16, 128), 0)
    for x_rel in range(2):
        put_columns(outs, x_rel, 0, heads[x_rel * 256 : x_rel * 256 + 256], 3)
        put_columns(outs, x_rel, 768, output[x_rel * 256 : x_rel * 256 + 256], 1)
        block = jnp.zeros((16, 128), jnp.float32)
        for j in range(4):
            at = x_rel * 256 + (j & 1) * 128
            block = jnp.where(row == j, gains[j >> 1][:, at : at + 128], block)
        for rel in range(4):
            put(outs, rel, x_rel, 1024, 1040, bf(block))


def slots_kernel(me, pixels, out):
    for g in range(2):
        for k in range(4):
            single = pixels[g, SINGLE_FRAMES[k]]
            out[g * 4 + k, 0] = single
            out[g * 4 + k, 1] = single
            out[8 + g * 4 + k, 0] = pixels[g, 2 * k + 1]
            out[8 + g * 4 + k, 1] = pixels[g, 2 * k + 2]


def spatial_forward_kernel(
    me, frames, single_ref, pair_ref, gains, heads_ref, output_ref, up_ref, down_ref, picks_ref, wins_ref,
    windows_out, start_out, projected_out, chance_out, mixed_out, resid_out, second_out, slope_out, middle_out,
    embed,
):
    is_pair = me[2]
    embed[...] = jnp.zeros_like(embed)

    @pl.when(is_pair == 1)
    def _():
        embed[0:600, :] = pair_ref[...]

    @pl.when(is_pair == 0)
    def _():
        embed[0:300, :] = single_ref[...]

    own = own_columns(256)
    picks = picks_ref[...]
    windows = None
    for f in range(2):
        frame = jnp.concatenate([frames[(f * 3 + ch) * 128 : (f * 3 + ch) * 128 + 128, :] for ch in range(3)], 1)
        cut = None
        for i in range(KERN):
            lift = bf(jnp.where(iota((256, 128), 1) == 8 * (iota((256, 128), 0) >> 4) + i - 1, 1.0, 0.0))
            spread = bf(jnp.where(own, dot(lift, frame), 0.0))
            part = dot(spread, picks_of(picks, i))
            cut = part if cut is None else cut + part
        part = dot(widen(cut), wins_ref[f])
        windows = part if windows is None else windows + part
    windows = bf(windows)
    windows_out[...] = windows
    start = dot(windows, embed[...])
    start_out[...] = start
    normed, _, _ = normalize(start, gains[0:1, :])
    projected = bf(dot(normed, heads_ref[...]))
    projected_out[...] = projected
    mixed = attention(projected, None, chance_out, 64**-0.5)
    mixed_out[...] = mixed
    resid = start + dot(mixed, output_ref[...])
    resid_out[...] = resid
    second, _, _ = normalize(resid, gains[1:2, :])
    second_out[...] = second
    middle_out[...] = bf(resid + feed_forward(second, up_ref, down_ref, slope_out))


def spatial_back_kernel(
    me, incoming_ref, gains, resid_ref, slope_ref, start_ref, projected_ref, chance_ref, mixed_ref, windows_ref,
    up_ref, down_ref, heads_ref, output_ref,
    keep_out, send_near, send_far, start_out,
    grads,
):
    mx, quarter, is_pair = me[0], me[1], me[2]
    outs = (keep_out, send_near, send_far)
    incoming = incoming_ref[...]
    _, unit, inverse = normalize(resid_ref[...], gains[1:2, :])
    back = feed_forward_back(incoming, up_ref, down_ref, slope_ref)
    grad, scale_grad = normalize_back(back, unit, inverse, gains[1:2, :])
    incoming = f32(incoming) + grad
    lowered = bf(incoming)
    grad_mixed = bf(dot_nt(lowered, output_ref[...]))
    grad_projected = attention_back(grad_mixed, projected_ref[...], chance_ref, 64**-0.5)
    normed, unit, inverse = normalize(start_ref[...], gains[0:1, :])
    back, gain_grad = normalize_back(dot_nt(grad_projected, heads_ref[...]), unit, inverse, gains[0:1, :])
    grad_start = bf(incoming + back)
    start_out[...] = grad_start
    put_attention(outs, normed, grad_projected, mixed_ref[...], lowered, gain_grad, scale_grad, mx, quarter)
    grads[...] = dot_tn(windows_ref[...], swap_halves(grad_start, mx))
    pair_part = jnp.where(is_pair == 1, 1.0, 0.0)
    single_part = 1.0 - pair_part
    for x_rel in range(2):
        for rel in range(4):
            for j in range(2):
                at = x_rel * 256 + j * 128
                first = pl.multiple_of((quarter ^ rel) * 80, 16)
                put(outs, rel, x_rel, 1040 + j * 80, 1120 + j * 80, bf(grads[pl.ds(first, 80), at : at + 128] * single_part))
                first = pl.multiple_of((quarter ^ rel) * 160, 16)
                put(outs, rel, x_rel, 1200 + j * 160, 1360 + j * 160, bf(grads[pl.ds(first, 160), at : at + 128] * pair_part))
            put(outs, rel, x_rel, 1520, SPACE_ROWS, jnp.zeros((SPACE_ROWS - 1520, 128), jnp.bfloat16))


def pixel_fold_kernel(me, start_ref, single_ref, pair_ref, picks_ref, wins_ref, pixel_out, embed):
    is_pair = me[2]
    embed[...] = jnp.zeros_like(embed)

    @pl.when(is_pair == 1)
    def _():
        embed[0:600, :] = pair_ref[...]

    @pl.when(is_pair == 0)
    def _():
        embed[0:300, :] = single_ref[...]

    window_grads = bf(dot_nt(start_ref[...], embed[...]))
    own = own_columns(256)
    picks = picks_ref[...]
    for f in range(2):
        folded = narrow(dot_nt(window_grads, wins_ref[f]))
        frame = None
        for i in range(KERN):
            spread = bf(jnp.where(own, dot_nt(folded, picks_of(picks, i)), 0.0))
            lift = bf(jnp.where(iota((128, 256), 0) == 8 * (iota((128, 256), 1) >> 4) + i - 1, 1.0, 0.0))
            part = dot(lift, spread)
            frame = part if frame is None else frame + part
        for ch in range(3):
            pixel_out[(f * 3 + ch) * 128 : (f * 3 + ch) * 128 + 128, :] = bf(frame[:, ch * 128 : ch * 128 + 128])


def slots_seen():
    def parts(dim):
        t = iota((256, 256), dim)
        index = (t >> 4) & 3
        slot = jnp.where(t < 128, jnp.where(index == 0, 0, index + 4), index + 1)
        return ((t >> 2) & 16) | (t & 15), slot

    here, query = parts(0)
    there, key = parts(1)
    near = (key <= query) & (((key < VSTEPS) & (query < VSTEPS)) | (key == query))
    return (here == there) & near


def cotangent_kernel(
    me, cot_ref, edges_ref, single_ref, pair_ref, picks_ref, wins_ref, rows_ref, cut_out, grad_out,
    unpatch_one, unpatch_two, cot,
):
    fill_unpatch(unpatch_one, unpatch_two, single_ref, pair_ref)
    own = own_columns(384)
    picks = picks_ref[...]
    cot[...] = f32(cot_ref[...])
    places = rows_ref[...]
    cut = None
    for i in range(KERN):
        parts = []
        for ch in range(3):
            if i == 0:
                parts.append(edges_ref[pl.ds(ch, 24, stride=3), :])
            elif i == KERN - 1:
                parts.append(edges_ref[pl.ds(72 + ch, 24, stride=3), :])
            else:
                parts.append(cot[pl.ds(ch * 8 + i - 1, 24, stride=24), :])
        row = jnp.concatenate([jnp.concatenate(parts, 1), jnp.zeros((8, 384), jnp.float32)], 0)
        spread = bf(jnp.where(own, dot(places, bf(row)), 0.0))
        part = dot(spread, picks_of(picks, i))
        cut = part if cut is None else cut + part
    wide = widen(cut)
    one = bf(dot(wide[:128], wins_ref[0, :, 0:384]))
    two = bf(dot(wide[128:256], wins_ref[0]) + dot(wide[256:], wins_ref[1]))
    cut_out[:, 0:384] = one
    cut_out[:, 384:1024] = two
    grad_out[...] = jnp.concatenate([dot(one, unpatch_one[...]), dot(two, unpatch_two[...])], 0)


def fill_unpatch(unpatch_one, unpatch_two, single_ref, pair_ref):
    unpatch_one[...] = jnp.zeros_like(unpatch_one)
    unpatch_two[...] = jnp.zeros_like(unpatch_two)
    unpatch_one[0:300, :] = single_ref[...]
    unpatch_two[0:600, :] = pair_ref[...]


def rebuilt_kernel(me, final_ref, single_ref, pair_ref, picks_ref, wins_ref, sums_ref, rebuilt_out, rims_out, unpatch_one, unpatch_two):
    fill_unpatch(unpatch_one, unpatch_two, single_ref, pair_ref)
    own = own_columns(384)
    picks = picks_ref[...]
    one = bf(dot_nt(final_ref[0:128, :], unpatch_one[...]))
    two = bf(dot_nt(final_ref[128:256, :], unpatch_two[...]))
    folded = jnp.concatenate(
        [
            narrow(dot_nt(one, wins_ref[0, :, 0:384])),
            narrow(dot_nt(two, wins_ref[0])),
            narrow(dot_nt(two, wins_ref[1])),
        ],
        0,
    )
    sums = sums_ref[...]
    for i in range(KERN):
        spread = bf(jnp.where(own, dot_nt(folded, picks_of(picks, i)), 0.0))
        row = dot(sums, spread)
        if i == 0:
            rims_out[0:32, :] = bf(row)
        elif i == KERN - 1:
            rims_out[32:64, :] = bf(row)
        else:
            for ch in range(3):
                rebuilt_out[pl.ds(ch * 8 + i - 1, 24, stride=24), :] = row[:24, ch * 128 : ch * 128 + 128]


def temporal_one_kernel(
    me, middle_ref, incoming_ref, gains, heads_ref, output_ref, up_ref, down_ref,
    both_out, grad_out, gain_out, projected_out, chance_out, mixed_out, final_out,
    slope_ref,
):
    middle = f32(middle_ref[...])
    normed, _, _ = normalize(middle, gains[2:3, :])
    projected = bf(dot(normed, heads_ref[...]))
    projected_out[...] = projected
    mixed = attention(projected, slots_seen(), chance_out, 64**-0.5)
    mixed_out[...] = mixed
    resid = middle + dot(mixed, output_ref[...])
    second, unit, inverse = normalize(resid, gains[3:4, :])
    incoming = incoming_ref[...]
    lowered = bf(incoming)
    both_out[0] = second
    both_out[1] = lowered
    final_out[...] = bf(resid + feed_forward(second, up_ref, down_ref, slope_ref))
    back = feed_forward_back(lowered, up_ref, down_ref, slope_ref)
    grad, gain_grad = normalize_back(back, unit, inverse, gains[3:4, :])
    grad_out[...] = incoming + grad
    gain_out[...] = jnp.broadcast_to(gain_grad, gain_out.shape)


def temporal_two_kernel(
    me, incoming_ref, gains, middle_ref, projected_ref, chance_ref, heads_ref, output_ref,
    grad_out, projected_out, lowered_out, normed_out, gain_out,
):
    incoming = incoming_ref[...]
    lowered = bf(incoming)
    lowered_out[...] = lowered
    grad_mixed = bf(dot_nt(lowered, output_ref[...]))
    grad_projected = attention_back(grad_mixed, projected_ref[...], chance_ref, 64**-0.5)
    projected_out[...] = grad_projected
    normed, unit, inverse = normalize(f32(middle_ref[...]), gains[2:3, :])
    normed_out[...] = normed
    back, gain_grad = normalize_back(dot_nt(grad_projected, heads_ref[...]), unit, inverse, gains[2:3, :])
    gain_out[...] = jnp.broadcast_to(gain_grad, gain_out.shape)
    grad_out[...] = bf(incoming + back)


def temporal_grad_kernel(
    me, normed_ref, projected_ref, mixed_ref, lowered_ref, gain_ref, scale_ref, final_ref, cut_ref,
    keep_out, send_near, send_far,
    grads,
):
    mx, quarter = me[0], me[1]
    outs = (keep_out, send_near, send_far)
    put_attention(
        outs, normed_ref[...], projected_ref[...], mixed_ref[...], lowered_ref[...], gain_ref[0:1, :], scale_ref[0:1, :],
        mx, quarter,
    )
    final = swap_halves(final_ref[...], mx)
    grads[0:384, :] = dot_tn(cut_ref[:, 0:384], final[:128])
    grads[384:1024, :] = dot_tn(cut_ref[:, 384:1024], final[128:])
    for x_rel in range(2):
        for rel in range(4):
            for j in range(2):
                at = x_rel * 256 + j * 128
                first = pl.multiple_of((quarter ^ rel) * 96, 16)
                put(outs, rel, x_rel, 1040 + j * 96, 1136 + j * 96, bf(grads[pl.ds(first, 96), at : at + 128]))
                first = pl.multiple_of(384 + (quarter ^ rel) * 160, 16)
                put(outs, rel, x_rel, 1232 + j * 160, 1392 + j * 160, bf(grads[pl.ds(first, 160), at : at + 128]))
            put(outs, rel, x_rel, 1552, TIME_ROWS, jnp.zeros((TIME_ROWS - 1552, 128), jnp.bfloat16))


TIME_ROWS = 1600
SPACE_ROWS = 1536


class Leaving:
    def __init__(self, semaphores):
        self.semaphores, self.copies = semaphores, []

    def send(self, source, out):
        copy = pltpu.make_async_copy(source, out, self.semaphores.at[len(self.copies)])
        copy.start()
        self.copies.append(copy)

    def wait(self):
        for copy in self.copies:
            copy.wait()


def unpack_feed(me, sources, first, up_out, down_out, up, down, leaving):
    for rel, source in enumerate(sources):
        at = pl.multiple_of((me[1] ^ rel) * 512, 512)
        for j in range(2):
            rows = slice(first + 1024 + j * 512, first + 1536 + j * 512)
            down[pl.ds(at, 512), j * 128 : j * 128 + 128] = f32(source[rows, :])
        leaving.send(down.at[pl.ds(at, 512), :], down_out.at[pl.ds(at, 512), :])
    for rel, source in enumerate(sources):
        at = pl.multiple_of((me[1] ^ rel) * 512, 512)
        for j in range(4):
            rows = slice(first + j * 256, first + j * 256 + 256)
            up[:, pl.ds(pl.multiple_of(at + j * 128, 128), 128)] = f32(source[rows, :])
        leaving.send(up.at[:, pl.ds(at, 512)], up_out.at[:, pl.ds(at, 512)])


def unpack_rest(
    me, sources, first, one, two, heads_out, output_out, gains_out, single_out, pair_out, heads, output, gains, single, pair,
    leaving,
):
    for rel, source in enumerate(sources):
        quarter = me[1] ^ rel
        for j in range(3):
            at = pl.multiple_of(quarter * 384 + j * 128, 128)
            heads[:, pl.ds(at, 128)] = f32(source[first + j * 256 : first + j * 256 + 256, :])
        at = pl.multiple_of(quarter * 384, 128)
        leaving.send(heads.at[:, pl.ds(at, 384)], heads_out.at[:, pl.ds(at, 384)])
    gains[...] = f32(sources[0][first + 1024 : first + 1040, :])
    leaving.send(gains, gains_out)
    for rel, source in enumerate(sources):
        quarter = me[1] ^ rel
        at = pl.multiple_of(quarter * 128, 128)
        output[:, pl.ds(at, 128)] = f32(source[first + 768 : first + 1024, :])
        for j in range(2):
            row = first + 1040 + j * one
            at = pl.multiple_of(quarter * one, 16)
            single[pl.ds(at, one), j * 128 : j * 128 + 128] = f32(source[row : row + one, :])
            row = first + 1040 + 2 * one + j * two
            at = pl.multiple_of(quarter * two, 16)
            pair[pl.ds(at, two), j * 128 : j * 128 + 128] = f32(source[row : row + two, :])
    leaving.send(output, output_out)
    single_out[...] = single[0:300, :]
    leaving.send(pair.at[0:600, :], pair_out)


def unpack_kernel(me, *refs, feed, rest):
    sources, refs = refs[:4], refs[4:]
    leaving = Leaving(refs[-1])
    many = 2 * (feed is not None) + 5 * (rest is not None)
    outs, scratch = list(refs[:many]), list(refs[many:-1])
    if feed is not None:
        unpack_feed(me, sources, feed, *outs[:2], *scratch[:2], leaving)
        outs, scratch = outs[2:], scratch[2:]
    if rest is not None:
        unpack_rest(me, sources, *rest, *outs, *scratch, leaving)
    leaving.wait()


def call(kernel, name, outs, args, scratch=(), after=(), vmem=48, micros=1.0, gated=(), leave=()):
    any_space = pl.BlockSpec(memory_space=pl.ANY)
    whole = pl.BlockSpec(memory_space=pltpu.VMEM)
    count, made = len(args), len(outs)
    waits = len(after) + len(gated)

    def body(*refs):
        kernel(*refs[:count], *refs[count + waits : count + waits + made], *refs[count + waits + made + len(gated) :])

    return pl.pallas_call(
        body,
        name=name,
        out_shape=[jax.ShapeDtypeStruct(s, d) for s, d in outs] + [jax.ShapeDtypeStruct(a.shape, a.dtype) for a in gated],
        in_specs=[pl.BlockSpec(memory_space=pltpu.SMEM)] + [whole] * (count - 1) + [any_space] * waits,
        out_specs=[any_space if k in leave else whole for k in range(made)] + [any_space] * len(gated),
        scratch_shapes=[pltpu.VMEM(s, d) for s, d in scratch] + [pltpu.SemaphoreType.DMA((12,))] * (len(leave) > 0),
        input_output_aliases={count + len(after) + k: made + k for k in range(len(gated))},
        compiler_params=pltpu.CompilerParams(vmem_limit_bytes=vmem * MIB),
        cost_estimate=pl.CostEstimate(flops=int(micros * MICRO), bytes_accessed=0, transcendentals=0),
    )(*args, *after, *gated)


def flips(size, bit):
    return [(i, i ^ bit) for i in range(size)]


def total_of(*refs):
    out = f32(refs[0])
    for r in refs[1:]:
        out = out + f32(r)
    return bf(out)


def split_core_kernel(me, keep, *refs, first, count):
    got, (near, far) = refs[:count], refs[count:]
    for half, out in enumerate((near, far)):
        for j in range(2):
            x, y = (half, j) if first == 0 else (j, half)
            came = got[0][x, y] if count == 1 else got[x][y]
            out[j] = total_of(keep[x, y], came)


def split_kernel(me, keep, got, near, far):
    for half, out in enumerate((near, far)):
        out[...] = total_of(keep[half], got[half])


def sum_kernel(me, keep, got, out):
    out[...] = total_of(keep[...], got[...])


def merge_kernel(me, *refs, place, count):
    others, keep, got = list(refs[: count - 1]), refs[count - 1], refs[count]
    outs, whole = refs[count + 1 : -1], refs[-1]
    at = 0
    for k in range(count):
        if k == place:
            rows = keep.shape[0]
            whole[at : at + rows, :] = total_of(keep[...], got[...])
        else:
            ref = others.pop(0)
            rows = ref.shape[0]
            whole[at : at + rows, :] = ref[...]
        at += rows
    if len(outs) == 1:
        outs[0][...] = whole[...]
    else:
        size = whole.shape[0] // 4
        for rel in range(4):
            outs[rel][...] = whole[pl.ds(pl.multiple_of(((me[3] >> 2) ^ rel) * size, 16), size), :]


def quarter_sum_kernel(me, a, b, c, d, out):
    out[...] = total_of(a[...], b[...], c[...], d[...])


def gather_kernel(me, a, b, c, d, out):
    size = a.shape[0]
    for rel, ref in enumerate((a, b, c, d)):
        out[pl.ds(pl.multiple_of(((me[3] >> 2) ^ rel) * size, 16), size), :] = ref[...]


def ends_kernel(me, total, got, out):
    place = me[3] >> 2
    at_end = (place == 0) | (place == 3)

    @pl.when(at_end)
    def _():
        out[...] = got[...]

    @pl.when(jnp.logical_not(at_end))
    def _():
        out[...] = total[...]


class Chain:
    def __init__(self, name, me, near=None, far=None):
        self.name, self.route, self.me = name, ROUTES[name], me
        self.near, self.far = near, far
        self.at = 0

    def launch(self):
        grp, rows = lax.axis_size("grp"), lax.axis_size("rows")
        step = self.route[self.at]
        line = [[z * 4 + i for i in range(4)] for z in range(rows // 4)]
        if step == "C":
            self.got = [lax.ppermute(v, "rows", flips(rows, 1)) for v in self.far]
        elif step in "Xx":
            self.got = lax.ppermute(self.far, "grp", flips(grp, grp // 2))
        elif step in "Yy":
            self.got = lax.ppermute(self.far, "rows", flips(rows, 2))
        elif step == "R":
            self.got = [lax.ppermute(self.parts[k], "rows", flips(rows, 4 * k)) for k in (1, 2, 3)]
        elif step == "G":
            self.got = [lax.ppermute(self.parts[0], "rows", flips(rows, 4 * k)) for k in (1, 2, 3)]
        elif step == "1":
            pairs = list(zip(line[0] + line[3], line[1] + line[2]))
            self.got = lax.ppermute(self.total, "rows", pairs)
        elif step == "2":
            pairs = list(zip(line[1] + line[2], line[2] + line[1]))
            self.got = lax.ppermute(self.total, "rows", pairs)
        elif step == "3":
            pairs = list(zip(line[1] + line[2], line[0] + line[3]))
            self.got = lax.ppermute(self.total, "rows", pairs)
        elif step == "W":
            beside = lax.ppermute(self.total, "rows", flips(rows, 2))
            core = flips(rows, 1)
            self.got = [beside, lax.ppermute(self.total, "rows", core), lax.ppermute(beside, "rows", core)]

    def advance(self, after, gated, chains):
        step, then = self.route[self.at], self.route[self.at + 1 : self.at + 2]
        b16 = jnp.bfloat16

        def run(kernel, outs, args, scratch=()):
            made = [(shape, b16) for shape in outs]
            ahead = [v for c in gated for v in c.far]
            got = call(kernel, self.name + step, made, [self.me, *args], scratch, after, 24, 1.5, ahead)
            rest = got[len(outs) :]
            for c in gated:
                c.far, rest = rest[: len(c.far)], rest[len(c.far) :]
                c.launch()
            return got[: len(outs)]

        self.at += 1
        if step == "C":
            kernel = functools.partial(split_core_kernel, first=0 if then == "X" else 1, count=len(self.got))
            n = self.near.shape[2]
            self.near, self.far = run(kernel, [(2, n, 128)] * 2, [self.near, *self.got])
            token = self.near
        elif step in "XY":
            n = self.near.shape[1]
            self.near, self.far = run(split_kernel, [(n, 128)] * 2, [self.near, self.got])
            token = self.near
        elif step in "xy":
            group = next((g for g in GROUPS if self.name in GROUPS[g]), self.name)
            names = GROUPS.get(group, self.name)
            others = [chains[c].total for c in names if c != self.name and c in chains and hasattr(chains[c], "total")]
            n = self.near.shape[0]
            if len(others) < len(names) - 1:
                (self.total,) = run(sum_kernel, [(n, 128)], [self.near, self.got])
                return self.total
            n += sum(t.shape[0] for t in others)
            kernel = functools.partial(merge_kernel, place=names.index(self.name), count=len(names))
            shapes = [(n // 4, 128)] * 4 if (then if group == self.name else ROUTES[group][0]) == "R" else [(n, 128)]
            outs = run(kernel, shapes, [*others, self.near, self.got], [((n, 128), b16)])
            if group != self.name:
                chains[group] = Chain(group, self.me)
            chains[group].parts = outs
            chains[group].total = outs[0]
            chains[group].launch()
            return outs[0]
        elif step in "12":
            (self.total,) = run(sum_kernel, [self.total.shape], [self.total, self.got])
            token = self.total
        elif step == "3":
            (self.total,) = run(ends_kernel, [self.total.shape], [self.total, self.got])
            token = self.total
        elif step == "R":
            self.parts = run(quarter_sum_kernel, [self.parts[0].shape], [self.parts[0], *self.got])
            token = self.parts[0]
        elif step == "G":
            n = self.parts[0].shape[0] * 4
            (self.total,) = run(gather_kernel, [(n, 128)], [self.parts[0], *self.got])
            token = self.total
        self.launch()
        return token

    def result(self):
        return [self.total, *self.got]


def finish_grp(values, dims):
    grp = lax.axis_size("grp")
    me = lax.axis_index("grp")
    bit = grp // 4
    while bit:
        mine = (me // bit) % 2
        out = []
        for v, dim in zip(values, dims):
            half = v.shape[dim] // 2
            near = lax.dynamic_slice_in_dim(v, mine * half, half, dim)
            far = lax.dynamic_slice_in_dim(v, (1 - mine) * half, half, dim)
            out.append(near + f32(lax.ppermute(bf(far), "grp", flips(grp, bit))))
        values = out
        bit //= 2
    return values


def on_device(
    pixels,
    cotangent,
    embed_single,
    embed_pair,
    spatial_gain,
    spatial_heads,
    spatial_output,
    spatial_scale,
    spatial_upward,
    spatial_down,
    temporal_gain,
    temporal_heads,
    temporal_output,
    temporal_scale,
    temporal_upward,
    temporal_down,
    unpatch_single,
    unpatch_pair,
):
    groups, frames = pixels.shape[:2]
    rows = lax.axis_size("rows")
    assert groups * 8 == rows == GRID and frames == 12 and pixels.shape[3] == STRIDE
    grp = lax.axis_size("grp")
    at = lax.axis_index("rows")
    core, along_y = at & 1, (at >> 1) & 1
    me = jnp.stack(
        [
            lax.axis_index("grp") // (grp // 2),
            core * 2 + along_y,
            jnp.where(at >= 8, 1, 0),
            at,
        ]
    ).astype(jnp.int32)
    picks = jnp.asarray(column_picks())
    wins = jnp.asarray(np.stack([window_picks(0, 640), window_picks(300, 640)]))
    places = frame_rows()
    sums = jnp.asarray(places.T)
    places = jnp.asarray(places)
    gains = f32(jnp.stack([spatial_gain, spatial_scale, temporal_gain, temporal_scale]))

    (sent,) = call(slots_kernel, "slots", [((16, 2, CHAN, STRIDE, 128), jnp.bfloat16)], [me, pixels])
    got = lax.all_to_all(sent, "rows", 0, 0)
    images = jnp.transpose(got, (1, 2, 0, 3, 4)).reshape(2 * CHAN * 128, 128)

    up = [(i, i + 1) for i in range(rows - 1)]
    down = [(i + 1, i) for i in range(rows - 1)]
    above = lax.ppermute(cotangent[:, :, :, 7, :], "rows", up)
    below = lax.ppermute(cotangent[:, :, :, 0, :], "rows", down)
    edges = f32(jnp.concatenate([above.reshape(72, 128), below.reshape(72, 128)], 0))

    b16, w32 = jnp.bfloat16, jnp.float32
    half = 256
    made, chains = {}, {}
    token = []

    def start(name, keep, send):
        chains[name] = Chain(name, me, keep, send)
        if name not in "".join(GATES.values()):
            chains[name].launch()

    def pieces(count):
        return [((2, 2, count, 128), b16)] + [((2, count, 128), b16)] * 2

    def shared(v):
        core = flips(rows, 1)
        across = lax.ppermute(v, "grp", flips(grp, grp // 2))
        return [v, lax.ppermute(v, "rows", core), across, lax.ppermute(across, "rows", core)]

    def feed_grads(name, label, shares, up_weight, down_weight):
        near, far = call(
            feed_grad_kernel,
            label,
            [((2048, 128), b16)] * 2,
            [me, *shares, up_weight, down_weight],
            [((1024, 512), b16)] * 4,
            after=token,
            micros=7,
        )
        start(name, near, far)
        return near

    def cut():
        out = call(
            cotangent_kernel,
            "cotangent_windows",
            [((128, 1024), b16), ((256, 512), w32)],
            [me, cotangent.reshape(576, 128), edges, unpatch_single.T, unpatch_pair.T, picks, wins, places],
            [((384, 512), b16), ((640, 512), b16), ((576, 128), w32)],
            after=token,
            micros=5,
        )
        made["cut"] = out
        return out[0]

    def spatial():
        out = call(
            spatial_forward_kernel,
            "spatial_forward",
            [
                ((256, 640), b16),
                ((256, 512), w32),
                ((256, 1536), b16),
                ((8, 256, 256), b16),
                ((256, 512), b16),
                ((256, 512), w32),
                ((256, 512), b16),
                ((256, 2048), b16),
                ((256, 512), b16),
            ],
            [me, images, embed_single, embed_pair, gains, spatial_heads, spatial_output, spatial_upward, spatial_down, picks, wins],
            [((640, 512), b16)],
            after=token + [edges],
            micros=13,
        )
        made["spatial"] = out
        made["middle"] = lax.all_to_all(out[8].reshape(16, 16, 512), "rows", 0, 0).reshape(256, 512)
        made["seconds"] = shared(out[6])
        return out[6]

    def temporal_one():
        out = call(
            temporal_one_kernel,
            "temporal_one",
            [
                ((2, 256, 512), b16),
                ((256, 512), w32),
                ((8, 512), w32),
                ((256, 1536), b16),
                ((8, 256, 256), b16),
                ((256, 512), b16),
                ((256, 512), b16),
            ],
            [me, made["middle"], made["cut"][1], gains, temporal_heads, temporal_output, temporal_upward, temporal_down],
            [((256, 2048), b16)],
            after=token + made["seconds"][1:],
            micros=9,
        )
        made["temporal"] = out[1:]
        made["temporal shares"] = shared(out[0])
        return out[2]

    def temporal_two():
        grad, _, projected, chance, _, _ = made["temporal"]
        grad_middle, *rest = call(
            temporal_two_kernel,
            "temporal_two",
            [((256, 512), b16), ((256, 1536), b16), ((256, 512), b16), ((256, 512), b16), ((8, 512), w32)],
            [me, grad, gains, made["middle"], projected, chance, temporal_heads, temporal_output],
            after=token,
            micros=5,
        )
        made["temporal back"] = rest
        made["grad_middle"] = lax.all_to_all(grad_middle.reshape(16, 16, 512), "rows", 0, 0).reshape(256, 512)
        return rest[0]

    def temporal_grads():
        _, scale_grad, _, _, mixed, final = made["temporal"]
        grad_projected, lowered, normed, gain_grad = made["temporal back"]
        keep, *send = call(
            temporal_grad_kernel,
            "temporal_grads",
            pieces(TIME_ROWS),
            [me, normed, grad_projected, mixed, lowered, gain_grad, scale_grad, final, made["cut"][0]],
            [((1024, 512), w32)],
            after=token,
            micros=4,
        )
        start("b", keep, send)
        return keep

    def temporal_feed():
        return feed_grads("a", "temporal_feed", made["temporal shares"], temporal_upward, temporal_down)

    def back():
        windows, first, projected, chance, mixed, resid, _, slope, _ = made["spatial"]
        made["grads in"] = shared(made["grad_middle"])
        keep, *send, grad_start = call(
            spatial_back_kernel,
            "spatial_back",
            pieces(SPACE_ROWS) + [((256, 512), b16)],
            [
                me, made["grad_middle"], gains, resid, slope, first, projected, chance, mixed, windows, spatial_upward,
                spatial_down, spatial_heads, spatial_output,
            ],
            [((640, 512), w32)],
            after=token,
            micros=12,
        )
        made["grad_start"] = grad_start
        start("d", keep, send)
        return grad_start

    def spatial_feed():
        return feed_grads("c", "spatial_feed", made["seconds"] + made["grads in"], spatial_upward, spatial_down)

    def fold_pixels():
        (frames_out,) = call(
            pixel_fold_kernel,
            "pixel_fold",
            [((768, 128), b16)],
            [me, made["grad_start"], embed_single, embed_pair, picks, wins],
            [((640, 512), b16)],
            after=token,
            micros=7,
        )
        sent = jnp.transpose(frames_out.reshape(2, CHAN, GRID, STRIDE, 128), (2, 0, 1, 3, 4))
        made["pixels"] = lax.all_to_all(sent, "rows", 0, 0)
        return frames_out

    def fold_rebuilt():
        whole, rims = call(
            rebuilt_kernel,
            "rebuilt_fold",
            [((576, 128), w32), ((64, 384), b16)],
            [me, made["temporal"][5], unpatch_single.T, unpatch_pair.T, picks, wins, sums],
            [((384, 512), b16), ((640, 512), b16)],
            after=token,
            micros=5,
        )
        top = rims[0:24].reshape(2, 12, CHAN, 1, 128)
        bottom = rims[32:56].reshape(2, 12, CHAN, 1, 128)
        made["rebuilt"] = whole, lax.ppermute(bottom, "rows", up), lax.ppermute(top, "rows", down)
        return rims

    def unpack(name):
        feed = 0 if name in "act" else None
        rest = {"b": (0, 96, 160), "d": (0, 80, 160), "t": (2048, 96, 160)}.get(name)
        outs, scratch, leave = [], [], []
        if feed is not None:
            outs += [((half, 2048), w32), ((2048, half), w32)]
            scratch += outs
            leave += [0, 1]
        if rest is not None:
            leave += [len(outs) + k for k in (0, 1, 2, 4)]
            some = [((half, 1536), w32), ((half, 512), w32), ((16, 128), w32)]
            outs += some + [((300, half), w32), ((600, half), w32)]
            scratch += some + [((4 * rest[1], half), w32), ((4 * rest[2], half), w32)]
        kernel = functools.partial(unpack_kernel, feed=feed, rest=rest)
        made[name] = call(kernel, "unpack_" + name, outs, [me, *chains[name].result()], scratch, token, 48, 3, (), leave)
        return chains[name].result()[1]

    work = {
        "cut": cut, "A": spatial, "T1": temporal_one, "T2": temporal_two, "T3": temporal_feed, "TG": temporal_grads, "C1": back, "C3": spatial_feed,
        "F": fold_rebuilt, "P": fold_pixels,
    }
    for step in ORDER:
        if step in work:
            out = work[step]()
        elif step[1] == "U":
            out = unpack(step[0])
        else:
            out = chains[step[0]].advance(token, [chains[c] for c in GATES.get(step, "")], chains)
        token[:] = [out]

    got = f32(made["pixels"])
    singles = got[:8, 0].reshape(2, 4, CHAN, STRIDE, 128)
    pairs = got[8:].reshape(2, 8, CHAN, STRIDE, 128)
    pixel_gradient = jnp.concatenate([singles[:, :1], pairs, singles[:, 1:]], 1)

    whole, from_above, from_below = made["rebuilt"]
    gap = jnp.zeros((2, 12, CHAN, STRIDE - 2, 128), w32)
    rebuilt = whole.reshape(2, 12, CHAN, STRIDE, 128) + jnp.concatenate([f32(from_above), gap, f32(from_below)], 3)

    t_up, t_down, t_heads, t_output, t_gains, un_single, un_pair = made.get("t") or made["a"] + made["b"]
    s_up, s_down = made["c"]
    s_heads, s_output, s_gains, em_single, em_pair = made["d"]
    grads = [
        em_single,
        em_pair,
        s_gains[0:2].reshape(256),
        s_heads,
        s_output,
        s_gains[2:4].reshape(256),
        s_up,
        s_down,
        t_gains[0:2].reshape(256),
        t_heads,
        t_output,
        t_gains[2:4].reshape(256),
        t_up,
        t_down,
        un_single.T,
        un_pair.T,
    ]
    dims = [1, 1, 0, 0, 0, 0, 0, 1, 0, 0, 0, 0, 0, 1, 0, 0]
    return (rebuilt, pixel_gradient, *finish_grp(grads, dims))


def solution(mesh):
    in_specs = (
        P("grp", None, None, "rows", None),
        P("grp", None, None, "rows", None),
    ) + (P(),) * 16
    out_specs = (
        P("grp", None, None, "rows", None),
        P("grp", None, None, "rows", None),
        P(None, "grp"),
        P(None, "grp"),
        P("grp"),
        P("grp", None),
        P("grp", None),
        P("grp"),
        P("grp", None),
        P(None, "grp"),
        P("grp"),
        P("grp", None),
        P("grp", None),
        P("grp"),
        P("grp", None),
        P(None, "grp"),
        P("grp", None),
        P("grp", None),
    )
    return jax.shard_map(
        on_device, mesh=mesh, in_specs=in_specs, out_specs=out_specs, check_vma=False
    )
```

```python
import functools

import jax
import jax.numpy as jnp
import numpy as np
from jax import lax
from jax.experimental import pallas as pl
from jax.experimental.pallas import tpu as pltpu
from jax.sharding import PartitionSpec as P

HEADS = 8
STRIDE = 8
KERN = 10
GRID = 16
VSTEPS = 5
CHAN = 3
LANES = 128

epsilon = 1e-05
gelu_coef = 0.7978845608028654
cubic_coef = 0.044715
masked_score = -1000000000.0

WIN = CHAN * KERN * KERN
CUTS = KERN * CHAN * STRIDE
SINGLE_FRAMES = (0, 9, 10, 11)
MIB = 1 << 20
MICRO = 1_000_000_000


def column_picks():
    n = np.arange(256)
    chan, bit = (n % 24) // 8, n % 8
    at = np.arange(CHAN * 128)
    return ((n < CUTS) & (at[:, None] // 128 == chan) & (at[:, None] % 8 == bit)).astype(jnp.bfloat16)


def window_picks(first, width):
    n = np.arange(256)
    row, chan, bit = n // 24, (n % 24) // 8, n % 8
    w = np.arange(width) - first
    hit = (w >= 0) & (w < WIN)
    same = hit & (n < CUTS)[:, None] & (chan[:, None] == w // 100) & (row[:, None] == (w % 100) // 10)
    step = w % 10
    own = same & (step == bit[:, None] + 1)
    before = same & (step == 0) & (bit[:, None] == 7)
    after = same & (step == 9) & (bit[:, None] == 0)
    return np.concatenate([own, before, after], 0).astype(jnp.bfloat16)


def frame_rows():
    order = (SINGLE_FRAMES, (1, 3, 5, 7), (2, 4, 6, 8))
    out = np.zeros((384, 32), np.float32)
    for k in range(3):
        for g in range(2):
            for i in range(4):
                at = ((k * 2 + g) * 4 + i) * 16
                out[at : at + 16, g * 12 + order[k][i]] = 1
    return out.astype(jnp.bfloat16)


ROUTES = {"a": "y123W", "b": "CXy123W", "c": "y123W", "d": "CXy123W"}
AFTER = {}
GATES = {"g0": "b", "g1": "d"}
GROUPS = {}
ORDER = (
    "A", "cut", "T1", "TG", "g0", "bC", "F", "C1", "g1", "bX", "dC", "T3", "ay", "C3", "by", "a1", "cy", "dX", "b1",
    "a2", "c1", "dy", "b2", "a3", "c2", "d1", "P", "b3", "aU", "c3", "d2", "bU", "d3", "cU", "dU",
)


def dot(a, b):
    return jnp.dot(a, b, preferred_element_type=jnp.float32)


def dot_nt(a, b):
    return lax.dot_general(a, b, (((1,), (1,)), ((), ())), preferred_element_type=jnp.float32)


def dot_tn(a, b):
    return lax.dot_general(a, b, (((0,), (0,)), ((), ())), preferred_element_type=jnp.float32)


def bf(x):
    return x.astype(jnp.bfloat16)


def f32(x):
    return x.astype(jnp.float32)


def iota(shape, dim):
    return lax.broadcasted_iota(jnp.int32, shape, dim)


def own_columns(rows):
    return ((iota((rows, 384), 1) & 127) >> 3) == (iota((rows, 384), 0) & 15)


def picks_of(picks, i):
    lane = iota((1, 256), 1)
    return picks * bf(jnp.where((lane >= 24 * i) & (lane < 24 * i + 24), 1.0, 0.0))


def shift_up(v):
    return jnp.where((iota(v.shape, 0) & 15) == 15, 0.0, pltpu.roll(v, v.shape[0] - 1, 0))


def shift_down(v):
    return jnp.where((iota(v.shape, 0) & 15) == 0, 0.0, pltpu.roll(v, 1, 0))


def widen(v):
    return bf(jnp.concatenate([v, shift_down(v), shift_up(v)], 1))


def narrow(t):
    return bf(t[:, :256] + shift_up(t[:, 256:512]) + shift_down(t[:, 512:]))


def normalize(x, gain):
    centered = x - jnp.mean(x, -1, keepdims=True)
    inverse = lax.rsqrt(jnp.mean(centered * centered, -1, keepdims=True) + epsilon)
    unit = centered * inverse
    return bf(unit * gain), unit, inverse


def normalize_back(incoming, unit, inverse, gain):
    scaled = incoming * gain
    gain_grad = jnp.sum(incoming * unit, 0, keepdims=True)
    first = jnp.mean(scaled, -1, keepdims=True)
    second = jnp.mean(scaled * unit, -1, keepdims=True)
    return inverse * (scaled - first - unit * second), gain_grad


def halves_mask(width=128):
    lane = iota((1, width), 1)
    return lane < 64


def attention(projected, seen, chance_ref, scale):
    low = halves_mask()
    keep = (bf(jnp.where(low, 1.0, 0.0)), bf(jnp.where(low, 0.0, 1.0)))
    outs = []
    for pair in range(HEADS // 2):
        q = projected[:, pair * 128 : pair * 128 + 128]
        k = projected[:, 512 + pair * 128 : 512 + pair * 128 + 128]
        v = projected[:, 1024 + pair * 128 : 1024 + pair * 128 + 128]
        both = []
        for half in range(2):
            scores = dot_nt(q * keep[half], k) * scale
            if seen is not None:
                scores = jnp.where(seen, scores, masked_score)
            powers = jnp.exp(scores - jnp.max(scores, -1, keepdims=True))
            chance = bf(powers * (1.0 / jnp.sum(powers, -1, keepdims=True)))
            chance_ref[2 * pair + half] = chance
            both.append(dot(chance, v))
        outs.append(jnp.where(low, both[0], both[1]))
    return bf(jnp.concatenate(outs, 1))


def attention_back(grad_mixed, projected, chance_ref, scale):
    low = halves_mask()
    keep = (bf(jnp.where(low, 1.0, 0.0)), bf(jnp.where(low, 0.0, 1.0)))
    grads = ([], [], [])
    for pair in range(HEADS // 2):
        q = projected[:, pair * 128 : pair * 128 + 128]
        k = projected[:, 512 + pair * 128 : 512 + pair * 128 + 128]
        v = projected[:, 1024 + pair * 128 : 1024 + pair * 128 + 128]
        g = grad_mixed[:, pair * 128 : pair * 128 + 128]
        both = ([], [], [])
        for half in range(2):
            chance = chance_ref[2 * pair + half]
            wide = f32(chance)
            grad_chance = dot_nt(g * keep[half], v)
            inner = jnp.sum(wide * grad_chance, -1, keepdims=True)
            grad_scores = bf(wide * (grad_chance - inner))
            both[0].append(dot(grad_scores, k))
            both[1].append(dot_tn(grad_scores, q))
            both[2].append(dot_tn(chance, g))
        for part, factor in zip(range(3), (scale, scale, 1.0)):
            grads[part].append(bf(jnp.where(low, both[part][0], both[part][1]) * factor))
    return jnp.concatenate(grads[0] + grads[1] + grads[2], 1)


def gelu_parts(inner):
    square = inner * inner
    bent = jnp.tanh(gelu_coef * inner * (1.0 + cubic_coef * square))
    half = 0.5 * (1.0 + bent)
    slope = half + 0.5 * inner * (1.0 - bent * bent) * gelu_coef * (1.0 + 3.0 * cubic_coef * square)
    return bf(inner * half), slope


def feed_forward(second, up_ref, down_ref, slope_ref):
    total = None
    for k in range(4):
        columns = slice(k * 512, k * 512 + 512)
        active, slope = gelu_parts(dot(second, up_ref[:, columns]))
        slope_ref[:, columns] = bf(slope)
        part = dot(active, down_ref[columns, :])
        total = part if total is None else total + part
    return total


def feed_forward_back(lowered, up_ref, down_ref, slope_ref):
    total = None
    for k in range(4):
        columns = slice(k * 512, k * 512 + 512)
        grad_inner = bf(dot_nt(lowered, down_ref[columns, :]) * f32(slope_ref[:, columns]))
        part = dot_nt(grad_inner, up_ref[:, columns])
        total = part if total is None else total + part
    return total


def feed_grad_kernel(me, *refs):
    *shares, up, down, near, far, second, incoming, active, grad_inner = refs
    for k in range(4):
        rows = slice(k * 256, k * 256 + 256)
        if len(shares) == 4:
            second[rows, :] = shares[k][0]
            incoming[rows, :] = shares[k][1]
        else:
            second[rows, :] = shares[k][...]
            incoming[rows, :] = shares[4 + k][...]
    half = pl.ds(pl.multiple_of(me[0] * 256, 256), 256)
    up_ref, down_ref = held(up), held(down)
    for rel, out in enumerate((near, far)):
        at = pl.multiple_of((me[1] ^ rel) * 512, 512)
        up_part, down_part = up_ref[:, pl.ds(at, 512)], down_ref[pl.ds(at, 512), :]
        for k in range(4):
            rows = slice(k * 256, k * 256 + 256)
            act, slope = gelu_parts(dot(second[rows, :], up_part))
            active[rows, :] = act
            grad_inner[rows, :] = bf(dot_nt(incoming[rows, :], down_part) * slope)
        up_grad = dot_tn(second[:, half], grad_inner[...])
        for j in range(4):
            out[j * 256 : j * 256 + 256, :] = bf(up_grad[:, j * 128 : j * 128 + 128])
        down_grad = dot_tn(active[...], incoming[:, half])
        for j in range(2):
            out[1024 + j * 512 : 1536 + j * 512, :] = bf(down_grad[:, j * 128 : j * 128 + 128])


def swap_halves(v, bit):
    half = v.shape[1] // 2
    return jnp.where(bit == 1, jnp.concatenate([v[:, half:], v[:, :half]], 1), v)


def swap_quarters(v, quarter):
    v = swap_halves(v, quarter >> 1)
    half = v.shape[1] // 2
    return jnp.concatenate([swap_halves(v[:, :half], quarter & 1), swap_halves(v[:, half:], quarter & 1)], 1)


def put(outs, rel, x_rel, first, last, value):
    if rel < 2:
        outs[0][x_rel, rel, first:last, :] = value
    elif len(outs) == 2:
        outs[1][x_rel, rel & 1, first:last, :] = value
    else:
        outs[1 + x_rel][rel & 1, first:last, :] = value


def put_columns(outs, x_rel, at, value, count):
    rows, width = value.shape[0], value.shape[1] // 4
    for rel in range(4):
        for j in range(width // LANES):
            block = value[:, rel * width + j * LANES : rel * width + (j + 1) * LANES]
            put(outs, rel, x_rel, at + j * rows, at + (j + 1) * rows, bf(block))


def put_rows(outs, x_rel, at, source, row0, rows, quarter):
    size = rows // 4
    blocks = source.shape[1] // LANES
    for rel in range(4):
        first = pl.multiple_of(row0 + (quarter ^ rel) * size, 16)
        for j in range(blocks):
            put(outs, rel, x_rel, at + j * size, at + (j + 1) * size, bf(source[pl.ds(first, size), j * LANES : (j + 1) * LANES]))


def put_attention(outs, normed, grad_projected, mixed, lowered, first_grad, second_grad, mx, quarter):
    heads = dot_tn(swap_halves(normed, mx), swap_quarters(grad_projected, quarter))
    output = dot_tn(swap_halves(mixed, mx), swap_quarters(lowered, quarter))
    gains = (swap_halves(first_grad, mx), swap_halves(second_grad, mx))
    row = iota((16, 128), 0)
    for x_rel in range(2):
        put_columns(outs, x_rel, 0, heads[x_rel * 256 : x_rel * 256 + 256], 3)
        put_columns(outs, x_rel, 768, output[x_rel * 256 : x_rel * 256 + 256], 1)
        block = jnp.zeros((16, 128), jnp.float32)
        for j in range(4):
            at = x_rel * 256 + (j & 1) * 128
            block = jnp.where(row == j, gains[j >> 1][:, at : at + 128], block)
        for rel in range(4):
            put(outs, rel, x_rel, 1024, 1040, bf(block))


def fill_embed(embed, single_ref, pair_ref, is_pair):
    embed[...] = jnp.zeros_like(embed)

    @pl.when(is_pair == 1)
    def _():
        embed[0:600, :] = pair_ref[...]

    @pl.when(is_pair == 0)
    def _():
        embed[0:300, :] = single_ref[...]


def gate_kernel(me, out):
    out[...] = jnp.zeros_like(out)


def slots_kernel(me, pixels, cot_ref, out, last, first, cot):
    cot[...] = f32(cot_ref[...])
    last[...] = bf(cot[pl.ds(7, 72, stride=8), :])
    first[...] = bf(cot[pl.ds(0, 72, stride=8), :])
    for g in range(2):
        for k in range(4):
            single = pixels[g, SINGLE_FRAMES[k]]
            out[g * 4 + k, 0] = single
            out[g * 4 + k, 1] = single
            out[8 + g * 4 + k, 0] = pixels[g, 2 * k + 1]
            out[8 + g * 4 + k, 1] = pixels[g, 2 * k + 2]


def spatial_forward_kernel(
    me, frames, single, pair, gains, heads, output, up, down, picks_ref, wins,
    windows_out, start_out, projected_out, chance_out, mixed_out, resid_out, second_out, slope_out, middle_out,
    embed,
    post,
):
    is_pair = me[2]
    own = own_columns(256)
    picks = picks_ref[...]
    cuts = []
    for f in range(2):
        frame = jnp.concatenate([frames[(f * 3 + ch) * 128 : (f * 3 + ch) * 128 + 128, :] for ch in range(3)], 1)
        cut = None
        for i in range(KERN):
            lift = bf(jnp.where(iota((256, 128), 1) == 8 * (iota((256, 128), 0) >> 4) + i - 1, 1.0, 0.0))
            spread = bf(jnp.where(own, dot(lift, frame), 0.0))
            part = dot(spread, picks_of(picks, i))
            cut = part if cut is None else cut + part
        cuts.append(widen(cut))
    wins_ref = held(wins)
    windows = bf(dot(cuts[0], wins_ref[0]) + dot(cuts[1], wins_ref[1]))
    windows_out[...] = windows
    post(0)
    fill_embed(embed, held(single), held(pair), is_pair)
    start = dot(windows, embed[...])
    start_out[...] = start
    post(1)
    normed, _, _ = normalize(start, gains[0:1, :])
    projected = bf(dot(normed, held(heads)[...]))
    projected_out[...] = projected
    post(2)
    mixed = attention(projected, None, chance_out, 64**-0.5)
    mixed_out[...] = mixed
    post(3, 4)
    resid = start + dot(mixed, held(output)[...])
    resid_out[...] = resid
    post(5)
    second, _, _ = normalize(resid, gains[1:2, :])
    second_out[...] = second
    middle_out[...] = bf(resid + feed_forward(second, held(up), held(down), slope_out))


def spatial_back_kernel(
    me, incoming_ref, gains, resid_ref, slope, start_in, projected, chance, mixed, windows, up, down, heads, output,
    keep_out, send_near, send_far, start_out,
    grads,
):
    mx, quarter, is_pair = me[0], me[1], me[2]
    outs = (keep_out, send_near, send_far)
    incoming = incoming_ref[...]
    _, unit, inverse = normalize(resid_ref[...], gains[1:2, :])
    back = feed_forward_back(incoming, held(up), held(down), held(slope))
    grad, scale_grad = normalize_back(back, unit, inverse, gains[1:2, :])
    incoming = f32(incoming) + grad
    lowered = bf(incoming)
    grad_mixed = bf(dot_nt(lowered, held(output)[...]))
    grad_projected = attention_back(grad_mixed, held(projected)[...], held(chance), 64**-0.5)
    normed, unit, inverse = normalize(held(start_in)[...], gains[0:1, :])
    back, gain_grad = normalize_back(dot_nt(grad_projected, held(heads)[...]), unit, inverse, gains[0:1, :])
    grad_start = bf(incoming + back)
    start_out[...] = grad_start
    put_attention(outs, normed, grad_projected, held(mixed)[...], lowered, gain_grad, scale_grad, mx, quarter)
    grads[...] = dot_tn(held(windows)[...], swap_halves(grad_start, mx))
    pair_part = jnp.where(is_pair == 1, 1.0, 0.0)
    single_part = 1.0 - pair_part
    for x_rel in range(2):
        for rel in range(4):
            for j in range(2):
                at = x_rel * 256 + j * 128
                first = pl.multiple_of((quarter ^ rel) * 80, 16)
                put(outs, rel, x_rel, 1040 + j * 80, 1120 + j * 80, bf(grads[pl.ds(first, 80), at : at + 128] * single_part))
                first = pl.multiple_of((quarter ^ rel) * 160, 16)
                put(outs, rel, x_rel, 1200 + j * 160, 1360 + j * 160, bf(grads[pl.ds(first, 160), at : at + 128] * pair_part))
            put(outs, rel, x_rel, 1520, SPACE_ROWS, jnp.zeros((SPACE_ROWS - 1520, 128), jnp.bfloat16))


def pixel_fold_kernel(me, start_ref, single_ref, pair_ref, picks_ref, wins_ref, pixel_out, embed):
    fill_embed(embed, single_ref, pair_ref, me[2])
    window_grads = bf(dot_nt(start_ref[...], embed[...]))
    own = own_columns(256)
    picks = picks_ref[...]
    for f in range(2):
        folded = narrow(dot_nt(window_grads, wins_ref[f]))
        frame = None
        for i in range(KERN):
            spread = bf(jnp.where(own, dot_nt(folded, picks_of(picks, i)), 0.0))
            lift = bf(jnp.where(iota((128, 256), 0) == 8 * (iota((128, 256), 1) >> 4) + i - 1, 1.0, 0.0))
            part = dot(lift, spread)
            frame = part if frame is None else frame + part
        for ch in range(3):
            pixel_out[(f * 3 + ch) * 128 : (f * 3 + ch) * 128 + 128, :] = bf(frame[:, ch * 128 : ch * 128 + 128])


def slots_seen():
    def parts(dim):
        t = iota((256, 256), dim)
        index = (t >> 4) & 3
        slot = jnp.where(t < 128, jnp.where(index == 0, 0, index + 4), index + 1)
        return ((t >> 2) & 16) | (t & 15), slot

    here, query = parts(0)
    there, key = parts(1)
    near = (key <= query) & (((key < VSTEPS) & (query < VSTEPS)) | (key == query))
    return (here == there) & near


def cotangent_kernel(
    me, cot_ref, edges_ref, single_ref, pair_ref, picks_ref, wins_ref, rows_ref, cut_out, grad_out,
    unpatch_one, unpatch_two, cot,
):
    fill_unpatch(unpatch_one, unpatch_two, single_ref, pair_ref)
    own = own_columns(384)
    picks = picks_ref[...]
    cot[...] = f32(cot_ref[...])
    places = rows_ref[...]
    cut = None
    for i in range(KERN):
        parts = []
        for ch in range(3):
            if i == 0:
                parts.append(edges_ref[pl.ds(ch, 24, stride=3), :])
            elif i == KERN - 1:
                parts.append(edges_ref[pl.ds(72 + ch, 24, stride=3), :])
            else:
                parts.append(cot[pl.ds(ch * 8 + i - 1, 24, stride=24), :])
        row = jnp.concatenate([jnp.concatenate(parts, 1), jnp.zeros((8, 384), jnp.float32)], 0)
        spread = bf(jnp.where(own, dot(places, bf(row)), 0.0))
        part = dot(spread, picks_of(picks, i))
        cut = part if cut is None else cut + part
    wide = widen(cut)
    one = bf(dot(wide[:128], wins_ref[0, :, 0:384]))
    two = bf(dot(wide[128:256], wins_ref[0]) + dot(wide[256:], wins_ref[1]))
    cut_out[:, 0:384] = one
    cut_out[:, 384:1024] = two
    grad_out[...] = jnp.concatenate([dot(one, unpatch_one[...]), dot(two, unpatch_two[...])], 0)


def fill_unpatch(unpatch_one, unpatch_two, single_ref, pair_ref):
    unpatch_one[...] = jnp.zeros_like(unpatch_one)
    unpatch_two[...] = jnp.zeros_like(unpatch_two)
    unpatch_one[0:300, :] = single_ref[...]
    unpatch_two[0:600, :] = pair_ref[...]


def rebuilt_kernel(me, final_ref, single_ref, pair_ref, picks_ref, wins_ref, sums_ref, rebuilt_out, rims_out, unpatch_one, unpatch_two):
    fill_unpatch(unpatch_one, unpatch_two, single_ref, pair_ref)
    own = own_columns(384)
    picks = picks_ref[...]
    one = bf(dot_nt(final_ref[0:128, :], unpatch_one[...]))
    two = bf(dot_nt(final_ref[128:256, :], unpatch_two[...]))
    folded = jnp.concatenate(
        [
            narrow(dot_nt(one, wins_ref[0, :, 0:384])),
            narrow(dot_nt(two, wins_ref[0])),
            narrow(dot_nt(two, wins_ref[1])),
        ],
        0,
    )
    sums = sums_ref[...]
    for i in range(KERN):
        spread = bf(jnp.where(own, dot_nt(folded, picks_of(picks, i)), 0.0))
        row = dot(sums, spread)
        if i == 0:
            rims_out[0:32, :] = bf(row)
        elif i == KERN - 1:
            rims_out[32:64, :] = bf(row)
        else:
            for ch in range(3):
                rebuilt_out[pl.ds(ch * 8 + i - 1, 24, stride=24), :] = row[:24, ch * 128 : ch * 128 + 128]


def temporal_kernel(
    me, middle_ref, incoming_in, gains, heads, output, up, down,
    both_out, grad_out, mixed_out, final_out, projected_out, lowered_out, normed_out, gain_out,
    slope_ref, chance_ref,
    post,
):
    middle = f32(middle_ref[...])
    normed, first_unit, first_inverse = normalize(middle, gains[2:3, :])
    normed_out[...] = normed
    post(6)
    heads_ref = held(heads)
    projected = bf(dot(normed, heads_ref[...]))
    mixed = attention(projected, slots_seen(), chance_ref, 64**-0.5)
    mixed_out[...] = mixed
    post(2)
    output_ref = held(output)
    resid = middle + dot(mixed, output_ref[...])
    second, unit, inverse = normalize(resid, gains[3:4, :])
    incoming = held(incoming_in)[...]
    lowered = bf(incoming)
    both_out[0] = second
    both_out[1] = lowered
    up_ref, down_ref = held(up), held(down)
    final_out[...] = bf(resid + feed_forward(second, up_ref, down_ref, slope_ref))
    post(3)
    back = feed_forward_back(lowered, up_ref, down_ref, slope_ref)
    grad, scale_grad = normalize_back(back, unit, inverse, gains[3:4, :])
    incoming = incoming + grad
    lowered = bf(incoming)
    lowered_out[...] = lowered
    post(5)
    grad_mixed = bf(dot_nt(lowered, output_ref[...]))
    grad_projected = attention_back(grad_mixed, projected, chance_ref, 64**-0.5)
    projected_out[...] = grad_projected
    post(4)
    back, gain_grad = normalize_back(dot_nt(grad_projected, heads_ref[...]), first_unit, first_inverse, gains[2:3, :])
    gain_out[0:8, :] = jnp.broadcast_to(gain_grad, (8, 512))
    gain_out[8:16, :] = jnp.broadcast_to(scale_grad, (8, 512))
    grad_out[...] = bf(incoming + back)


def temporal_grad_kernel(
    me, normed_ref, projected_ref, mixed_ref, lowered_ref, gain_ref, final_ref, cut_ref,
    keep_out, send_near, send_far,
    grads,
):
    mx, quarter = me[0], me[1]
    outs = (keep_out, send_near, send_far)
    put_attention(
        outs, normed_ref[...], projected_ref[...], mixed_ref[...], lowered_ref[...], gain_ref[0:1, :], gain_ref[8:9, :],
        mx, quarter,
    )
    final = swap_halves(final_ref[...], mx)
    grads[0:384, :] = dot_tn(cut_ref[:, 0:384], final[:128])
    grads[384:1024, :] = dot_tn(cut_ref[:, 384:1024], final[128:])
    for x_rel in range(2):
        for rel in range(4):
            for j in range(2):
                at = x_rel * 256 + j * 128
                first = pl.multiple_of((quarter ^ rel) * 96, 16)
                put(outs, rel, x_rel, 1040 + j * 96, 1136 + j * 96, bf(grads[pl.ds(first, 96), at : at + 128]))
                first = pl.multiple_of(384 + (quarter ^ rel) * 160, 16)
                put(outs, rel, x_rel, 1232 + j * 160, 1392 + j * 160, bf(grads[pl.ds(first, 160), at : at + 128]))
            put(outs, rel, x_rel, 1552, TIME_ROWS, jnp.zeros((TIME_ROWS - 1552, 128), jnp.bfloat16))


TIME_ROWS = 1600
SPACE_ROWS = 1536


class Leaving:
    def __init__(self, semaphores):
        self.semaphores, self.copies = semaphores, []

    def send(self, source, out):
        copy = pltpu.make_async_copy(source, out, self.semaphores.at[len(self.copies)])
        copy.start()
        self.copies.append(copy)

    def wait(self):
        for copy in self.copies:
            copy.wait()


def unpack_feed(me, sources, first, up_out, down_out, up, down, leaving):
    for rel, source in enumerate(sources):
        at = pl.multiple_of((me[1] ^ rel) * 512, 512)
        for j in range(2):
            rows = slice(first + 1024 + j * 512, first + 1536 + j * 512)
            down[pl.ds(at, 512), j * 128 : j * 128 + 128] = f32(source[rows, :])
        leaving.send(down.at[pl.ds(at, 512), :], down_out.at[pl.ds(at, 512), :])
    for rel, source in enumerate(sources):
        at = pl.multiple_of((me[1] ^ rel) * 512, 512)
        for j in range(4):
            rows = slice(first + j * 256, first + j * 256 + 256)
            up[:, pl.ds(pl.multiple_of(at + j * 128, 128), 128)] = f32(source[rows, :])
        leaving.send(up.at[:, pl.ds(at, 512)], up_out.at[:, pl.ds(at, 512)])


def unpack_rest(
    me, sources, first, one, two, heads_out, output_out, gains_out, single_out, pair_out, heads, output, gains, single, pair,
    leaving,
):
    for rel, source in enumerate(sources):
        quarter = me[1] ^ rel
        for j in range(3):
            at = pl.multiple_of(quarter * 384 + j * 128, 128)
            heads[:, pl.ds(at, 128)] = f32(source[first + j * 256 : first + j * 256 + 256, :])
        at = pl.multiple_of(quarter * 384, 128)
        leaving.send(heads.at[:, pl.ds(at, 384)], heads_out.at[:, pl.ds(at, 384)])
    gains[...] = f32(sources[0][first + 1024 : first + 1040, :])
    leaving.send(gains, gains_out)
    for rel, source in enumerate(sources):
        quarter = me[1] ^ rel
        at = pl.multiple_of(quarter * 128, 128)
        output[:, pl.ds(at, 128)] = f32(source[first + 768 : first + 1024, :])
        for j in range(2):
            row = first + 1040 + j * one
            at = pl.multiple_of(quarter * one, 16)
            single[pl.ds(at, one), j * 128 : j * 128 + 128] = f32(source[row : row + one, :])
            row = first + 1040 + 2 * one + j * two
            at = pl.multiple_of(quarter * two, 16)
            pair[pl.ds(at, two), j * 128 : j * 128 + 128] = f32(source[row : row + two, :])
    leaving.send(output, output_out)
    single_out[...] = single[0:300, :]
    leaving.send(pair.at[0:600, :], pair_out)


def unpack_kernel(me, *refs, feed, rest):
    sources, refs = refs[:4], refs[4:]
    leaving = Leaving(refs[-1])
    many = 2 * (feed is not None) + 5 * (rest is not None)
    outs, scratch = list(refs[:many]), list(refs[many:-1])
    if feed is not None:
        unpack_feed(me, sources, feed, *outs[:2], *scratch[:2], leaving)
        outs, scratch = outs[2:], scratch[2:]
    if rest is not None:
        unpack_rest(me, sources, *rest, *outs, *scratch, leaving)
    leaving.wait()


class Arriving:
    def __init__(self, source, held, semaphore, line):
        self.held = held
        self.copy = pltpu.make_async_copy(source, held, semaphore)
        self.line = line
        line.append(self)
        self.started = False
        if len(line) <= 3:
            self.start()

    def start(self):
        if not self.started:
            self.started = True
            self.copy.start()

    def ready(self):
        if self.copy is not None:
            self.start()
            self.copy.wait()
            self.copy = None
            for other in self.line:
                if not other.started:
                    other.start()
                    break
        return self.held


def held(ref):
    return ref.ready() if isinstance(ref, Arriving) else ref


def call(
    kernel, name, outs, args, scratch=(), after=(), vmem=60, micros=1.0, gated=(), leave=(), enter=(), post=()
):
    any_space = pl.BlockSpec(memory_space=pl.ANY)
    whole = pl.BlockSpec(memory_space=pltpu.VMEM)
    count, made = len(args), len(outs)
    waits = len(after) + len(gated)
    held = [pltpu.VMEM(args[k].shape, args[k].dtype) for k in enter]
    kept = [pltpu.VMEM(*outs[k]) for k in post]
    own = [pltpu.VMEM(s, d) for s, d in scratch]
    if leave:
        own.append(pltpu.SemaphoreType.DMA((12,)))

    def body(*refs):
        ins = list(refs[:count])
        results = list(refs[count + waits : count + waits + made])
        rest = refs[count + waits + made + len(gated) :]
        mine, rest = rest[: len(own)], rest[len(own) :]
        copies = {}
        line = []
        for n, k in enumerate(enter):
            ins[k] = Arriving(ins[k], rest[n], rest[-2].at[n], line)
        if post:
            places = {}
            for n, k in enumerate(post):
                places[k] = (rest[len(enter) + n], results[k], n)
                results[k] = rest[len(enter) + n]

            def go(*which):
                for k in which:
                    source, out, n = places[k]
                    copies[k] = pltpu.make_async_copy(source, out, rest[-1].at[n])
                    copies[k].start()

            kernel(*ins, *results, *mine, post=go)
            go(*[k for k in post if k not in copies])
        else:
            kernel(*ins, *results, *mine)
        for k in enter:
            ins[k].ready()
        for copy in copies.values():
            copy.wait()

    return pl.pallas_call(
        body,
        name=name,
        out_shape=[jax.ShapeDtypeStruct(s, d) for s, d in outs] + [jax.ShapeDtypeStruct(a.shape, a.dtype) for a in gated],
        in_specs=[pl.BlockSpec(memory_space=pltpu.SMEM)]
        + [any_space if k in enter else whole for k in range(1, count)]
        + [any_space] * waits,
        out_specs=[any_space if k in leave or k in post else whole for k in range(made)] + [any_space] * len(gated),
        scratch_shapes=own
        + held
        + kept
        + [pltpu.SemaphoreType.DMA((max(len(enter), 1),)), pltpu.SemaphoreType.DMA((max(len(post), 1),))],
        input_output_aliases={count + len(after) + k: made + k for k in range(len(gated))},
        compiler_params=pltpu.CompilerParams(vmem_limit_bytes=vmem * MIB),
        cost_estimate=pl.CostEstimate(flops=int(micros * MICRO), bytes_accessed=0, transcendentals=0),
    )(*args, *after, *gated)


def flips(size, bit):
    return [(i, i ^ bit) for i in range(size)]


def total_of(*refs):
    out = f32(refs[0])
    for r in refs[1:]:
        out = out + f32(r)
    return bf(out)


def split_core_kernel(me, keep, *refs, first, count):
    got, (near, far) = refs[:count], refs[count:]
    for half, out in enumerate((near, far)):
        for j in range(2):
            x, y = (half, j) if first == 0 else (j, half)
            came = got[0][x, y] if count == 1 else got[x][y]
            out[j] = total_of(keep[x, y], came)


def split_kernel(me, keep, got, near, far):
    for half, out in enumerate((near, far)):
        out[...] = total_of(keep[half], got[half])


def sum_kernel(me, keep, got, out):
    out[...] = total_of(keep[...], got[...])


def merge_kernel(me, *refs, place, count):
    others, keep, got = list(refs[: count - 1]), refs[count - 1], refs[count]
    outs, whole = refs[count + 1 : -1], refs[-1]
    at = 0
    for k in range(count):
        if k == place:
            rows = keep.shape[0]
            whole[at : at + rows, :] = total_of(keep[...], got[...])
        else:
            ref = others.pop(0)
            rows = ref.shape[0]
            whole[at : at + rows, :] = ref[...]
        at += rows
    if len(outs) == 1:
        outs[0][...] = whole[...]
    else:
        size = whole.shape[0] // 4
        for rel in range(4):
            outs[rel][...] = whole[pl.ds(pl.multiple_of(((me[3] >> 2) ^ rel) * size, 16), size), :]


def quarter_sum_kernel(me, a, b, c, d, out):
    out[...] = total_of(a[...], b[...], c[...], d[...])


def gather_kernel(me, a, b, c, d, out):
    size = a.shape[0]
    for rel, ref in enumerate((a, b, c, d)):
        out[pl.ds(pl.multiple_of(((me[3] >> 2) ^ rel) * size, 16), size), :] = ref[...]


def ends_kernel(me, total, got, out):
    place = me[3] >> 2
    at_end = (place == 0) | (place == 3)

    @pl.when(at_end)
    def _():
        out[...] = got[...]

    @pl.when(jnp.logical_not(at_end))
    def _():
        out[...] = total[...]


def pass_gate(kernel, name, outs, args, after, gated, scratch=()):
    ahead = [v for c in gated for v in c.far]
    got = call(kernel, name, outs, args, scratch, after, 24, 1.5, ahead)
    rest = got[len(outs) :]
    for c in gated:
        c.far, rest = rest[: len(c.far)], rest[len(c.far) :]
        c.launch()
    return got[: len(outs)]


class Chain:
    def __init__(self, name, me, near=None, far=None):
        self.name, self.route, self.me = name, ROUTES[name], me
        self.near, self.far = near, far
        self.at = 0

    def launch(self):
        grp, rows = lax.axis_size("grp"), lax.axis_size("rows")
        step = self.route[self.at]
        line = [[z * 4 + i for i in range(4)] for z in range(rows // 4)]
        if step == "C":
            self.got = [lax.ppermute(v, "rows", flips(rows, 1)) for v in self.far]
        elif step in "Xx":
            self.got = lax.ppermute(self.far, "grp", flips(grp, grp // 2))
        elif step in "Yy":
            self.got = lax.ppermute(self.far, "rows", flips(rows, 2))
        elif step == "R":
            self.got = [lax.ppermute(self.parts[k], "rows", flips(rows, 4 * k)) for k in (1, 2, 3)]
        elif step == "G":
            self.got = [lax.ppermute(self.parts[0], "rows", flips(rows, 4 * k)) for k in (1, 2, 3)]
        elif step in "PQ":
            self.got = lax.ppermute(self.total, "rows", flips(rows, 4 if step == "P" else 8))
        elif step == "1":
            pairs = list(zip(line[0] + line[3], line[1] + line[2]))
            self.got = lax.ppermute(self.total, "rows", pairs)
        elif step == "2":
            pairs = list(zip(line[1] + line[2], line[2] + line[1]))
            self.got = lax.ppermute(self.total, "rows", pairs)
        elif step == "3":
            pairs = list(zip(line[1] + line[2], line[0] + line[3]))
            self.got = lax.ppermute(self.total, "rows", pairs)
        elif step == "W":
            beside = lax.ppermute(self.total, "rows", flips(rows, 2))
            core = flips(rows, 1)
            self.got = [beside, lax.ppermute(self.total, "rows", core), lax.ppermute(beside, "rows", core)]

    def advance(self, after, gated, chains):
        step, then = self.route[self.at], self.route[self.at + 1 : self.at + 2]
        b16 = jnp.bfloat16

        def run(kernel, outs, args, scratch=()):
            return pass_gate(kernel, self.name + step, [(shape, b16) for shape in outs], [self.me, *args], after, gated, scratch)

        self.at += 1
        if step == "C":
            kernel = functools.partial(split_core_kernel, first=0 if then == "X" else 1, count=len(self.got))
            n = self.near.shape[2]
            self.near, self.far = run(kernel, [(2, n, 128)] * 2, [self.near, *self.got])
            token = self.near
        elif step in "XY":
            n = self.near.shape[1]
            self.near, self.far = run(split_kernel, [(n, 128)] * 2, [self.near, self.got])
            token = self.near
        elif step in "xy":
            group = next((g for g in GROUPS if self.name in GROUPS[g]), self.name)
            names = GROUPS.get(group, self.name)
            others = [chains[c].total for c in names if c != self.name and c in chains and hasattr(chains[c], "total")]
            n = self.near.shape[0]
            if len(others) < len(names) - 1:
                (self.total,) = run(sum_kernel, [(n, 128)], [self.near, self.got])
                return self.total
            n += sum(t.shape[0] for t in others)
            kernel = functools.partial(merge_kernel, place=names.index(self.name), count=len(names))
            shapes = [(n // 4, 128)] * 4 if (then if group == self.name else ROUTES[group][0]) == "R" else [(n, 128)]
            outs = run(kernel, shapes, [*others, self.near, self.got], [((n, 128), b16)])
            if group != self.name:
                chains[group] = Chain(group, self.me)
            chains[group].parts = outs
            chains[group].total = outs[0]
            chains[group].launch()
            return outs[0]
        elif step in "12PQ":
            (self.total,) = run(sum_kernel, [self.total.shape], [self.total, self.got])
            token = self.total
        elif step == "3":
            (self.total,) = run(ends_kernel, [self.total.shape], [self.total, self.got])
            token = self.total
        elif step == "R":
            self.parts = run(quarter_sum_kernel, [self.parts[0].shape], [self.parts[0], *self.got])
            token = self.parts[0]
        elif step == "G":
            n = self.parts[0].shape[0] * 4
            (self.total,) = run(gather_kernel, [(n, 128)], [self.parts[0], *self.got])
            token = self.total
        self.launch()
        return token

    def result(self):
        return [self.total, *self.got]


def finish_grp(values, dims):
    grp = lax.axis_size("grp")
    me = lax.axis_index("grp")
    bit = grp // 4
    while bit:
        mine = (me // bit) % 2
        out = []
        for v, dim in zip(values, dims):
            half = v.shape[dim] // 2
            near = lax.dynamic_slice_in_dim(v, mine * half, half, dim)
            far = lax.dynamic_slice_in_dim(v, (1 - mine) * half, half, dim)
            out.append(near + f32(lax.ppermute(bf(far), "grp", flips(grp, bit))))
        values = out
        bit //= 2
    return values


def on_device(
    pixels,
    cotangent,
    embed_single,
    embed_pair,
    spatial_gain,
    spatial_heads,
    spatial_output,
    spatial_scale,
    spatial_upward,
    spatial_down,
    temporal_gain,
    temporal_heads,
    temporal_output,
    temporal_scale,
    temporal_upward,
    temporal_down,
    unpatch_single,
    unpatch_pair,
):
    groups, frames = pixels.shape[:2]
    rows = lax.axis_size("rows")
    assert groups * 8 == rows == GRID and frames == 12 and pixels.shape[3] == STRIDE
    grp = lax.axis_size("grp")
    at = lax.axis_index("rows")
    core, along_y = at & 1, (at >> 1) & 1
    me = jnp.stack(
        [
            lax.axis_index("grp") // (grp // 2),
            core * 2 + along_y,
            jnp.where(at >= 8, 1, 0),
            at,
        ]
    ).astype(jnp.int32)
    picks = jnp.asarray(column_picks())
    wins = jnp.asarray(np.stack([window_picks(0, 640), window_picks(300, 640)]))
    places = frame_rows()
    sums = jnp.asarray(places.T)
    places = jnp.asarray(places)
    gains = f32(jnp.stack([spatial_gain, spatial_scale, temporal_gain, temporal_scale]))

    sent, last, first = call(
        slots_kernel,
        "slots",
        [((16, 2, CHAN, STRIDE, 128), jnp.bfloat16), ((72, 128), jnp.bfloat16), ((72, 128), jnp.bfloat16)],
        [me, pixels, cotangent.reshape(576, 128)],
        [((576, 128), jnp.float32)],
        vmem=60,
    )
    got = lax.all_to_all(sent, "rows", 0, 0)
    images = jnp.transpose(got, (1, 2, 0, 3, 4)).reshape(2 * CHAN * 128, 128)

    up = [(i, i + 1) for i in range(rows - 1)]
    down = [(i + 1, i) for i in range(rows - 1)]
    above = lax.ppermute(last, "rows", up)
    below = lax.ppermute(first, "rows", down)
    edges = f32(jnp.concatenate([above, below], 0))

    b16, w32 = jnp.bfloat16, jnp.float32
    half = 256
    made, chains = {}, {}
    token = []

    def start(name, keep, send):
        chains[name] = Chain(name, me, keep, send)
        if name not in "".join(GATES.values()):
            chains[name].launch()

    def pieces(count):
        return [((2, 2, count, 128), b16)] + [((2, count, 128), b16)] * 2

    def shared(v):
        core = flips(rows, 1)
        across = lax.ppermute(v, "grp", flips(grp, grp // 2))
        return [v, lax.ppermute(v, "rows", core), across, lax.ppermute(across, "rows", core)]

    def feed_grads(name, label, shares, up_weight, down_weight):
        near, far = call(
            feed_grad_kernel,
            label,
            [((2048, 128), b16)] * 2,
            [me, *shares, up_weight, down_weight],
            [((1024, 512), b16)] * 4,
            after=token,
            vmem=26,
            micros=7,
        )
        start(name, near, far)
        return near

    def cut():
        out = call(
            cotangent_kernel,
            "cotangent_windows",
            [((128, 1024), b16), ((256, 512), w32)],
            [me, cotangent.reshape(576, 128), edges, unpatch_single.T, unpatch_pair.T, picks, wins, places],
            [((384, 512), b16), ((640, 512), b16), ((576, 128), w32)],
            after=token,
            micros=5,
        )
        made["cut"] = out
        return out[0]

    def spatial():
        out = call(
            spatial_forward_kernel,
            "spatial_forward",
            [
                ((256, 640), b16),
                ((256, 512), w32),
                ((256, 1536), b16),
                ((8, 256, 256), b16),
                ((256, 512), b16),
                ((256, 512), w32),
                ((256, 512), b16),
                ((256, 2048), b16),
                ((256, 512), b16),
            ],
            [me, images, embed_single, embed_pair, gains, spatial_heads, spatial_output, spatial_upward, spatial_down, picks, wins],
            [((640, 512), b16)],
            after=token + [edges],
            vmem=60,
            enter=(10, 2, 3, 5, 6, 7, 8),
            post=(0, 1, 2, 3, 4, 5, 7),
            micros=13,
        )
        made["spatial"] = out
        made["middle"] = lax.all_to_all(out[8].reshape(16, 16, 512), "rows", 0, 0).reshape(256, 512)
        made["seconds"] = shared(out[6])
        return out[6]

    def temporal():
        both, grad_middle, *rest = call(
            temporal_kernel,
            "temporal",
            [
                ((2, 256, 512), b16),
                ((256, 512), b16),
                ((256, 512), b16),
                ((256, 512), b16),
                ((256, 1536), b16),
                ((256, 512), b16),
                ((256, 512), b16),
                ((16, 512), w32),
            ],
            [me, made["middle"], made["cut"][1], gains, temporal_heads, temporal_output, temporal_upward, temporal_down],
            [((256, 2048), b16), ((8, 256, 256), b16)],
            after=token + made["seconds"][1:],
            vmem=60,
            enter=(4, 5, 6, 7, 2),
            post=(2, 3, 4, 5, 6),
            micros=13,
        )
        made["temporal"] = rest
        made["grad_middle"] = lax.all_to_all(grad_middle.reshape(16, 16, 512), "rows", 0, 0).reshape(256, 512)
        made["temporal shares"] = shared(both)
        return rest[5]

    def temporal_grads():
        mixed, final, grad_projected, lowered, normed, gain_grads = made["temporal"]
        keep, *send = call(
            temporal_grad_kernel,
            "temporal_grads",
            pieces(TIME_ROWS),
            [me, normed, grad_projected, mixed, lowered, gain_grads, final, made["cut"][0]],
            [((1024, 512), w32)],
            after=token,
            vmem=60,
            micros=4,
        )
        start("b", keep, send)
        return keep

    def temporal_feed():
        return feed_grads("a", "temporal_feed", made["temporal shares"], temporal_upward, temporal_down)

    def back():
        windows, first, projected, chance, mixed, resid, _, slope, _ = made["spatial"]
        made["grads in"] = shared(made["grad_middle"])
        keep, *send, grad_start = call(
            spatial_back_kernel,
            "spatial_back",
            pieces(SPACE_ROWS) + [((256, 512), b16)],
            [
                me, made["grad_middle"], gains, resid, slope, first, projected, chance, mixed, windows, spatial_upward,
                spatial_down, spatial_heads, spatial_output,
            ],
            [((640, 512), w32)],
            after=token,
            enter=(11, 4, 10, 13, 6, 7, 5, 12, 8, 9),
            micros=12,
        )
        made["grad_start"] = grad_start
        start("d", keep, send)
        return grad_start

    def spatial_feed():
        return feed_grads("c", "spatial_feed", made["seconds"] + made["grads in"], spatial_upward, spatial_down)

    def fold_pixels():
        (frames_out,) = call(
            pixel_fold_kernel,
            "pixel_fold",
            [((768, 128), b16)],
            [me, made["grad_start"], embed_single, embed_pair, picks, wins],
            [((640, 512), b16)],
            after=token,
            vmem=48,
            micros=7,
        )
        sent = jnp.transpose(frames_out.reshape(2, CHAN, GRID, STRIDE, 128), (2, 0, 1, 3, 4))
        made["pixels"] = lax.all_to_all(sent, "rows", 0, 0)
        return frames_out

    def fold_rebuilt():
        whole, rims = call(
            rebuilt_kernel,
            "rebuilt_fold",
            [((576, 128), w32), ((64, 384), b16)],
            [me, made["temporal"][1], unpatch_single.T, unpatch_pair.T, picks, wins, sums],
            [((384, 512), b16), ((640, 512), b16)],
            after=token,
            micros=5,
        )
        top = rims[0:24].reshape(2, 12, CHAN, 1, 128)
        bottom = rims[32:56].reshape(2, 12, CHAN, 1, 128)
        made["rebuilt"] = whole, lax.ppermute(bottom, "rows", up), lax.ppermute(top, "rows", down)
        return rims

    def unpack(name):
        feed = 0 if name in "act" else None
        rest = {"b": (0, 96, 160), "d": (0, 80, 160), "t": (2048, 96, 160)}.get(name)
        outs, scratch, leave = [], [], []
        if feed is not None:
            outs += [((half, 2048), w32), ((2048, half), w32)]
            scratch += outs
            leave += [0, 1]
        if rest is not None:
            leave += [len(outs) + k for k in (0, 1, 2, 4)]
            some = [((half, 1536), w32), ((half, 512), w32), ((16, 128), w32)]
            outs += some + [((300, half), w32), ((600, half), w32)]
            scratch += some + [((4 * rest[1], half), w32), ((4 * rest[2], half), w32)]
        kernel = functools.partial(unpack_kernel, feed=feed, rest=rest)
        made[name] = call(kernel, "unpack_" + name, outs, [me, *chains[name].result()], scratch, token, 48, 3, (), leave)
        return chains[name].result()[1]

    work = {
        "cut": cut, "A": spatial, "T1": temporal, "T3": temporal_feed, "TG": temporal_grads, "C1": back, "C3": spatial_feed,
        "F": fold_rebuilt, "P": fold_pixels,
    }
    for step in ORDER:
        if step in work:
            out = work[step]()
        elif step[1] == "U":
            out = unpack(step[0])
        else:
            gated = [chains[c] for c in GATES.get(step, "")]
            ready = {"G": lambda: made["grad_middle"], "x": lambda: made["grads in"][2], "t": lambda: made["temporal shares"][2],
                     "r": lambda: made["rebuilt"][1], "s": lambda: made["rebuilt"][2]}
            extra = [ready[c]() if c in ready else chains[c].got for c in AFTER.get(step, "")]
            if step[0] == "g":
                out = pass_gate(gate_kernel, "gate", [((8, 128), w32)], [me], token + extra, gated)[0]
            else:
                out = chains[step[0]].advance(token + extra, gated, chains)
        token[:] = [out]

    got = f32(made["pixels"])
    singles = got[:8, 0].reshape(2, 4, CHAN, STRIDE, 128)
    pairs = got[8:].reshape(2, 8, CHAN, STRIDE, 128)
    pixel_gradient = jnp.concatenate([singles[:, :1], pairs, singles[:, 1:]], 1)

    whole, from_above, from_below = made["rebuilt"]
    gap = jnp.zeros((2, 12, CHAN, STRIDE - 2, 128), w32)
    rebuilt = whole.reshape(2, 12, CHAN, STRIDE, 128) + jnp.concatenate([f32(from_above), gap, f32(from_below)], 3)

    t_up, t_down, t_heads, t_output, t_gains, un_single, un_pair = made.get("t") or made["a"] + made["b"]
    s_up, s_down = made["c"]
    s_heads, s_output, s_gains, em_single, em_pair = made["d"]
    grads = [
        em_single,
        em_pair,
        s_gains[0:2].reshape(256),
        s_heads,
        s_output,
        s_gains[2:4].reshape(256),
        s_up,
        s_down,
        t_gains[0:2].reshape(256),
        t_heads,
        t_output,
        t_gains[2:4].reshape(256),
        t_up,
        t_down,
        un_single.T,
        un_pair.T,
    ]
    dims = [1, 1, 0, 0, 0, 0, 0, 1, 0, 0, 0, 0, 0, 1, 0, 0]
    return (rebuilt, pixel_gradient, *finish_grp(grads, dims))


def solution(mesh):
    in_specs = (
        P("grp", None, None, "rows", None),
        P("grp", None, None, "rows", None),
    ) + (P(),) * 16
    out_specs = (
        P("grp", None, None, "rows", None),
        P("grp", None, None, "rows", None),
        P(None, "grp"),
        P(None, "grp"),
        P("grp"),
        P("grp", None),
        P("grp", None),
        P("grp"),
        P("grp", None),
        P(None, "grp"),
        P("grp"),
        P("grp", None),
        P("grp", None),
        P("grp"),
        P("grp", None),
        P(None, "grp"),
        P("grp", None),
        P("grp", None),
    )
    return jax.shard_map(
        on_device, mesh=mesh, in_specs=in_specs, out_specs=out_specs, check_vma=False
    )
```

```python
import functools

import jax
import jax.numpy as jnp
import numpy as np
from jax import lax
from jax.experimental import pallas as pl
from jax.experimental.pallas import tpu as pltpu
from jax.sharding import PartitionSpec as P

HEADS = 8
STRIDE = 8
KERN = 10
GRID = 16
VSTEPS = 5
CHAN = 3
LANES = 128

epsilon = 1e-05
gelu_coef = 0.7978845608028654
cubic_coef = 0.044715
masked_score = -1000000000.0

WIN = CHAN * KERN * KERN
CUTS = KERN * CHAN * STRIDE
SINGLE_FRAMES = (0, 9, 10, 11)
MIB = 1 << 20
MICRO = 1_000_000_000


def column_picks():
    n = np.arange(256)
    chan, bit = (n % 24) // 8, n % 8
    at = np.arange(CHAN * 128)
    return ((n < CUTS) & (at[:, None] // 128 == chan) & (at[:, None] % 8 == bit)).astype(jnp.bfloat16)


def window_picks(first, width):
    n = np.arange(256)
    row, chan, bit = n // 24, (n % 24) // 8, n % 8
    w = np.arange(width) - first
    hit = (w >= 0) & (w < WIN)
    same = hit & (n < CUTS)[:, None] & (chan[:, None] == w // 100) & (row[:, None] == (w % 100) // 10)
    step = w % 10
    own = same & (step == bit[:, None] + 1)
    before = same & (step == 0) & (bit[:, None] == 7)
    after = same & (step == 9) & (bit[:, None] == 0)
    return np.concatenate([own, before, after], 0).astype(jnp.bfloat16)


def frame_rows():
    order = (SINGLE_FRAMES, (1, 3, 5, 7), (2, 4, 6, 8))
    out = np.zeros((384, 32), np.float32)
    for k in range(3):
        for g in range(2):
            for i in range(4):
                at = ((k * 2 + g) * 4 + i) * 16
                out[at : at + 16, g * 12 + order[k][i]] = 1
    return out.astype(jnp.bfloat16)


ROUTES = {"a": "y123W", "b": "CXy123W", "c": "y123W", "d": "CXy123W"}
AFTER = {}
GATES = {"g0": "b", "g1": "d"}
GROUPS = {}
ORDER = (
    "A", "cut", "T1", "TG", "g0", "bC", "F", "C1", "g1", "bX", "dC", "T3", "ay", "C3", "by", "a1", "cy", "dX", "b1",
    "a2", "c1", "dy", "b2", "a3", "c2", "P", "d1", "b3", "aU", "c3", "d2", "bU", "d3", "cU", "dU",
)


def dot(a, b):
    return jnp.dot(a, b, preferred_element_type=jnp.float32)


def dot_nt(a, b):
    return lax.dot_general(a, b, (((1,), (1,)), ((), ())), preferred_element_type=jnp.float32)


def dot_tn(a, b):
    return lax.dot_general(a, b, (((0,), (0,)), ((), ())), preferred_element_type=jnp.float32)


def bf(x):
    return x.astype(jnp.bfloat16)


def f32(x):
    return x.astype(jnp.float32)


def iota(shape, dim):
    return lax.broadcasted_iota(jnp.int32, shape, dim)


def own_columns(rows):
    return ((iota((rows, 384), 1) & 127) >> 3) == (iota((rows, 384), 0) & 15)


def picks_of(picks, i):
    lane = iota((1, 256), 1)
    return picks * bf(jnp.where((lane >= 24 * i) & (lane < 24 * i + 24), 1.0, 0.0))


def shift_up(v):
    return jnp.where((iota(v.shape, 0) & 15) == 15, 0.0, pltpu.roll(v, v.shape[0] - 1, 0))


def shift_down(v):
    return jnp.where((iota(v.shape, 0) & 15) == 0, 0.0, pltpu.roll(v, 1, 0))


def widen(v):
    return bf(jnp.concatenate([v, shift_down(v), shift_up(v)], 1))


def narrow(t):
    return bf(t[:, :256] + shift_up(t[:, 256:512]) + shift_down(t[:, 512:]))


def normalize(x, gain):
    centered = x - jnp.mean(x, -1, keepdims=True)
    inverse = lax.rsqrt(jnp.mean(centered * centered, -1, keepdims=True) + epsilon)
    unit = centered * inverse
    return bf(unit * gain), unit, inverse


def normalize_back(incoming, unit, inverse, gain):
    scaled = incoming * gain
    gain_grad = jnp.sum(incoming * unit, 0, keepdims=True)
    first = jnp.mean(scaled, -1, keepdims=True)
    second = jnp.mean(scaled * unit, -1, keepdims=True)
    return inverse * (scaled - first - unit * second), gain_grad


def halves_mask(width=128):
    lane = iota((1, width), 1)
    return lane < 64


def attention(projected, seen, chance_ref, scale):
    low = halves_mask()
    keep = (bf(jnp.where(low, 1.0, 0.0)), bf(jnp.where(low, 0.0, 1.0)))
    outs = []
    for pair in range(HEADS // 2):
        q = projected[:, pair * 128 : pair * 128 + 128]
        k = projected[:, 512 + pair * 128 : 512 + pair * 128 + 128]
        v = projected[:, 1024 + pair * 128 : 1024 + pair * 128 + 128]
        both = []
        for half in range(2):
            scores = dot_nt(q * keep[half], k) * scale
            if seen is not None:
                scores = jnp.where(seen, scores, masked_score)
            powers = jnp.exp(scores - jnp.max(scores, -1, keepdims=True))
            chance = bf(powers * (1.0 / jnp.sum(powers, -1, keepdims=True)))
            chance_ref[2 * pair + half] = chance
            both.append(dot(chance, v))
        outs.append(jnp.where(low, both[0], both[1]))
    return bf(jnp.concatenate(outs, 1))


def attention_back(grad_mixed, projected, chance_ref, scale):
    low = halves_mask()
    keep = (bf(jnp.where(low, 1.0, 0.0)), bf(jnp.where(low, 0.0, 1.0)))
    grads = ([], [], [])
    for pair in range(HEADS // 2):
        q = projected[:, pair * 128 : pair * 128 + 128]
        k = projected[:, 512 + pair * 128 : 512 + pair * 128 + 128]
        v = projected[:, 1024 + pair * 128 : 1024 + pair * 128 + 128]
        g = grad_mixed[:, pair * 128 : pair * 128 + 128]
        both = ([], [], [])
        for half in range(2):
            chance = chance_ref[2 * pair + half]
            wide = f32(chance)
            grad_chance = dot_nt(g * keep[half], v)
            inner = jnp.sum(wide * grad_chance, -1, keepdims=True)
            grad_scores = bf(wide * (grad_chance - inner))
            both[0].append(dot(grad_scores, k))
            both[1].append(dot_tn(grad_scores, q))
            both[2].append(dot_tn(chance, g))
        for part, factor in zip(range(3), (scale, scale, 1.0)):
            grads[part].append(bf(jnp.where(low, both[part][0], both[part][1]) * factor))
    return jnp.concatenate(grads[0] + grads[1] + grads[2], 1)


def gelu_parts(inner):
    square = inner * inner
    bent = jnp.tanh(gelu_coef * inner * (1.0 + cubic_coef * square))
    half = 0.5 * (1.0 + bent)
    slope = half + 0.5 * inner * (1.0 - bent * bent) * gelu_coef * (1.0 + 3.0 * cubic_coef * square)
    return bf(inner * half), slope


def feed_forward(second, up_ref, down_ref, slope_ref):
    total = None
    for k in range(4):
        columns = slice(k * 512, k * 512 + 512)
        active, slope = gelu_parts(dot(second, up_ref[:, columns]))
        slope_ref[:, columns] = bf(slope)
        part = dot(active, down_ref[columns, :])
        total = part if total is None else total + part
    return total


def feed_forward_back(lowered, up_ref, down_ref, slope_ref):
    total = None
    for k in range(4):
        columns = slice(k * 512, k * 512 + 512)
        grad_inner = bf(dot_nt(lowered, down_ref[columns, :]) * f32(slope_ref[:, columns]))
        part = dot_nt(grad_inner, up_ref[:, columns])
        total = part if total is None else total + part
    return total


def feed_grad_kernel(me, *refs):
    *shares, up, down, near, far, second, incoming, active, grad_inner = refs
    for k in range(4):
        rows = slice(k * 256, k * 256 + 256)
        if len(shares) == 4:
            second[rows, :] = shares[k][0]
            incoming[rows, :] = shares[k][1]
        else:
            second[rows, :] = shares[k][...]
            incoming[rows, :] = shares[4 + k][...]
    half = pl.ds(pl.multiple_of(me[0] * 256, 256), 256)
    up_ref, down_ref = held(up), held(down)
    for rel, out in enumerate((near, far)):
        at = pl.multiple_of((me[1] ^ rel) * 512, 512)
        up_part, down_part = up_ref[:, pl.ds(at, 512)], down_ref[pl.ds(at, 512), :]
        for k in range(4):
            rows = slice(k * 256, k * 256 + 256)
            act, slope = gelu_parts(dot(second[rows, :], up_part))
            active[rows, :] = act
            grad_inner[rows, :] = bf(dot_nt(incoming[rows, :], down_part) * slope)
        up_grad = dot_tn(second[:, half], grad_inner[...])
        for j in range(4):
            out[j * 256 : j * 256 + 256, :] = bf(up_grad[:, j * 128 : j * 128 + 128])
        down_grad = dot_tn(active[...], incoming[:, half])
        for j in range(2):
            out[1024 + j * 512 : 1536 + j * 512, :] = bf(down_grad[:, j * 128 : j * 128 + 128])


def swap_halves(v, bit):
    half = v.shape[1] // 2
    return jnp.where(bit == 1, jnp.concatenate([v[:, half:], v[:, :half]], 1), v)


def swap_quarters(v, quarter):
    v = swap_halves(v, quarter >> 1)
    half = v.shape[1] // 2
    return jnp.concatenate([swap_halves(v[:, :half], quarter & 1), swap_halves(v[:, half:], quarter & 1)], 1)


def put(outs, rel, x_rel, first, last, value):
    if rel < 2:
        outs[0][x_rel, rel, first:last, :] = value
    elif len(outs) == 2:
        outs[1][x_rel, rel & 1, first:last, :] = value
    else:
        outs[1 + x_rel][rel & 1, first:last, :] = value


def put_columns(outs, x_rel, at, value, count):
    rows, width = value.shape[0], value.shape[1] // 4
    for rel in range(4):
        for j in range(width // LANES):
            block = value[:, rel * width + j * LANES : rel * width + (j + 1) * LANES]
            put(outs, rel, x_rel, at + j * rows, at + (j + 1) * rows, bf(block))


def put_rows(outs, x_rel, at, source, row0, rows, quarter):
    size = rows // 4
    blocks = source.shape[1] // LANES
    for rel in range(4):
        first = pl.multiple_of(row0 + (quarter ^ rel) * size, 16)
        for j in range(blocks):
            put(outs, rel, x_rel, at + j * size, at + (j + 1) * size, bf(source[pl.ds(first, size), j * LANES : (j + 1) * LANES]))


def put_attention(outs, normed, grad_projected, mixed, lowered, first_grad, second_grad, mx, quarter):
    heads = dot_tn(swap_halves(normed, mx), swap_quarters(grad_projected, quarter))
    output = dot_tn(swap_halves(mixed, mx), swap_quarters(lowered, quarter))
    gains = (swap_halves(first_grad, mx), swap_halves(second_grad, mx))
    row = iota((16, 128), 0)
    for x_rel in range(2):
        put_columns(outs, x_rel, 0, heads[x_rel * 256 : x_rel * 256 + 256], 3)
        put_columns(outs, x_rel, 768, output[x_rel * 256 : x_rel * 256 + 256], 1)
        block = jnp.zeros((16, 128), jnp.float32)
        for j in range(4):
            at = x_rel * 256 + (j & 1) * 128
            block = jnp.where(row == j, gains[j >> 1][:, at : at + 128], block)
        for rel in range(4):
            put(outs, rel, x_rel, 1024, 1040, bf(block))


def fill_embed(embed, single_ref, pair_ref, is_pair):
    embed[...] = jnp.zeros_like(embed)

    @pl.when(is_pair == 1)
    def _():
        embed[0:600, :] = pair_ref[...]

    @pl.when(is_pair == 0)
    def _():
        embed[0:300, :] = single_ref[...]


def gate_kernel(me, out):
    out[...] = jnp.zeros_like(out)


def slots_kernel(me, pixels, cot_ref, out, last, first, cot):
    cot[...] = f32(cot_ref[...])
    last[...] = bf(cot[pl.ds(7, 72, stride=8), :])
    first[...] = bf(cot[pl.ds(0, 72, stride=8), :])
    for g in range(2):
        for k in range(4):
            single = pixels[g, SINGLE_FRAMES[k]]
            out[g * 4 + k, 0] = single
            out[g * 4 + k, 1] = single
            out[8 + g * 4 + k, 0] = pixels[g, 2 * k + 1]
            out[8 + g * 4 + k, 1] = pixels[g, 2 * k + 2]


def spatial_forward_kernel(
    me, frames, single, pair, gains, heads, output, up, down, picks_ref, wins,
    windows_out, start_out, projected_out, chance_out, mixed_out, resid_out, second_out, slope_out, middle_out,
    embed,
    post,
):
    is_pair = me[2]
    own = own_columns(256)
    picks = picks_ref[...]
    cuts = []
    for f in range(2):
        frame = jnp.concatenate([frames[(f * 3 + ch) * 128 : (f * 3 + ch) * 128 + 128, :] for ch in range(3)], 1)
        cut = None
        for i in range(KERN):
            lift = bf(jnp.where(iota((256, 128), 1) == 8 * (iota((256, 128), 0) >> 4) + i - 1, 1.0, 0.0))
            spread = bf(jnp.where(own, dot(lift, frame), 0.0))
            part = dot(spread, picks_of(picks, i))
            cut = part if cut is None else cut + part
        cuts.append(widen(cut))
    wins_ref = held(wins)
    windows = bf(dot(cuts[0], wins_ref[0]) + dot(cuts[1], wins_ref[1]))
    windows_out[...] = windows
    post(0)
    fill_embed(embed, held(single), held(pair), is_pair)
    start = dot(windows, embed[...])
    start_out[...] = start
    post(1)
    normed, _, _ = normalize(start, gains[0:1, :])
    projected = bf(dot(normed, held(heads)[...]))
    projected_out[...] = projected
    post(2)
    mixed = attention(projected, None, chance_out, 64**-0.5)
    mixed_out[...] = mixed
    post(3, 4)
    resid = start + dot(mixed, held(output)[...])
    resid_out[...] = resid
    post(5)
    second, _, _ = normalize(resid, gains[1:2, :])
    second_out[...] = second
    middle_out[...] = bf(resid + feed_forward(second, held(up), held(down), slope_out))


def spatial_back_kernel(
    me, incoming_ref, gains, resid_ref, slope, start_in, projected, chance, mixed, windows, up, down, heads, output,
    keep_out, send_near, send_far, start_out,
    grads,
):
    mx, quarter, is_pair = me[0], me[1], me[2]
    outs = (keep_out, send_near, send_far)
    incoming = incoming_ref[...]
    _, unit, inverse = normalize(resid_ref[...], gains[1:2, :])
    back = feed_forward_back(incoming, held(up), held(down), held(slope))
    grad, scale_grad = normalize_back(back, unit, inverse, gains[1:2, :])
    incoming = f32(incoming) + grad
    lowered = bf(incoming)
    grad_mixed = bf(dot_nt(lowered, held(output)[...]))
    grad_projected = attention_back(grad_mixed, held(projected)[...], held(chance), 64**-0.5)
    normed, unit, inverse = normalize(held(start_in)[...], gains[0:1, :])
    back, gain_grad = normalize_back(dot_nt(grad_projected, held(heads)[...]), unit, inverse, gains[0:1, :])
    grad_start = bf(incoming + back)
    start_out[...] = grad_start
    put_attention(outs, normed, grad_projected, held(mixed)[...], lowered, gain_grad, scale_grad, mx, quarter)
    grads[...] = dot_tn(held(windows)[...], swap_halves(grad_start, mx))
    pair_part = jnp.where(is_pair == 1, 1.0, 0.0)
    single_part = 1.0 - pair_part
    for x_rel in range(2):
        for rel in range(4):
            for j in range(2):
                at = x_rel * 256 + j * 128
                first = pl.multiple_of((quarter ^ rel) * 80, 16)
                put(outs, rel, x_rel, 1040 + j * 80, 1120 + j * 80, bf(grads[pl.ds(first, 80), at : at + 128] * single_part))
                first = pl.multiple_of((quarter ^ rel) * 160, 16)
                put(outs, rel, x_rel, 1200 + j * 160, 1360 + j * 160, bf(grads[pl.ds(first, 160), at : at + 128] * pair_part))
            put(outs, rel, x_rel, 1520, SPACE_ROWS, jnp.zeros((SPACE_ROWS - 1520, 128), jnp.bfloat16))


def pixel_fold_kernel(me, start_ref, single_ref, pair_ref, picks_ref, wins_ref, pixel_out, embed):
    fill_embed(embed, single_ref, pair_ref, me[2])
    window_grads = bf(dot_nt(start_ref[...], embed[...]))
    own = own_columns(256)
    picks = picks_ref[...]
    for f in range(2):
        folded = narrow(dot_nt(window_grads, wins_ref[f]))
        frame = None
        for i in range(KERN):
            spread = bf(jnp.where(own, dot_nt(folded, picks_of(picks, i)), 0.0))
            lift = bf(jnp.where(iota((128, 256), 0) == 8 * (iota((128, 256), 1) >> 4) + i - 1, 1.0, 0.0))
            part = dot(lift, spread)
            frame = part if frame is None else frame + part
        for ch in range(3):
            pixel_out[(f * 3 + ch) * 128 : (f * 3 + ch) * 128 + 128, :] = bf(frame[:, ch * 128 : ch * 128 + 128])


def slots_seen():
    def parts(dim):
        t = iota((256, 256), dim)
        index = (t >> 4) & 3
        slot = jnp.where(t < 128, jnp.where(index == 0, 0, index + 4), index + 1)
        return ((t >> 2) & 16) | (t & 15), slot

    here, query = parts(0)
    there, key = parts(1)
    near = (key <= query) & (((key < VSTEPS) & (query < VSTEPS)) | (key == query))
    return (here == there) & near


def cotangent_kernel(
    me, cot_ref, edges_ref, single_ref, pair_ref, picks_ref, wins_ref, rows_ref, cut_out, grad_out,
    unpatch_one, unpatch_two, cot,
):
    fill_unpatch(unpatch_one, unpatch_two, single_ref, pair_ref)
    own = own_columns(384)
    picks = picks_ref[...]
    cot[...] = f32(cot_ref[...])
    places = rows_ref[...]
    cut = None
    for i in range(KERN):
        parts = []
        for ch in range(3):
            if i == 0:
                parts.append(edges_ref[pl.ds(ch, 24, stride=3), :])
            elif i == KERN - 1:
                parts.append(edges_ref[pl.ds(72 + ch, 24, stride=3), :])
            else:
                parts.append(cot[pl.ds(ch * 8 + i - 1, 24, stride=24), :])
        row = jnp.concatenate([jnp.concatenate(parts, 1), jnp.zeros((8, 384), jnp.float32)], 0)
        spread = bf(jnp.where(own, dot(places, bf(row)), 0.0))
        part = dot(spread, picks_of(picks, i))
        cut = part if cut is None else cut + part
    wide = widen(cut)
    one = bf(dot(wide[:128], wins_ref[0, :, 0:384]))
    two = bf(dot(wide[128:256], wins_ref[0]) + dot(wide[256:], wins_ref[1]))
    cut_out[:, 0:384] = one
    cut_out[:, 384:1024] = two
    grad_out[...] = jnp.concatenate([dot(one, unpatch_one[...]), dot(two, unpatch_two[...])], 0)


def fill_unpatch(unpatch_one, unpatch_two, single_ref, pair_ref):
    unpatch_one[...] = jnp.zeros_like(unpatch_one)
    unpatch_two[...] = jnp.zeros_like(unpatch_two)
    unpatch_one[0:300, :] = single_ref[...]
    unpatch_two[0:600, :] = pair_ref[...]


def rebuilt_kernel(me, final_ref, single_ref, pair_ref, picks_ref, wins_ref, sums_ref, rebuilt_out, rims_out, unpatch_one, unpatch_two):
    fill_unpatch(unpatch_one, unpatch_two, single_ref, pair_ref)
    own = own_columns(384)
    picks = picks_ref[...]
    one = bf(dot_nt(final_ref[0:128, :], unpatch_one[...]))
    two = bf(dot_nt(final_ref[128:256, :], unpatch_two[...]))
    folded = jnp.concatenate(
        [
            narrow(dot_nt(one, wins_ref[0, :, 0:384])),
            narrow(dot_nt(two, wins_ref[0])),
            narrow(dot_nt(two, wins_ref[1])),
        ],
        0,
    )
    sums = sums_ref[...]
    for i in range(KERN):
        spread = bf(jnp.where(own, dot_nt(folded, picks_of(picks, i)), 0.0))
        row = dot(sums, spread)
        if i == 0:
            rims_out[0:32, :] = bf(row)
        elif i == KERN - 1:
            rims_out[32:64, :] = bf(row)
        else:
            for ch in range(3):
                rebuilt_out[pl.ds(ch * 8 + i - 1, 24, stride=24), :] = row[:24, ch * 128 : ch * 128 + 128]


def temporal_kernel(
    me, middle_ref, incoming_in, gains, heads, output, up, down,
    both_out, grad_out, mixed_out, final_out, projected_out, lowered_out, normed_out, gain_out,
    slope_ref, chance_ref,
    post,
):
    middle = f32(middle_ref[...])
    normed, first_unit, first_inverse = normalize(middle, gains[2:3, :])
    normed_out[...] = normed
    post(6)
    heads_ref = held(heads)
    projected = bf(dot(normed, heads_ref[...]))
    mixed = attention(projected, slots_seen(), chance_ref, 64**-0.5)
    mixed_out[...] = mixed
    post(2)
    output_ref = held(output)
    resid = middle + dot(mixed, output_ref[...])
    second, unit, inverse = normalize(resid, gains[3:4, :])
    incoming = held(incoming_in)[...]
    lowered = bf(incoming)
    both_out[0] = second
    both_out[1] = lowered
    up_ref, down_ref = held(up), held(down)
    final_out[...] = bf(resid + feed_forward(second, up_ref, down_ref, slope_ref))
    post(3)
    back = feed_forward_back(lowered, up_ref, down_ref, slope_ref)
    grad, scale_grad = normalize_back(back, unit, inverse, gains[3:4, :])
    incoming = incoming + grad
    lowered = bf(incoming)
    lowered_out[...] = lowered
    post(5)
    grad_mixed = bf(dot_nt(lowered, output_ref[...]))
    grad_projected = attention_back(grad_mixed, projected, chance_ref, 64**-0.5)
    projected_out[...] = grad_projected
    post(4)
    back, gain_grad = normalize_back(dot_nt(grad_projected, heads_ref[...]), first_unit, first_inverse, gains[2:3, :])
    gain_out[0:8, :] = jnp.broadcast_to(gain_grad, (8, 512))
    gain_out[8:16, :] = jnp.broadcast_to(scale_grad, (8, 512))
    grad_out[...] = bf(incoming + back)


def temporal_grad_kernel(
    me, normed_ref, projected_ref, mixed_ref, lowered_ref, gain_ref, final_ref, cut_ref,
    keep_out, send_near, send_far,
    grads,
):
    mx, quarter = me[0], me[1]
    outs = (keep_out, send_near, send_far)
    put_attention(
        outs, normed_ref[...], projected_ref[...], mixed_ref[...], lowered_ref[...], gain_ref[0:1, :], gain_ref[8:9, :],
        mx, quarter,
    )
    final = swap_halves(final_ref[...], mx)
    grads[0:384, :] = dot_tn(cut_ref[:, 0:384], final[:128])
    grads[384:1024, :] = dot_tn(cut_ref[:, 384:1024], final[128:])
    for x_rel in range(2):
        for rel in range(4):
            for j in range(2):
                at = x_rel * 256 + j * 128
                first = pl.multiple_of((quarter ^ rel) * 96, 16)
                put(outs, rel, x_rel, 1040 + j * 96, 1136 + j * 96, bf(grads[pl.ds(first, 96), at : at + 128]))
                first = pl.multiple_of(384 + (quarter ^ rel) * 160, 16)
                put(outs, rel, x_rel, 1232 + j * 160, 1392 + j * 160, bf(grads[pl.ds(first, 160), at : at + 128]))
            put(outs, rel, x_rel, 1552, TIME_ROWS, jnp.zeros((TIME_ROWS - 1552, 128), jnp.bfloat16))


TIME_ROWS = 1600
SPACE_ROWS = 1536


class Leaving:
    def __init__(self, semaphores):
        self.semaphores, self.copies = semaphores, []

    def send(self, source, out):
        copy = pltpu.make_async_copy(source, out, self.semaphores.at[len(self.copies)])
        copy.start()
        self.copies.append(copy)

    def wait(self):
        for copy in self.copies:
            copy.wait()


def unpack_feed(me, sources, first, up_out, down_out, up, down, leaving):
    for rel, source in enumerate(sources):
        at = pl.multiple_of((me[1] ^ rel) * 512, 512)
        for j in range(2):
            rows = slice(first + 1024 + j * 512, first + 1536 + j * 512)
            down[pl.ds(at, 512), j * 128 : j * 128 + 128] = f32(source[rows, :])
        leaving.send(down.at[pl.ds(at, 512), :], down_out.at[pl.ds(at, 512), :])
    for rel, source in enumerate(sources):
        at = pl.multiple_of((me[1] ^ rel) * 512, 512)
        for j in range(4):
            rows = slice(first + j * 256, first + j * 256 + 256)
            up[:, pl.ds(pl.multiple_of(at + j * 128, 128), 128)] = f32(source[rows, :])
        leaving.send(up.at[:, pl.ds(at, 512)], up_out.at[:, pl.ds(at, 512)])


def unpack_rest(
    me, sources, first, one, two, heads_out, output_out, gains_out, single_out, pair_out, heads, output, gains, single, pair,
    leaving,
):
    for rel, source in enumerate(sources):
        quarter = me[1] ^ rel
        for j in range(3):
            at = pl.multiple_of(quarter * 384 + j * 128, 128)
            heads[:, pl.ds(at, 128)] = f32(source[first + j * 256 : first + j * 256 + 256, :])
        at = pl.multiple_of(quarter * 384, 128)
        leaving.send(heads.at[:, pl.ds(at, 384)], heads_out.at[:, pl.ds(at, 384)])
    gains[...] = f32(sources[0][first + 1024 : first + 1040, :])
    leaving.send(gains, gains_out)
    for rel, source in enumerate(sources):
        quarter = me[1] ^ rel
        at = pl.multiple_of(quarter * 128, 128)
        output[:, pl.ds(at, 128)] = f32(source[first + 768 : first + 1024, :])
        for j in range(2):
            row = first + 1040 + j * one
            at = pl.multiple_of(quarter * one, 16)
            single[pl.ds(at, one), j * 128 : j * 128 + 128] = f32(source[row : row + one, :])
            row = first + 1040 + 2 * one + j * two
            at = pl.multiple_of(quarter * two, 16)
            pair[pl.ds(at, two), j * 128 : j * 128 + 128] = f32(source[row : row + two, :])
    leaving.send(output, output_out)
    single_out[...] = single[0:300, :]
    leaving.send(pair.at[0:600, :], pair_out)


def unpack_kernel(me, *refs, feed, rest):
    sources, refs = refs[:4], refs[4:]
    leaving = Leaving(refs[-1])
    many = 2 * (feed is not None) + 5 * (rest is not None)
    outs, scratch = list(refs[:many]), list(refs[many:-1])
    if feed is not None:
        unpack_feed(me, sources, feed, *outs[:2], *scratch[:2], leaving)
        outs, scratch = outs[2:], scratch[2:]
    if rest is not None:
        unpack_rest(me, sources, *rest, *outs, *scratch, leaving)
    leaving.wait()


class Arriving:
    def __init__(self, source, held, semaphore, line):
        self.held = held
        self.copy = pltpu.make_async_copy(source, held, semaphore)
        self.line = line
        line.append(self)
        self.started = False
        if len(line) <= 6:
            self.start()

    def start(self):
        if not self.started:
            self.started = True
            self.copy.start()

    def ready(self):
        if self.copy is not None:
            self.start()
            self.copy.wait()
            self.copy = None
            for other in self.line:
                if not other.started:
                    other.start()
                    break
        return self.held


def held(ref):
    return ref.ready() if isinstance(ref, Arriving) else ref


def call(
    kernel, name, outs, args, scratch=(), after=(), vmem=60, micros=1.0, gated=(), leave=(), enter=(), post=()
):
    any_space = pl.BlockSpec(memory_space=pl.ANY)
    whole = pl.BlockSpec(memory_space=pltpu.VMEM)
    count, made = len(args), len(outs)
    waits = len(after) + len(gated)
    held = [pltpu.VMEM(args[k].shape, args[k].dtype) for k in enter]
    kept = [pltpu.VMEM(*outs[k]) for k in post]
    own = [pltpu.VMEM(s, d) for s, d in scratch]
    if leave:
        own.append(pltpu.SemaphoreType.DMA((12,)))

    def body(*refs):
        ins = list(refs[:count])
        results = list(refs[count + waits : count + waits + made])
        rest = refs[count + waits + made + len(gated) :]
        mine, rest = rest[: len(own)], rest[len(own) :]
        copies = {}
        line = []
        for n, k in enumerate(enter):
            ins[k] = Arriving(ins[k], rest[n], rest[-2].at[n], line)
        if post:
            places = {}
            for n, k in enumerate(post):
                places[k] = (rest[len(enter) + n], results[k], n)
                results[k] = rest[len(enter) + n]

            def go(*which):
                for k in which:
                    source, out, n = places[k]
                    copies[k] = pltpu.make_async_copy(source, out, rest[-1].at[n])
                    copies[k].start()

            kernel(*ins, *results, *mine, post=go)
            go(*[k for k in post if k not in copies])
        else:
            kernel(*ins, *results, *mine)
        for k in enter:
            ins[k].ready()
        for copy in copies.values():
            copy.wait()

    return pl.pallas_call(
        body,
        name=name,
        out_shape=[jax.ShapeDtypeStruct(s, d) for s, d in outs] + [jax.ShapeDtypeStruct(a.shape, a.dtype) for a in gated],
        in_specs=[pl.BlockSpec(memory_space=pltpu.SMEM)]
        + [any_space if k in enter else whole for k in range(1, count)]
        + [any_space] * waits,
        out_specs=[any_space if k in leave or k in post else whole for k in range(made)] + [any_space] * len(gated),
        scratch_shapes=own
        + held
        + kept
        + [pltpu.SemaphoreType.DMA((max(len(enter), 1),)), pltpu.SemaphoreType.DMA((max(len(post), 1),))],
        input_output_aliases={count + len(after) + k: made + k for k in range(len(gated))},
        compiler_params=pltpu.CompilerParams(vmem_limit_bytes=vmem * MIB),
        cost_estimate=pl.CostEstimate(flops=int(micros * MICRO), bytes_accessed=0, transcendentals=0),
    )(*args, *after, *gated)


def flips(size, bit):
    return [(i, i ^ bit) for i in range(size)]


def total_of(*refs):
    out = f32(refs[0])
    for r in refs[1:]:
        out = out + f32(r)
    return bf(out)


def split_core_kernel(me, keep, *refs, first, count):
    got, (near, far) = refs[:count], refs[count:]
    for half, out in enumerate((near, far)):
        for j in range(2):
            x, y = (half, j) if first == 0 else (j, half)
            came = got[0][x, y] if count == 1 else got[x][y]
            out[j] = total_of(keep[x, y], came)


def split_kernel(me, keep, got, near, far):
    for half, out in enumerate((near, far)):
        out[...] = total_of(keep[half], got[half])


def sum_kernel(me, keep, got, out):
    out[...] = total_of(keep[...], got[...])


def merge_kernel(me, *refs, place, count):
    others, keep, got = list(refs[: count - 1]), refs[count - 1], refs[count]
    outs, whole = refs[count + 1 : -1], refs[-1]
    at = 0
    for k in range(count):
        if k == place:
            rows = keep.shape[0]
            whole[at : at + rows, :] = total_of(keep[...], got[...])
        else:
            ref = others.pop(0)
            rows = ref.shape[0]
            whole[at : at + rows, :] = ref[...]
        at += rows
    if len(outs) == 1:
        outs[0][...] = whole[...]
    else:
        size = whole.shape[0] // 4
        for rel in range(4):
            outs[rel][...] = whole[pl.ds(pl.multiple_of(((me[3] >> 2) ^ rel) * size, 16), size), :]


def quarter_sum_kernel(me, a, b, c, d, out):
    out[...] = total_of(a[...], b[...], c[...], d[...])


def gather_kernel(me, a, b, c, d, out):
    size = a.shape[0]
    for rel, ref in enumerate((a, b, c, d)):
        out[pl.ds(pl.multiple_of(((me[3] >> 2) ^ rel) * size, 16), size), :] = ref[...]


def ends_kernel(me, total, got, out):
    place = me[3] >> 2
    at_end = (place == 0) | (place == 3)

    @pl.when(at_end)
    def _():
        out[...] = got[...]

    @pl.when(jnp.logical_not(at_end))
    def _():
        out[...] = total[...]


def pass_gate(kernel, name, outs, args, after, gated, scratch=()):
    ahead = [v for c in gated for v in c.far]
    got = call(kernel, name, outs, args, scratch, after, 24, 1.5, ahead)
    rest = got[len(outs) :]
    for c in gated:
        c.far, rest = rest[: len(c.far)], rest[len(c.far) :]
        c.launch()
    return got[: len(outs)]


class Chain:
    def __init__(self, name, me, near=None, far=None):
        self.name, self.route, self.me = name, ROUTES[name], me
        self.near, self.far = near, far
        self.at = 0

    def launch(self):
        grp, rows = lax.axis_size("grp"), lax.axis_size("rows")
        step = self.route[self.at]
        line = [[z * 4 + i for i in range(4)] for z in range(rows // 4)]
        if step == "C":
            self.got = [lax.ppermute(v, "rows", flips(rows, 1)) for v in self.far]
        elif step in "Xx":
            self.got = lax.ppermute(self.far, "grp", flips(grp, grp // 2))
        elif step in "Yy":
            self.got = lax.ppermute(self.far, "rows", flips(rows, 2))
        elif step == "R":
            self.got = [lax.ppermute(self.parts[k], "rows", flips(rows, 4 * k)) for k in (1, 2, 3)]
        elif step == "G":
            self.got = [lax.ppermute(self.parts[0], "rows", flips(rows, 4 * k)) for k in (1, 2, 3)]
        elif step in "PQ":
            self.got = lax.ppermute(self.total, "rows", flips(rows, 4 if step == "P" else 8))
        elif step == "1":
            pairs = list(zip(line[0] + line[3], line[1] + line[2]))
            self.got = lax.ppermute(self.total, "rows", pairs)
        elif step == "2":
            pairs = list(zip(line[1] + line[2], line[2] + line[1]))
            self.got = lax.ppermute(self.total, "rows", pairs)
        elif step == "3":
            pairs = list(zip(line[1] + line[2], line[0] + line[3]))
            self.got = lax.ppermute(self.total, "rows", pairs)
        elif step == "W":
            beside = lax.ppermute(self.total, "rows", flips(rows, 2))
            core = flips(rows, 1)
            self.got = [beside, lax.ppermute(self.total, "rows", core), lax.ppermute(beside, "rows", core)]

    def advance(self, after, gated, chains):
        step, then = self.route[self.at], self.route[self.at + 1 : self.at + 2]
        b16 = jnp.bfloat16

        def run(kernel, outs, args, scratch=()):
            return pass_gate(kernel, self.name + step, [(shape, b16) for shape in outs], [self.me, *args], after, gated, scratch)

        self.at += 1
        if step == "C":
            kernel = functools.partial(split_core_kernel, first=0 if then == "X" else 1, count=len(self.got))
            n = self.near.shape[2]
            self.near, self.far = run(kernel, [(2, n, 128)] * 2, [self.near, *self.got])
            token = self.near
        elif step in "XY":
            n = self.near.shape[1]
            self.near, self.far = run(split_kernel, [(n, 128)] * 2, [self.near, self.got])
            token = self.near
        elif step in "xy":
            group = next((g for g in GROUPS if self.name in GROUPS[g]), self.name)
            names = GROUPS.get(group, self.name)
            others = [chains[c].total for c in names if c != self.name and c in chains and hasattr(chains[c], "total")]
            n = self.near.shape[0]
            if len(others) < len(names) - 1:
                (self.total,) = run(sum_kernel, [(n, 128)], [self.near, self.got])
                return self.total
            n += sum(t.shape[0] for t in others)
            kernel = functools.partial(merge_kernel, place=names.index(self.name), count=len(names))
            shapes = [(n // 4, 128)] * 4 if (then if group == self.name else ROUTES[group][0]) == "R" else [(n, 128)]
            outs = run(kernel, shapes, [*others, self.near, self.got], [((n, 128), b16)])
            if group != self.name:
                chains[group] = Chain(group, self.me)
            chains[group].parts = outs
            chains[group].total = outs[0]
            chains[group].launch()
            return outs[0]
        elif step in "12PQ":
            (self.total,) = run(sum_kernel, [self.total.shape], [self.total, self.got])
            token = self.total
        elif step == "3":
            (self.total,) = run(ends_kernel, [self.total.shape], [self.total, self.got])
            token = self.total
        elif step == "R":
            self.parts = run(quarter_sum_kernel, [self.parts[0].shape], [self.parts[0], *self.got])
            token = self.parts[0]
        elif step == "G":
            n = self.parts[0].shape[0] * 4
            (self.total,) = run(gather_kernel, [(n, 128)], [self.parts[0], *self.got])
            token = self.total
        self.launch()
        return token

    def result(self):
        return [self.total, *self.got]


def finish_grp(values, dims):
    grp = lax.axis_size("grp")
    me = lax.axis_index("grp")
    bit = grp // 4
    while bit:
        mine = (me // bit) % 2
        out = []
        for v, dim in zip(values, dims):
            half = v.shape[dim] // 2
            near = lax.dynamic_slice_in_dim(v, mine * half, half, dim)
            far = lax.dynamic_slice_in_dim(v, (1 - mine) * half, half, dim)
            out.append(near + f32(lax.ppermute(bf(far), "grp", flips(grp, bit))))
        values = out
        bit //= 2
    return values


def on_device(
    pixels,
    cotangent,
    embed_single,
    embed_pair,
    spatial_gain,
    spatial_heads,
    spatial_output,
    spatial_scale,
    spatial_upward,
    spatial_down,
    temporal_gain,
    temporal_heads,
    temporal_output,
    temporal_scale,
    temporal_upward,
    temporal_down,
    unpatch_single,
    unpatch_pair,
):
    groups, frames = pixels.shape[:2]
    rows = lax.axis_size("rows")
    assert groups * 8 == rows == GRID and frames == 12 and pixels.shape[3] == STRIDE
    grp = lax.axis_size("grp")
    at = lax.axis_index("rows")
    core, along_y = at & 1, (at >> 1) & 1
    me = jnp.stack(
        [
            lax.axis_index("grp") // (grp // 2),
            core * 2 + along_y,
            jnp.where(at >= 8, 1, 0),
            at,
        ]
    ).astype(jnp.int32)
    picks = jnp.asarray(column_picks())
    wins = jnp.asarray(np.stack([window_picks(0, 640), window_picks(300, 640)]))
    places = frame_rows()
    sums = jnp.asarray(places.T)
    places = jnp.asarray(places)
    gains = f32(jnp.stack([spatial_gain, spatial_scale, temporal_gain, temporal_scale]))

    sent, last, first = call(
        slots_kernel,
        "slots",
        [((16, 2, CHAN, STRIDE, 128), jnp.bfloat16), ((72, 128), jnp.bfloat16), ((72, 128), jnp.bfloat16)],
        [me, pixels, cotangent.reshape(576, 128)],
        [((576, 128), jnp.float32)],
        vmem=60,
    )
    got = lax.all_to_all(sent, "rows", 0, 0)
    images = jnp.transpose(got, (1, 2, 0, 3, 4)).reshape(2 * CHAN * 128, 128)

    up = [(i, i + 1) for i in range(rows - 1)]
    down = [(i + 1, i) for i in range(rows - 1)]
    above = lax.ppermute(last, "rows", up)
    below = lax.ppermute(first, "rows", down)
    edges = f32(jnp.concatenate([above, below], 0))

    b16, w32 = jnp.bfloat16, jnp.float32
    half = 256
    made, chains = {}, {}
    token = []

    def start(name, keep, send):
        chains[name] = Chain(name, me, keep, send)
        if name not in "".join(GATES.values()):
            chains[name].launch()

    def pieces(count):
        return [((2, 2, count, 128), b16)] + [((2, count, 128), b16)] * 2

    def shared(v):
        core = flips(rows, 1)
        across = lax.ppermute(v, "grp", flips(grp, grp // 2))
        return [v, lax.ppermute(v, "rows", core), across, lax.ppermute(across, "rows", core)]

    def feed_grads(name, label, shares, up_weight, down_weight):
        near, far = call(
            feed_grad_kernel,
            label,
            [((2048, 128), b16)] * 2,
            [me, *shares, up_weight, down_weight],
            [((1024, 512), b16)] * 4,
            after=token,
            vmem=26,
            micros=7,
        )
        start(name, near, far)
        return near

    def cut():
        out = call(
            cotangent_kernel,
            "cotangent_windows",
            [((128, 1024), b16), ((256, 512), w32)],
            [me, cotangent.reshape(576, 128), edges, unpatch_single.T, unpatch_pair.T, picks, wins, places],
            [((384, 512), b16), ((640, 512), b16), ((576, 128), w32)],
            after=token,
            micros=5,
        )
        made["cut"] = out
        return out[0]

    def spatial():
        out = call(
            spatial_forward_kernel,
            "spatial_forward",
            [
                ((256, 640), b16),
                ((256, 512), w32),
                ((256, 1536), b16),
                ((8, 256, 256), b16),
                ((256, 512), b16),
                ((256, 512), w32),
                ((256, 512), b16),
                ((256, 2048), b16),
                ((256, 512), b16),
            ],
            [me, images, embed_single, embed_pair, gains, spatial_heads, spatial_output, spatial_upward, spatial_down, picks, wins],
            [((640, 512), b16)],
            after=token + [edges],
            vmem=60,
            enter=(10, 2, 3, 5, 6, 7, 8),
            post=(0, 1, 2, 3, 4, 5, 7),
            micros=13,
        )
        made["spatial"] = out
        made["middle"] = lax.all_to_all(out[8].reshape(16, 16, 512), "rows", 0, 0).reshape(256, 512)
        made["seconds"] = shared(out[6])
        return out[6]

    def temporal():
        both, grad_middle, *rest = call(
            temporal_kernel,
            "temporal",
            [
                ((2, 256, 512), b16),
                ((256, 512), b16),
                ((256, 512), b16),
                ((256, 512), b16),
                ((256, 1536), b16),
                ((256, 512), b16),
                ((256, 512), b16),
                ((16, 512), w32),
            ],
            [me, made["middle"], made["cut"][1], gains, temporal_heads, temporal_output, temporal_upward, temporal_down],
            [((256, 2048), b16), ((8, 256, 256), b16)],
            after=token + made["seconds"][1:],
            vmem=60,
            enter=(4, 5, 6, 7, 2),
            post=(2, 3, 4, 5, 6),
            micros=13,
        )
        made["temporal"] = rest
        made["grad_middle"] = lax.all_to_all(grad_middle.reshape(16, 16, 512), "rows", 0, 0).reshape(256, 512)
        made["temporal shares"] = shared(both)
        return rest[5]

    def temporal_grads():
        mixed, final, grad_projected, lowered, normed, gain_grads = made["temporal"]
        keep, *send = call(
            temporal_grad_kernel,
            "temporal_grads",
            pieces(TIME_ROWS),
            [me, normed, grad_projected, mixed, lowered, gain_grads, final, made["cut"][0]],
            [((1024, 512), w32)],
            after=token,
            vmem=60,
            micros=4,
        )
        start("b", keep, send)
        return keep

    def temporal_feed():
        return feed_grads("a", "temporal_feed", made["temporal shares"], temporal_upward, temporal_down)

    def back():
        windows, first, projected, chance, mixed, resid, _, slope, _ = made["spatial"]
        made["grads in"] = shared(made["grad_middle"])
        keep, *send, grad_start = call(
            spatial_back_kernel,
            "spatial_back",
            pieces(SPACE_ROWS) + [((256, 512), b16)],
            [
                me, made["grad_middle"], gains, resid, slope, first, projected, chance, mixed, windows, spatial_upward,
                spatial_down, spatial_heads, spatial_output,
            ],
            [((640, 512), w32)],
            after=token,
            enter=(12, 5, 8, 9),
            micros=12,
        )
        made["grad_start"] = grad_start
        start("d", keep, send)
        return grad_start

    def spatial_feed():
        return feed_grads("c", "spatial_feed", made["seconds"] + made["grads in"], spatial_upward, spatial_down)

    def fold_pixels():
        (frames_out,) = call(
            pixel_fold_kernel,
            "pixel_fold",
            [((768, 128), b16)],
            [me, made["grad_start"], embed_single, embed_pair, picks, wins],
            [((640, 512), b16)],
            after=token,
            vmem=48,
            micros=7,
        )
        sent = jnp.transpose(frames_out.reshape(2, CHAN, GRID, STRIDE, 128), (2, 0, 1, 3, 4))
        made["pixels"] = lax.all_to_all(sent, "rows", 0, 0)
        return frames_out

    def fold_rebuilt():
        whole, rims = call(
            rebuilt_kernel,
            "rebuilt_fold",
            [((576, 128), w32), ((64, 384), b16)],
            [me, made["temporal"][1], unpatch_single.T, unpatch_pair.T, picks, wins, sums],
            [((384, 512), b16), ((640, 512), b16)],
            after=token,
            micros=5,
        )
        top = rims[0:24].reshape(2, 12, CHAN, 1, 128)
        bottom = rims[32:56].reshape(2, 12, CHAN, 1, 128)
        made["rebuilt"] = whole, lax.ppermute(bottom, "rows", up), lax.ppermute(top, "rows", down)
        return rims

    def unpack(name):
        feed = 0 if name in "act" else None
        rest = {"b": (0, 96, 160), "d": (0, 80, 160), "t": (2048, 96, 160)}.get(name)
        outs, scratch, leave = [], [], []
        if feed is not None:
            outs += [((half, 2048), w32), ((2048, half), w32)]
            scratch += outs
            leave += [0, 1]
        if rest is not None:
            leave += [len(outs) + k for k in (0, 1, 2, 4)]
            some = [((half, 1536), w32), ((half, 512), w32), ((16, 128), w32)]
            outs += some + [((300, half), w32), ((600, half), w32)]
            scratch += some + [((4 * rest[1], half), w32), ((4 * rest[2], half), w32)]
        kernel = functools.partial(unpack_kernel, feed=feed, rest=rest)
        made[name] = call(kernel, "unpack_" + name, outs, [me, *chains[name].result()], scratch, token, 48, 3, (), leave)
        return chains[name].result()[1]

    work = {
        "cut": cut, "A": spatial, "T1": temporal, "T3": temporal_feed, "TG": temporal_grads, "C1": back, "C3": spatial_feed,
        "F": fold_rebuilt, "P": fold_pixels,
    }
    for step in ORDER:
        if step in work:
            out = work[step]()
        elif step[1] == "U":
            out = unpack(step[0])
        else:
            gated = [chains[c] for c in GATES.get(step, "")]
            ready = {"G": lambda: made["grad_middle"], "x": lambda: made["grads in"][2], "t": lambda: made["temporal shares"][2],
                     "r": lambda: made["rebuilt"][1], "s": lambda: made["rebuilt"][2]}
            extra = [ready[c]() if c in ready else chains[c].got for c in AFTER.get(step, "")]
            if step[0] == "g":
                out = pass_gate(gate_kernel, "gate", [((8, 128), w32)], [me], token + extra, gated)[0]
            else:
                out = chains[step[0]].advance(token + extra, gated, chains)
        token[:] = [out]

    got = f32(made["pixels"])
    singles = got[:8, 0].reshape(2, 4, CHAN, STRIDE, 128)
    pairs = got[8:].reshape(2, 8, CHAN, STRIDE, 128)
    pixel_gradient = jnp.concatenate([singles[:, :1], pairs, singles[:, 1:]], 1)

    whole, from_above, from_below = made["rebuilt"]
    gap = jnp.zeros((2, 12, CHAN, STRIDE - 2, 128), w32)
    rebuilt = whole.reshape(2, 12, CHAN, STRIDE, 128) + jnp.concatenate([f32(from_above), gap, f32(from_below)], 3)

    t_up, t_down, t_heads, t_output, t_gains, un_single, un_pair = made.get("t") or made["a"] + made["b"]
    s_up, s_down = made["c"]
    s_heads, s_output, s_gains, em_single, em_pair = made["d"]
    grads = [
        em_single,
        em_pair,
        s_gains[0:2].reshape(256),
        s_heads,
        s_output,
        s_gains[2:4].reshape(256),
        s_up,
        s_down,
        t_gains[0:2].reshape(256),
        t_heads,
        t_output,
        t_gains[2:4].reshape(256),
        t_up,
        t_down,
        un_single.T,
        un_pair.T,
    ]
    dims = [1, 1, 0, 0, 0, 0, 0, 1, 0, 0, 0, 0, 0, 1, 0, 0]
    return (rebuilt, pixel_gradient, *finish_grp(grads, dims))


def solution(mesh):
    in_specs = (
        P("grp", None, None, "rows", None),
        P("grp", None, None, "rows", None),
    ) + (P(),) * 16
    out_specs = (
        P("grp", None, None, "rows", None),
        P("grp", None, None, "rows", None),
        P(None, "grp"),
        P(None, "grp"),
        P("grp"),
        P("grp", None),
        P("grp", None),
        P("grp"),
        P("grp", None),
        P(None, "grp"),
        P("grp"),
        P("grp", None),
        P("grp", None),
        P("grp"),
        P("grp", None),
        P(None, "grp"),
        P("grp", None),
        P("grp", None),
    )
    return jax.shard_map(
        on_device, mesh=mesh, in_specs=in_specs, out_specs=out_specs, check_vma=False
    )
```

```python
import functools

import jax
import jax.numpy as jnp
import numpy as np
from jax import lax
from jax.experimental import pallas as pl
from jax.experimental.pallas import tpu as pltpu
from jax.sharding import PartitionSpec as P

HEADS = 8
STRIDE = 8
KERN = 10
GRID = 16
VSTEPS = 5
CHAN = 3
LANES = 128

epsilon = 1e-05
gelu_coef = 0.7978845608028654
cubic_coef = 0.044715
masked_score = -1000000000.0

WIN = CHAN * KERN * KERN
CUTS = KERN * CHAN * STRIDE
SINGLE_FRAMES = (0, 9, 10, 11)
MIB = 1 << 20
MICRO = 1_000_000_000


def column_picks():
    n = np.arange(256)
    chan, bit = (n % 24) // 8, n % 8
    at = np.arange(CHAN * 128)
    return ((n < CUTS) & (at[:, None] // 128 == chan) & (at[:, None] % 8 == bit)).astype(jnp.bfloat16)


def window_picks(first, width):
    n = np.arange(256)
    row, chan, bit = n // 24, (n % 24) // 8, n % 8
    w = np.arange(width) - first
    hit = (w >= 0) & (w < WIN)
    same = hit & (n < CUTS)[:, None] & (chan[:, None] == w // 100) & (row[:, None] == (w % 100) // 10)
    step = w % 10
    own = same & (step == bit[:, None] + 1)
    before = same & (step == 0) & (bit[:, None] == 7)
    after = same & (step == 9) & (bit[:, None] == 0)
    return np.concatenate([own, before, after], 0).astype(jnp.bfloat16)


def frame_rows():
    order = (SINGLE_FRAMES, (1, 3, 5, 7), (2, 4, 6, 8))
    out = np.zeros((384, 32), np.float32)
    for k in range(3):
        for g in range(2):
            for i in range(4):
                at = ((k * 2 + g) * 4 + i) * 16
                out[at : at + 16, g * 12 + order[k][i]] = 1
    return out.astype(jnp.bfloat16)


ROUTES = {"a": "y123W", "b": "CXy123W", "c": "y123W", "d": "CXy123W"}
AFTER = {}
GATES = {"g0": "b", "g1": "d"}
GROUPS = {}
ORDER = (
    "A", "cut", "T1", "TG", "g0", "bC", "F", "C1", "g1", "bX", "dC", "T3", "ay", "C3", "by", "a1", "cy", "dX", "b1",
    "a2", "c1", "dy", "b2", "a3", "c2", "P", "d1", "b3", "aU", "c3", "d2", "bU", "d3", "cU", "dU",
)


def dot(a, b):
    return jnp.dot(a, b, preferred_element_type=jnp.float32)


def dot_nt(a, b):
    return lax.dot_general(a, b, (((1,), (1,)), ((), ())), preferred_element_type=jnp.float32)


def dot_tn(a, b):
    return lax.dot_general(a, b, (((0,), (0,)), ((), ())), preferred_element_type=jnp.float32)


def bf(x):
    return x.astype(jnp.bfloat16)


def f32(x):
    return x.astype(jnp.float32)


def iota(shape, dim):
    return lax.broadcasted_iota(jnp.int32, shape, dim)


def own_columns(rows):
    return ((iota((rows, 384), 1) & 127) >> 3) == (iota((rows, 384), 0) & 15)


def picks_of(picks, i):
    lane = iota((1, 256), 1)
    return picks * bf(jnp.where((lane >= 24 * i) & (lane < 24 * i + 24), 1.0, 0.0))


def shift_up(v):
    return jnp.where((iota(v.shape, 0) & 15) == 15, 0.0, pltpu.roll(v, v.shape[0] - 1, 0))


def shift_down(v):
    return jnp.where((iota(v.shape, 0) & 15) == 0, 0.0, pltpu.roll(v, 1, 0))


def widen(v):
    return bf(jnp.concatenate([v, shift_down(v), shift_up(v)], 1))


def narrow(t):
    return bf(t[:, :256] + shift_up(t[:, 256:512]) + shift_down(t[:, 512:]))


def normalize(x, gain):
    centered = x - jnp.mean(x, -1, keepdims=True)
    inverse = lax.rsqrt(jnp.mean(centered * centered, -1, keepdims=True) + epsilon)
    unit = centered * inverse
    return bf(unit * gain), unit, inverse


def normalize_back(incoming, unit, inverse, gain):
    scaled = incoming * gain
    gain_grad = jnp.sum(incoming * unit, 0, keepdims=True)
    first = jnp.mean(scaled, -1, keepdims=True)
    second = jnp.mean(scaled * unit, -1, keepdims=True)
    return inverse * (scaled - first - unit * second), gain_grad


def halves_mask(width=128):
    lane = iota((1, width), 1)
    return lane < 64


def attention(projected, seen, chance_ref, scale):
    low = halves_mask()
    keep = (bf(jnp.where(low, 1.0, 0.0)), bf(jnp.where(low, 0.0, 1.0)))
    outs = []
    for pair in range(HEADS // 2):
        q = projected[:, pair * 128 : pair * 128 + 128]
        k = projected[:, 512 + pair * 128 : 512 + pair * 128 + 128]
        v = projected[:, 1024 + pair * 128 : 1024 + pair * 128 + 128]
        both = []
        for half in range(2):
            scores = dot_nt(q * keep[half], k) * scale
            if seen is not None:
                scores = jnp.where(seen, scores, masked_score)
            powers = jnp.exp(scores - jnp.max(scores, -1, keepdims=True))
            chance = bf(powers * (1.0 / jnp.sum(powers, -1, keepdims=True)))
            chance_ref[2 * pair + half] = chance
            both.append(dot(chance, v))
        outs.append(jnp.where(low, both[0], both[1]))
    return bf(jnp.concatenate(outs, 1))


def attention_back(grad_mixed, projected, chance_ref, scale):
    low = halves_mask()
    keep = (bf(jnp.where(low, 1.0, 0.0)), bf(jnp.where(low, 0.0, 1.0)))
    grads = ([], [], [])
    for pair in range(HEADS // 2):
        q = projected[:, pair * 128 : pair * 128 + 128]
        k = projected[:, 512 + pair * 128 : 512 + pair * 128 + 128]
        v = projected[:, 1024 + pair * 128 : 1024 + pair * 128 + 128]
        g = grad_mixed[:, pair * 128 : pair * 128 + 128]
        both = ([], [], [])
        for half in range(2):
            chance = chance_ref[2 * pair + half]
            wide = f32(chance)
            grad_chance = dot_nt(g * keep[half], v)
            inner = jnp.sum(wide * grad_chance, -1, keepdims=True)
            grad_scores = bf(wide * (grad_chance - inner))
            both[0].append(dot(grad_scores, k))
            both[1].append(dot_tn(grad_scores, q))
            both[2].append(dot_tn(chance, g))
        for part, factor in zip(range(3), (scale, scale, 1.0)):
            grads[part].append(bf(jnp.where(low, both[part][0], both[part][1]) * factor))
    return jnp.concatenate(grads[0] + grads[1] + grads[2], 1)


def gelu_parts(inner):
    square = inner * inner
    bent = jnp.tanh(gelu_coef * inner * (1.0 + cubic_coef * square))
    half = 0.5 * (1.0 + bent)
    slope = half + 0.5 * inner * (1.0 - bent * bent) * gelu_coef * (1.0 + 3.0 * cubic_coef * square)
    return bf(inner * half), slope


def feed_forward(second, up_ref, down_ref, slope_ref):
    total = None
    for k in range(4):
        columns = slice(k * 512, k * 512 + 512)
        active, slope = gelu_parts(dot(second, up_ref[:, columns]))
        slope_ref[:, columns] = bf(slope)
        part = dot(active, down_ref[columns, :])
        total = part if total is None else total + part
    return total


def feed_forward_back(lowered, up_ref, down_ref, slope_ref):
    total = None
    for k in range(4):
        columns = slice(k * 512, k * 512 + 512)
        grad_inner = bf(dot_nt(lowered, down_ref[columns, :]) * f32(slope_ref[:, columns]))
        part = dot_nt(grad_inner, up_ref[:, columns])
        total = part if total is None else total + part
    return total


def feed_grad_kernel(me, *refs):
    *shares, up, down, near, far, second, incoming, active, grad_inner = refs
    for k in range(4):
        rows = slice(k * 256, k * 256 + 256)
        if len(shares) == 4:
            second[rows, :] = shares[k][0]
            incoming[rows, :] = shares[k][1]
        else:
            second[rows, :] = shares[k][...]
            incoming[rows, :] = shares[4 + k][...]
    half = pl.ds(pl.multiple_of(me[0] * 256, 256), 256)
    up_ref, down_ref = held(up), held(down)
    for rel, out in enumerate((near, far)):
        at = pl.multiple_of((me[1] ^ rel) * 512, 512)
        up_part, down_part = up_ref[:, pl.ds(at, 512)], down_ref[pl.ds(at, 512), :]
        for k in range(4):
            rows = slice(k * 256, k * 256 + 256)
            act, slope = gelu_parts(dot(second[rows, :], up_part))
            active[rows, :] = act
            grad_inner[rows, :] = bf(dot_nt(incoming[rows, :], down_part) * slope)
        up_grad = dot_tn(second[:, half], grad_inner[...])
        for j in range(4):
            out[j * 256 : j * 256 + 256, :] = bf(up_grad[:, j * 128 : j * 128 + 128])
        down_grad = dot_tn(active[...], incoming[:, half])
        for j in range(2):
            out[1024 + j * 512 : 1536 + j * 512, :] = bf(down_grad[:, j * 128 : j * 128 + 128])


def swap_halves(v, bit):
    half = v.shape[1] // 2
    return jnp.where(bit == 1, jnp.concatenate([v[:, half:], v[:, :half]], 1), v)


def swap_quarters(v, quarter):
    v = swap_halves(v, quarter >> 1)
    half = v.shape[1] // 2
    return jnp.concatenate([swap_halves(v[:, :half], quarter & 1), swap_halves(v[:, half:], quarter & 1)], 1)


def put(outs, rel, x_rel, first, last, value):
    if rel < 2:
        outs[0][x_rel, rel, first:last, :] = value
    elif len(outs) == 2:
        outs[1][x_rel, rel & 1, first:last, :] = value
    else:
        outs[1 + x_rel][rel & 1, first:last, :] = value


def put_columns(outs, x_rel, at, value, count):
    rows, width = value.shape[0], value.shape[1] // 4
    for rel in range(4):
        for j in range(width // LANES):
            block = value[:, rel * width + j * LANES : rel * width + (j + 1) * LANES]
            put(outs, rel, x_rel, at + j * rows, at + (j + 1) * rows, bf(block))


def put_rows(outs, x_rel, at, source, row0, rows, quarter):
    size = rows // 4
    blocks = source.shape[1] // LANES
    for rel in range(4):
        first = pl.multiple_of(row0 + (quarter ^ rel) * size, 16)
        for j in range(blocks):
            put(outs, rel, x_rel, at + j * size, at + (j + 1) * size, bf(source[pl.ds(first, size), j * LANES : (j + 1) * LANES]))


def put_attention(outs, normed, grad_projected, mixed, lowered, first_grad, second_grad, mx, quarter):
    heads = dot_tn(swap_halves(normed, mx), swap_quarters(grad_projected, quarter))
    output = dot_tn(swap_halves(mixed, mx), swap_quarters(lowered, quarter))
    gains = (swap_halves(first_grad, mx), swap_halves(second_grad, mx))
    row = iota((16, 128), 0)
    for x_rel in range(2):
        put_columns(outs, x_rel, 0, heads[x_rel * 256 : x_rel * 256 + 256], 3)
        put_columns(outs, x_rel, 768, output[x_rel * 256 : x_rel * 256 + 256], 1)
        block = jnp.zeros((16, 128), jnp.float32)
        for j in range(4):
            at = x_rel * 256 + (j & 1) * 128
            block = jnp.where(row == j, gains[j >> 1][:, at : at + 128], block)
        for rel in range(4):
            put(outs, rel, x_rel, 1024, 1040, bf(block))


def fill_embed(embed, single_ref, pair_ref, is_pair):
    embed[...] = jnp.zeros_like(embed)

    @pl.when(is_pair == 1)
    def _():
        embed[0:600, :] = pair_ref[...]

    @pl.when(is_pair == 0)
    def _():
        embed[0:300, :] = single_ref[...]


def gate_kernel(me, out):
    out[...] = jnp.zeros_like(out)


def slots_kernel(me, pixels, cot_ref, out, last, first, cot):
    cot[...] = f32(cot_ref[...])
    last[...] = bf(cot[pl.ds(7, 72, stride=8), :])
    first[...] = bf(cot[pl.ds(0, 72, stride=8), :])
    for g in range(2):
        for k in range(4):
            single = pixels[g, SINGLE_FRAMES[k]]
            out[g * 4 + k, 0] = single
            out[g * 4 + k, 1] = single
            out[8 + g * 4 + k, 0] = pixels[g, 2 * k + 1]
            out[8 + g * 4 + k, 1] = pixels[g, 2 * k + 2]


def spatial_forward_kernel(
    me, frames, single, pair, gains, heads, output, up, down, picks_ref, wins,
    windows_out, start_out, projected_out, chance_out, mixed_out, resid_out, second_out, slope_out, middle_out,
    embed,
    post,
):
    is_pair = me[2]
    own = own_columns(512)
    picks = picks_ref[...]
    both = [
        jnp.concatenate([frames[(f * 3 + ch) * 128 : (f * 3 + ch) * 128 + 128, :] for ch in range(3)], 1) for f in range(2)
    ]
    cut = None
    for i in range(KERN):
        lift = bf(jnp.where(iota((256, 128), 1) == 8 * (iota((256, 128), 0) >> 4) + i - 1, 1.0, 0.0))
        lifted = jnp.concatenate([dot(lift, frame) for frame in both], 0)
        part = dot(bf(jnp.where(own, lifted, 0.0)), picks_of(picks, i))
        cut = part if cut is None else cut + part
    cuts = [widen(cut[:256]), widen(cut[256:])]
    wins_ref = held(wins)
    windows = bf(dot(cuts[0], wins_ref[0]) + dot(cuts[1], wins_ref[1]))
    windows_out[...] = windows
    post(0)
    fill_embed(embed, held(single), held(pair), is_pair)
    start = dot(windows, embed[...])
    start_out[...] = start
    post(1)
    normed, _, _ = normalize(start, gains[0:1, :])
    projected = bf(dot(normed, held(heads)[...]))
    projected_out[...] = projected
    post(2)
    mixed = attention(projected, None, chance_out, 64**-0.5)
    mixed_out[...] = mixed
    post(3, 4)
    resid = start + dot(mixed, held(output)[...])
    resid_out[...] = resid
    post(5)
    second, _, _ = normalize(resid, gains[1:2, :])
    second_out[...] = second
    middle_out[...] = bf(resid + feed_forward(second, held(up), held(down), slope_out))


def spatial_back_kernel(
    me, incoming_ref, gains, resid_ref, slope, start_in, projected, chance, mixed, windows, up, down, heads, output,
    keep_out, send_near, send_far, start_out,
    grads,
):
    mx, quarter, is_pair = me[0], me[1], me[2]
    outs = (keep_out, send_near, send_far)
    incoming = incoming_ref[...]
    _, unit, inverse = normalize(resid_ref[...], gains[1:2, :])
    back = feed_forward_back(incoming, held(up), held(down), held(slope))
    grad, scale_grad = normalize_back(back, unit, inverse, gains[1:2, :])
    incoming = f32(incoming) + grad
    lowered = bf(incoming)
    grad_mixed = bf(dot_nt(lowered, held(output)[...]))
    grad_projected = attention_back(grad_mixed, held(projected)[...], held(chance), 64**-0.5)
    normed, unit, inverse = normalize(held(start_in)[...], gains[0:1, :])
    back, gain_grad = normalize_back(dot_nt(grad_projected, held(heads)[...]), unit, inverse, gains[0:1, :])
    grad_start = bf(incoming + back)
    start_out[...] = grad_start
    put_attention(outs, normed, grad_projected, held(mixed)[...], lowered, gain_grad, scale_grad, mx, quarter)
    grads[...] = dot_tn(held(windows)[...], swap_halves(grad_start, mx))
    pair_part = jnp.where(is_pair == 1, 1.0, 0.0)
    single_part = 1.0 - pair_part
    for x_rel in range(2):
        for rel in range(4):
            for j in range(2):
                at = x_rel * 256 + j * 128
                first = pl.multiple_of((quarter ^ rel) * 80, 16)
                put(outs, rel, x_rel, 1040 + j * 80, 1120 + j * 80, bf(grads[pl.ds(first, 80), at : at + 128] * single_part))
                first = pl.multiple_of((quarter ^ rel) * 160, 16)
                put(outs, rel, x_rel, 1200 + j * 160, 1360 + j * 160, bf(grads[pl.ds(first, 160), at : at + 128] * pair_part))
            put(outs, rel, x_rel, 1520, SPACE_ROWS, jnp.zeros((SPACE_ROWS - 1520, 128), jnp.bfloat16))


def pixel_fold_kernel(me, start_ref, single_ref, pair_ref, picks_ref, wins_ref, pixel_out, embed):
    fill_embed(embed, single_ref, pair_ref, me[2])
    window_grads = bf(dot_nt(start_ref[...], embed[...]))
    own = own_columns(512)
    picks = picks_ref[...]
    folded = jnp.concatenate([narrow(dot_nt(window_grads, wins_ref[f])) for f in range(2)], 0)
    both = [None, None]
    for i in range(KERN):
        spread = bf(jnp.where(own, dot_nt(folded, picks_of(picks, i)), 0.0))
        lift = bf(jnp.where(iota((128, 256), 0) == 8 * (iota((128, 256), 1) >> 4) + i - 1, 1.0, 0.0))
        for f in range(2):
            part = dot(lift, spread[f * 256 : f * 256 + 256])
            both[f] = part if both[f] is None else both[f] + part
    for f in range(2):
        for ch in range(3):
            pixel_out[(f * 3 + ch) * 128 : (f * 3 + ch) * 128 + 128, :] = bf(both[f][:, ch * 128 : ch * 128 + 128])


def slots_seen():
    def parts(dim):
        t = iota((256, 256), dim)
        index = (t >> 4) & 3
        slot = jnp.where(t < 128, jnp.where(index == 0, 0, index + 4), index + 1)
        return ((t >> 2) & 16) | (t & 15), slot

    here, query = parts(0)
    there, key = parts(1)
    near = (key <= query) & (((key < VSTEPS) & (query < VSTEPS)) | (key == query))
    return (here == there) & near


def cotangent_kernel(
    me, cot_ref, edges_ref, single_ref, pair_ref, picks_ref, wins_ref, rows_ref, cut_out, grad_out,
    unpatch_one, unpatch_two, cot,
):
    fill_unpatch(unpatch_one, unpatch_two, single_ref, pair_ref)
    own = own_columns(384)
    picks = picks_ref[...]
    cot[...] = f32(cot_ref[...])
    places = rows_ref[...]
    cut = None
    for i in range(KERN):
        parts = []
        for ch in range(3):
            if i == 0:
                parts.append(edges_ref[pl.ds(ch, 24, stride=3), :])
            elif i == KERN - 1:
                parts.append(edges_ref[pl.ds(72 + ch, 24, stride=3), :])
            else:
                parts.append(cot[pl.ds(ch * 8 + i - 1, 24, stride=24), :])
        row = jnp.concatenate([jnp.concatenate(parts, 1), jnp.zeros((8, 384), jnp.float32)], 0)
        spread = bf(jnp.where(own, dot(places, bf(row)), 0.0))
        part = dot(spread, picks_of(picks, i))
        cut = part if cut is None else cut + part
    wide = widen(cut)
    one = bf(dot(wide[:128], wins_ref[0, :, 0:384]))
    two = bf(dot(wide[128:256], wins_ref[0]) + dot(wide[256:], wins_ref[1]))
    cut_out[:, 0:384] = one
    cut_out[:, 384:1024] = two
    grad_out[...] = jnp.concatenate([dot(one, unpatch_one[...]), dot(two, unpatch_two[...])], 0)


def fill_unpatch(unpatch_one, unpatch_two, single_ref, pair_ref):
    unpatch_one[...] = jnp.zeros_like(unpatch_one)
    unpatch_two[...] = jnp.zeros_like(unpatch_two)
    unpatch_one[0:300, :] = single_ref[...]
    unpatch_two[0:600, :] = pair_ref[...]


def rebuilt_kernel(me, final_ref, single_ref, pair_ref, picks_ref, wins_ref, sums_ref, rebuilt_out, rims_out, unpatch_one, unpatch_two):
    fill_unpatch(unpatch_one, unpatch_two, single_ref, pair_ref)
    own = own_columns(384)
    picks = picks_ref[...]
    one = bf(dot_nt(final_ref[0:128, :], unpatch_one[...]))
    two = bf(dot_nt(final_ref[128:256, :], unpatch_two[...]))
    folded = jnp.concatenate(
        [
            narrow(dot_nt(one, wins_ref[0, :, 0:384])),
            narrow(dot_nt(two, wins_ref[0])),
            narrow(dot_nt(two, wins_ref[1])),
        ],
        0,
    )
    sums = sums_ref[...]
    for i in range(KERN):
        spread = bf(jnp.where(own, dot_nt(folded, picks_of(picks, i)), 0.0))
        row = dot(sums, spread)
        if i == 0:
            rims_out[0:32, :] = bf(row)
        elif i == KERN - 1:
            rims_out[32:64, :] = bf(row)
        else:
            for ch in range(3):
                rebuilt_out[pl.ds(ch * 8 + i - 1, 24, stride=24), :] = row[:24, ch * 128 : ch * 128 + 128]


def temporal_kernel(
    me, middle_ref, incoming_in, gains, heads, output, up, down,
    both_out, grad_out, mixed_out, final_out, projected_out, lowered_out, normed_out, gain_out,
    slope_ref, chance_ref,
    post,
):
    middle = f32(middle_ref[...])
    normed, first_unit, first_inverse = normalize(middle, gains[2:3, :])
    normed_out[...] = normed
    post(6)
    heads_ref = held(heads)
    projected = bf(dot(normed, heads_ref[...]))
    mixed = attention(projected, slots_seen(), chance_ref, 64**-0.5)
    mixed_out[...] = mixed
    post(2)
    output_ref = held(output)
    resid = middle + dot(mixed, output_ref[...])
    second, unit, inverse = normalize(resid, gains[3:4, :])
    incoming = held(incoming_in)[...]
    lowered = bf(incoming)
    both_out[0] = second
    both_out[1] = lowered
    up_ref, down_ref = held(up), held(down)
    final_out[...] = bf(resid + feed_forward(second, up_ref, down_ref, slope_ref))
    post(3)
    back = feed_forward_back(lowered, up_ref, down_ref, slope_ref)
    grad, scale_grad = normalize_back(back, unit, inverse, gains[3:4, :])
    incoming = incoming + grad
    lowered = bf(incoming)
    lowered_out[...] = lowered
    post(5)
    grad_mixed = bf(dot_nt(lowered, output_ref[...]))
    grad_projected = attention_back(grad_mixed, projected, chance_ref, 64**-0.5)
    projected_out[...] = grad_projected
    post(4)
    back, gain_grad = normalize_back(dot_nt(grad_projected, heads_ref[...]), first_unit, first_inverse, gains[2:3, :])
    gain_out[0:8, :] = jnp.broadcast_to(gain_grad, (8, 512))
    gain_out[8:16, :] = jnp.broadcast_to(scale_grad, (8, 512))
    grad_out[...] = bf(incoming + back)


def temporal_grad_kernel(
    me, normed_ref, projected_ref, mixed_ref, lowered_ref, gain_ref, final_ref, cut_ref,
    keep_out, send_near, send_far,
    grads,
):
    mx, quarter = me[0], me[1]
    outs = (keep_out, send_near, send_far)
    put_attention(
        outs, normed_ref[...], projected_ref[...], mixed_ref[...], lowered_ref[...], gain_ref[0:1, :], gain_ref[8:9, :],
        mx, quarter,
    )
    final = swap_halves(final_ref[...], mx)
    grads[0:384, :] = dot_tn(cut_ref[:, 0:384], final[:128])
    grads[384:1024, :] = dot_tn(cut_ref[:, 384:1024], final[128:])
    for x_rel in range(2):
        for rel in range(4):
            for j in range(2):
                at = x_rel * 256 + j * 128
                first = pl.multiple_of((quarter ^ rel) * 96, 16)
                put(outs, rel, x_rel, 1040 + j * 96, 1136 + j * 96, bf(grads[pl.ds(first, 96), at : at + 128]))
                first = pl.multiple_of(384 + (quarter ^ rel) * 160, 16)
                put(outs, rel, x_rel, 1232 + j * 160, 1392 + j * 160, bf(grads[pl.ds(first, 160), at : at + 128]))
            put(outs, rel, x_rel, 1552, TIME_ROWS, jnp.zeros((TIME_ROWS - 1552, 128), jnp.bfloat16))


TIME_ROWS = 1600
SPACE_ROWS = 1536


class Leaving:
    def __init__(self, semaphores):
        self.semaphores, self.copies = semaphores, []

    def send(self, source, out):
        copy = pltpu.make_async_copy(source, out, self.semaphores.at[len(self.copies)])
        copy.start()
        self.copies.append(copy)

    def wait(self):
        for copy in self.copies:
            copy.wait()


def unpack_feed(me, sources, first, up_out, down_out, up, down, leaving):
    for rel, source in enumerate(sources):
        at = pl.multiple_of((me[1] ^ rel) * 512, 512)
        for j in range(2):
            rows = slice(first + 1024 + j * 512, first + 1536 + j * 512)
            down[pl.ds(at, 512), j * 128 : j * 128 + 128] = f32(source[rows, :])
        leaving.send(down.at[pl.ds(at, 512), :], down_out.at[pl.ds(at, 512), :])
    for rel, source in enumerate(sources):
        at = pl.multiple_of((me[1] ^ rel) * 512, 512)
        for j in range(4):
            rows = slice(first + j * 256, first + j * 256 + 256)
            up[:, pl.ds(pl.multiple_of(at + j * 128, 128), 128)] = f32(source[rows, :])
        leaving.send(up.at[:, pl.ds(at, 512)], up_out.at[:, pl.ds(at, 512)])


def unpack_rest(
    me, sources, first, one, two, heads_out, output_out, gains_out, single_out, pair_out, heads, output, gains, single, pair,
    leaving,
):
    for rel, source in enumerate(sources):
        quarter = me[1] ^ rel
        for j in range(3):
            at = pl.multiple_of(quarter * 384 + j * 128, 128)
            heads[:, pl.ds(at, 128)] = f32(source[first + j * 256 : first + j * 256 + 256, :])
        at = pl.multiple_of(quarter * 384, 128)
        leaving.send(heads.at[:, pl.ds(at, 384)], heads_out.at[:, pl.ds(at, 384)])
    gains[...] = f32(sources[0][first + 1024 : first + 1040, :])
    leaving.send(gains, gains_out)
    for rel, source in enumerate(sources):
        quarter = me[1] ^ rel
        at = pl.multiple_of(quarter * 128, 128)
        output[:, pl.ds(at, 128)] = f32(source[first + 768 : first + 1024, :])
        for j in range(2):
            row = first + 1040 + j * one
            at = pl.multiple_of(quarter * one, 16)
            single[pl.ds(at, one), j * 128 : j * 128 + 128] = f32(source[row : row + one, :])
            row = first + 1040 + 2 * one + j * two
            at = pl.multiple_of(quarter * two, 16)
            pair[pl.ds(at, two), j * 128 : j * 128 + 128] = f32(source[row : row + two, :])
    leaving.send(output, output_out)
    single_out[...] = single[0:300, :]
    leaving.send(pair.at[0:600, :], pair_out)


def unpack_kernel(me, *refs, feed, rest):
    sources, refs = refs[:4], refs[4:]
    leaving = Leaving(refs[-1])
    many = 2 * (feed is not None) + 5 * (rest is not None)
    outs, scratch = list(refs[:many]), list(refs[many:-1])
    if feed is not None:
        unpack_feed(me, sources, feed, *outs[:2], *scratch[:2], leaving)
        outs, scratch = outs[2:], scratch[2:]
    if rest is not None:
        unpack_rest(me, sources, *rest, *outs, *scratch, leaving)
    leaving.wait()


class Arriving:
    def __init__(self, source, held, semaphore, line):
        self.held = held
        self.copy = pltpu.make_async_copy(source, held, semaphore)
        self.line = line
        line.append(self)
        self.started = False
        if len(line) <= 6:
            self.start()

    def start(self):
        if not self.started:
            self.started = True
            self.copy.start()

    def ready(self):
        if self.copy is not None:
            self.start()
            self.copy.wait()
            self.copy = None
            for other in self.line:
                if not other.started:
                    other.start()
                    break
        return self.held


def held(ref):
    return ref.ready() if isinstance(ref, Arriving) else ref


def call(
    kernel, name, outs, args, scratch=(), after=(), vmem=60, micros=1.0, gated=(), leave=(), enter=(), post=()
):
    any_space = pl.BlockSpec(memory_space=pl.ANY)
    whole = pl.BlockSpec(memory_space=pltpu.VMEM)
    count, made = len(args), len(outs)
    waits = len(after) + len(gated)
    held = [pltpu.VMEM(args[k].shape, args[k].dtype) for k in enter]
    kept = [pltpu.VMEM(*outs[k]) for k in post]
    own = [pltpu.VMEM(s, d) for s, d in scratch]
    if leave:
        own.append(pltpu.SemaphoreType.DMA((12,)))

    def body(*refs):
        ins = list(refs[:count])
        results = list(refs[count + waits : count + waits + made])
        rest = refs[count + waits + made + len(gated) :]
        mine, rest = rest[: len(own)], rest[len(own) :]
        copies = {}
        line = []
        for n, k in enumerate(enter):
            ins[k] = Arriving(ins[k], rest[n], rest[-2].at[n], line)
        if post:
            places = {}
            for n, k in enumerate(post):
                places[k] = (rest[len(enter) + n], results[k], n)
                results[k] = rest[len(enter) + n]

            def go(*which):
                for k in which:
                    source, out, n = places[k]
                    copies[k] = pltpu.make_async_copy(source, out, rest[-1].at[n])
                    copies[k].start()

            kernel(*ins, *results, *mine, post=go)
            go(*[k for k in post if k not in copies])
        else:
            kernel(*ins, *results, *mine)
        for k in enter:
            ins[k].ready()
        for copy in copies.values():
            copy.wait()

    return pl.pallas_call(
        body,
        name=name,
        out_shape=[jax.ShapeDtypeStruct(s, d) for s, d in outs] + [jax.ShapeDtypeStruct(a.shape, a.dtype) for a in gated],
        in_specs=[pl.BlockSpec(memory_space=pltpu.SMEM)]
        + [any_space if k in enter else whole for k in range(1, count)]
        + [any_space] * waits,
        out_specs=[any_space if k in leave or k in post else whole for k in range(made)] + [any_space] * len(gated),
        scratch_shapes=own
        + held
        + kept
        + [pltpu.SemaphoreType.DMA((max(len(enter), 1),)), pltpu.SemaphoreType.DMA((max(len(post), 1),))],
        input_output_aliases={count + len(after) + k: made + k for k in range(len(gated))},
        compiler_params=pltpu.CompilerParams(vmem_limit_bytes=vmem * MIB),
        cost_estimate=pl.CostEstimate(flops=int(micros * MICRO), bytes_accessed=0, transcendentals=0),
    )(*args, *after, *gated)


def flips(size, bit):
    return [(i, i ^ bit) for i in range(size)]


def total_of(*refs):
    out = f32(refs[0])
    for r in refs[1:]:
        out = out + f32(r)
    return bf(out)


def split_core_kernel(me, keep, *refs, first, count):
    got, (near, far) = refs[:count], refs[count:]
    for half, out in enumerate((near, far)):
        for j in range(2):
            x, y = (half, j) if first == 0 else (j, half)
            came = got[0][x, y] if count == 1 else got[x][y]
            out[j] = total_of(keep[x, y], came)


def split_kernel(me, keep, got, near, far):
    for half, out in enumerate((near, far)):
        out[...] = total_of(keep[half], got[half])


def sum_kernel(me, keep, got, out):
    out[...] = total_of(keep[...], got[...])


def merge_kernel(me, *refs, place, count):
    others, keep, got = list(refs[: count - 1]), refs[count - 1], refs[count]
    outs, whole = refs[count + 1 : -1], refs[-1]
    at = 0
    for k in range(count):
        if k == place:
            rows = keep.shape[0]
            whole[at : at + rows, :] = total_of(keep[...], got[...])
        else:
            ref = others.pop(0)
            rows = ref.shape[0]
            whole[at : at + rows, :] = ref[...]
        at += rows
    if len(outs) == 1:
        outs[0][...] = whole[...]
    else:
        size = whole.shape[0] // 4
        for rel in range(4):
            outs[rel][...] = whole[pl.ds(pl.multiple_of(((me[3] >> 2) ^ rel) * size, 16), size), :]


def quarter_sum_kernel(me, a, b, c, d, out):
    out[...] = total_of(a[...], b[...], c[...], d[...])


def gather_kernel(me, a, b, c, d, out):
    size = a.shape[0]
    for rel, ref in enumerate((a, b, c, d)):
        out[pl.ds(pl.multiple_of(((me[3] >> 2) ^ rel) * size, 16), size), :] = ref[...]


def ends_kernel(me, total, got, out):
    place = me[3] >> 2
    at_end = (place == 0) | (place == 3)

    @pl.when(at_end)
    def _():
        out[...] = got[...]

    @pl.when(jnp.logical_not(at_end))
    def _():
        out[...] = total[...]


def pass_gate(kernel, name, outs, args, after, gated, scratch=()):
    ahead = [v for c in gated for v in c.far]
    got = call(kernel, name, outs, args, scratch, after, 24, 1.5, ahead)
    rest = got[len(outs) :]
    for c in gated:
        c.far, rest = rest[: len(c.far)], rest[len(c.far) :]
        c.launch()
    return got[: len(outs)]


class Chain:
    def __init__(self, name, me, near=None, far=None):
        self.name, self.route, self.me = name, ROUTES[name], me
        self.near, self.far = near, far
        self.at = 0

    def launch(self):
        grp, rows = lax.axis_size("grp"), lax.axis_size("rows")
        step = self.route[self.at]
        line = [[z * 4 + i for i in range(4)] for z in range(rows // 4)]
        if step == "C":
            self.got = [lax.ppermute(v, "rows", flips(rows, 1)) for v in self.far]
        elif step in "Xx":
            self.got = lax.ppermute(self.far, "grp", flips(grp, grp // 2))
        elif step in "Yy":
            self.got = lax.ppermute(self.far, "rows", flips(rows, 2))
        elif step == "R":
            self.got = [lax.ppermute(self.parts[k], "rows", flips(rows, 4 * k)) for k in (1, 2, 3)]
        elif step == "G":
            self.got = [lax.ppermute(self.parts[0], "rows", flips(rows, 4 * k)) for k in (1, 2, 3)]
        elif step in "PQ":
            self.got = lax.ppermute(self.total, "rows", flips(rows, 4 if step == "P" else 8))
        elif step == "1":
            pairs = list(zip(line[0] + line[3], line[1] + line[2]))
            self.got = lax.ppermute(self.total, "rows", pairs)
        elif step == "2":
            pairs = list(zip(line[1] + line[2], line[2] + line[1]))
            self.got = lax.ppermute(self.total, "rows", pairs)
        elif step == "3":
            pairs = list(zip(line[1] + line[2], line[0] + line[3]))
            self.got = lax.ppermute(self.total, "rows", pairs)
        elif step == "W":
            beside = lax.ppermute(self.total, "rows", flips(rows, 2))
            core = flips(rows, 1)
            self.got = [beside, lax.ppermute(self.total, "rows", core), lax.ppermute(beside, "rows", core)]

    def advance(self, after, gated, chains):
        step, then = self.route[self.at], self.route[self.at + 1 : self.at + 2]
        b16 = jnp.bfloat16

        def run(kernel, outs, args, scratch=()):
            return pass_gate(kernel, self.name + step, [(shape, b16) for shape in outs], [self.me, *args], after, gated, scratch)

        self.at += 1
        if step == "C":
            kernel = functools.partial(split_core_kernel, first=0 if then == "X" else 1, count=len(self.got))
            n = self.near.shape[2]
            self.near, self.far = run(kernel, [(2, n, 128)] * 2, [self.near, *self.got])
            token = self.near
        elif step in "XY":
            n = self.near.shape[1]
            self.near, self.far = run(split_kernel, [(n, 128)] * 2, [self.near, self.got])
            token = self.near
        elif step in "xy":
            group = next((g for g in GROUPS if self.name in GROUPS[g]), self.name)
            names = GROUPS.get(group, self.name)
            others = [chains[c].total for c in names if c != self.name and c in chains and hasattr(chains[c], "total")]
            n = self.near.shape[0]
            if len(others) < len(names) - 1:
                (self.total,) = run(sum_kernel, [(n, 128)], [self.near, self.got])
                return self.total
            n += sum(t.shape[0] for t in others)
            kernel = functools.partial(merge_kernel, place=names.index(self.name), count=len(names))
            shapes = [(n // 4, 128)] * 4 if (then if group == self.name else ROUTES[group][0]) == "R" else [(n, 128)]
            outs = run(kernel, shapes, [*others, self.near, self.got], [((n, 128), b16)])
            if group != self.name:
                chains[group] = Chain(group, self.me)
            chains[group].parts = outs
            chains[group].total = outs[0]
            chains[group].launch()
            return outs[0]
        elif step in "12PQ":
            (self.total,) = run(sum_kernel, [self.total.shape], [self.total, self.got])
            token = self.total
        elif step == "3":
            (self.total,) = run(ends_kernel, [self.total.shape], [self.total, self.got])
            token = self.total
        elif step == "R":
            self.parts = run(quarter_sum_kernel, [self.parts[0].shape], [self.parts[0], *self.got])
            token = self.parts[0]
        elif step == "G":
            n = self.parts[0].shape[0] * 4
            (self.total,) = run(gather_kernel, [(n, 128)], [self.parts[0], *self.got])
            token = self.total
        self.launch()
        return token

    def result(self):
        return [self.total, *self.got]


def finish_grp(values, dims):
    grp = lax.axis_size("grp")
    me = lax.axis_index("grp")
    bit = grp // 4
    while bit:
        mine = (me // bit) % 2
        out = []
        for v, dim in zip(values, dims):
            half = v.shape[dim] // 2
            near = lax.dynamic_slice_in_dim(v, mine * half, half, dim)
            far = lax.dynamic_slice_in_dim(v, (1 - mine) * half, half, dim)
            out.append(near + f32(lax.ppermute(bf(far), "grp", flips(grp, bit))))
        values = out
        bit //= 2
    return values


def on_device(
    pixels,
    cotangent,
    embed_single,
    embed_pair,
    spatial_gain,
    spatial_heads,
    spatial_output,
    spatial_scale,
    spatial_upward,
    spatial_down,
    temporal_gain,
    temporal_heads,
    temporal_output,
    temporal_scale,
    temporal_upward,
    temporal_down,
    unpatch_single,
    unpatch_pair,
):
    groups, frames = pixels.shape[:2]
    rows = lax.axis_size("rows")
    assert groups * 8 == rows == GRID and frames == 12 and pixels.shape[3] == STRIDE
    grp = lax.axis_size("grp")
    at = lax.axis_index("rows")
    core, along_y = at & 1, (at >> 1) & 1
    me = jnp.stack(
        [
            lax.axis_index("grp") // (grp // 2),
            core * 2 + along_y,
            jnp.where(at >= 8, 1, 0),
            at,
        ]
    ).astype(jnp.int32)
    picks = jnp.asarray(column_picks())
    wins = jnp.asarray(np.stack([window_picks(0, 640), window_picks(300, 640)]))
    places = frame_rows()
    sums = jnp.asarray(places.T)
    places = jnp.asarray(places)
    gains = f32(jnp.stack([spatial_gain, spatial_scale, temporal_gain, temporal_scale]))

    sent, last, first = call(
        slots_kernel,
        "slots",
        [((16, 2, CHAN, STRIDE, 128), jnp.bfloat16), ((72, 128), jnp.bfloat16), ((72, 128), jnp.bfloat16)],
        [me, pixels, cotangent.reshape(576, 128)],
        [((576, 128), jnp.float32)],
        vmem=60,
    )
    got = lax.all_to_all(sent, "rows", 0, 0)
    images = jnp.transpose(got, (1, 2, 0, 3, 4)).reshape(2 * CHAN * 128, 128)

    up = [(i, i + 1) for i in range(rows - 1)]
    down = [(i + 1, i) for i in range(rows - 1)]
    above = lax.ppermute(last, "rows", up)
    below = lax.ppermute(first, "rows", down)
    edges = f32(jnp.concatenate([above, below], 0))

    b16, w32 = jnp.bfloat16, jnp.float32
    half = 256
    made, chains = {}, {}
    token = []

    def start(name, keep, send):
        chains[name] = Chain(name, me, keep, send)
        if name not in "".join(GATES.values()):
            chains[name].launch()

    def pieces(count):
        return [((2, 2, count, 128), b16)] + [((2, count, 128), b16)] * 2

    def shared(v):
        core = flips(rows, 1)
        across = lax.ppermute(v, "grp", flips(grp, grp // 2))
        return [v, lax.ppermute(v, "rows", core), across, lax.ppermute(across, "rows", core)]

    def feed_grads(name, label, shares, up_weight, down_weight):
        near, far = call(
            feed_grad_kernel,
            label,
            [((2048, 128), b16)] * 2,
            [me, *shares, up_weight, down_weight],
            [((1024, 512), b16)] * 4,
            after=token,
            vmem=26,
            micros=7,
        )
        start(name, near, far)
        return near

    def cut():
        out = call(
            cotangent_kernel,
            "cotangent_windows",
            [((128, 1024), b16), ((256, 512), w32)],
            [me, cotangent.reshape(576, 128), edges, unpatch_single.T, unpatch_pair.T, picks, wins, places],
            [((384, 512), b16), ((640, 512), b16), ((576, 128), w32)],
            after=token,
            micros=5,
        )
        made["cut"] = out
        return out[0]

    def spatial():
        out = call(
            spatial_forward_kernel,
            "spatial_forward",
            [
                ((256, 640), b16),
                ((256, 512), w32),
                ((256, 1536), b16),
                ((8, 256, 256), b16),
                ((256, 512), b16),
                ((256, 512), w32),
                ((256, 512), b16),
                ((256, 2048), b16),
                ((256, 512), b16),
            ],
            [me, images, embed_single, embed_pair, gains, spatial_heads, spatial_output, spatial_upward, spatial_down, picks, wins],
            [((640, 512), b16)],
            after=token + [edges],
            vmem=60,
            enter=(10, 2, 3, 5, 6, 7, 8),
            post=(0, 1, 2, 3, 4, 5, 7),
            micros=13,
        )
        made["spatial"] = out
        made["middle"] = lax.all_to_all(out[8].reshape(16, 16, 512), "rows", 0, 0).reshape(256, 512)
        made["seconds"] = shared(out[6])
        return out[6]

    def temporal():
        both, grad_middle, *rest = call(
            temporal_kernel,
            "temporal",
            [
                ((2, 256, 512), b16),
                ((256, 512), b16),
                ((256, 512), b16),
                ((256, 512), b16),
                ((256, 1536), b16),
                ((256, 512), b16),
                ((256, 512), b16),
                ((16, 512), w32),
            ],
            [me, made["middle"], made["cut"][1], gains, temporal_heads, temporal_output, temporal_upward, temporal_down],
            [((256, 2048), b16), ((8, 256, 256), b16)],
            after=token + made["seconds"][1:],
            vmem=60,
            enter=(4, 5, 6, 7, 2),
            post=(2, 3, 4, 5, 6),
            micros=13,
        )
        made["temporal"] = rest
        made["grad_middle"] = lax.all_to_all(grad_middle.reshape(16, 16, 512), "rows", 0, 0).reshape(256, 512)
        made["temporal shares"] = shared(both)
        return rest[5]

    def temporal_grads():
        mixed, final, grad_projected, lowered, normed, gain_grads = made["temporal"]
        keep, *send = call(
            temporal_grad_kernel,
            "temporal_grads",
            pieces(TIME_ROWS),
            [me, normed, grad_projected, mixed, lowered, gain_grads, final, made["cut"][0]],
            [((1024, 512), w32)],
            after=token,
            vmem=60,
            micros=4,
        )
        start("b", keep, send)
        return keep

    def temporal_feed():
        return feed_grads("a", "temporal_feed", made["temporal shares"], temporal_upward, temporal_down)

    def back():
        windows, first, projected, chance, mixed, resid, _, slope, _ = made["spatial"]
        made["grads in"] = shared(made["grad_middle"])
        keep, *send, grad_start = call(
            spatial_back_kernel,
            "spatial_back",
            pieces(SPACE_ROWS) + [((256, 512), b16)],
            [
                me, made["grad_middle"], gains, resid, slope, first, projected, chance, mixed, windows, spatial_upward,
                spatial_down, spatial_heads, spatial_output,
            ],
            [((640, 512), w32)],
            after=token,
            enter=(12, 5, 8, 9),
            micros=12,
        )
        made["grad_start"] = grad_start
        start("d", keep, send)
        return grad_start

    def spatial_feed():
        return feed_grads("c", "spatial_feed", made["seconds"] + made["grads in"], spatial_upward, spatial_down)

    def fold_pixels():
        (frames_out,) = call(
            pixel_fold_kernel,
            "pixel_fold",
            [((768, 128), b16)],
            [me, made["grad_start"], embed_single, embed_pair, picks, wins],
            [((640, 512), b16)],
            after=token,
            vmem=48,
            micros=7,
        )
        sent = jnp.transpose(frames_out.reshape(2, CHAN, GRID, STRIDE, 128), (2, 0, 1, 3, 4))
        made["pixels"] = lax.all_to_all(sent, "rows", 0, 0)
        return frames_out

    def fold_rebuilt():
        whole, rims = call(
            rebuilt_kernel,
            "rebuilt_fold",
            [((576, 128), w32), ((64, 384), b16)],
            [me, made["temporal"][1], unpatch_single.T, unpatch_pair.T, picks, wins, sums],
            [((384, 512), b16), ((640, 512), b16)],
            after=token,
            micros=5,
        )
        top = rims[0:24].reshape(2, 12, CHAN, 1, 128)
        bottom = rims[32:56].reshape(2, 12, CHAN, 1, 128)
        made["rebuilt"] = whole, lax.ppermute(bottom, "rows", up), lax.ppermute(top, "rows", down)
        return rims

    def unpack(name):
        feed = 0 if name in "act" else None
        rest = {"b": (0, 96, 160), "d": (0, 80, 160), "t": (2048, 96, 160)}.get(name)
        outs, scratch, leave = [], [], []
        if feed is not None:
            outs += [((half, 2048), w32), ((2048, half), w32)]
            scratch += outs
            leave += [0, 1]
        if rest is not None:
            leave += [len(outs) + k for k in (0, 1, 2, 4)]
            some = [((half, 1536), w32), ((half, 512), w32), ((16, 128), w32)]
            outs += some + [((300, half), w32), ((600, half), w32)]
            scratch += some + [((4 * rest[1], half), w32), ((4 * rest[2], half), w32)]
        kernel = functools.partial(unpack_kernel, feed=feed, rest=rest)
        made[name] = call(kernel, "unpack_" + name, outs, [me, *chains[name].result()], scratch, token, 48, 3, (), leave)
        return chains[name].result()[1]

    work = {
        "cut": cut, "A": spatial, "T1": temporal, "T3": temporal_feed, "TG": temporal_grads, "C1": back, "C3": spatial_feed,
        "F": fold_rebuilt, "P": fold_pixels,
    }
    for step in ORDER:
        if step in work:
            out = work[step]()
        elif step[1] == "U":
            out = unpack(step[0])
        else:
            gated = [chains[c] for c in GATES.get(step, "")]
            ready = {"G": lambda: made["grad_middle"], "x": lambda: made["grads in"][2], "t": lambda: made["temporal shares"][2],
                     "r": lambda: made["rebuilt"][1], "s": lambda: made["rebuilt"][2]}
            extra = [ready[c]() if c in ready else chains[c].got for c in AFTER.get(step, "")]
            if step[0] == "g":
                out = pass_gate(gate_kernel, "gate", [((8, 128), w32)], [me], token + extra, gated)[0]
            else:
                out = chains[step[0]].advance(token + extra, gated, chains)
        token[:] = [out]

    got = f32(made["pixels"])
    singles = got[:8, 0].reshape(2, 4, CHAN, STRIDE, 128)
    pairs = got[8:].reshape(2, 8, CHAN, STRIDE, 128)
    pixel_gradient = jnp.concatenate([singles[:, :1], pairs, singles[:, 1:]], 1)

    whole, from_above, from_below = made["rebuilt"]
    gap = jnp.zeros((2, 12, CHAN, STRIDE - 2, 128), w32)
    rebuilt = whole.reshape(2, 12, CHAN, STRIDE, 128) + jnp.concatenate([f32(from_above), gap, f32(from_below)], 3)

    t_up, t_down, t_heads, t_output, t_gains, un_single, un_pair = made.get("t") or made["a"] + made["b"]
    s_up, s_down = made["c"]
    s_heads, s_output, s_gains, em_single, em_pair = made["d"]
    grads = [
        em_single,
        em_pair,
        s_gains[0:2].reshape(256),
        s_heads,
        s_output,
        s_gains[2:4].reshape(256),
        s_up,
        s_down,
        t_gains[0:2].reshape(256),
        t_heads,
        t_output,
        t_gains[2:4].reshape(256),
        t_up,
        t_down,
        un_single.T,
        un_pair.T,
    ]
    dims = [1, 1, 0, 0, 0, 0, 0, 1, 0, 0, 0, 0, 0, 1, 0, 0]
    return (rebuilt, pixel_gradient, *finish_grp(grads, dims))


def solution(mesh):
    in_specs = (
        P("grp", None, None, "rows", None),
        P("grp", None, None, "rows", None),
    ) + (P(),) * 16
    out_specs = (
        P("grp", None, None, "rows", None),
        P("grp", None, None, "rows", None),
        P(None, "grp"),
        P(None, "grp"),
        P("grp"),
        P("grp", None),
        P("grp", None),
        P("grp"),
        P("grp", None),
        P(None, "grp"),
        P("grp"),
        P("grp", None),
        P("grp", None),
        P("grp"),
        P("grp", None),
        P(None, "grp"),
        P("grp", None),
        P("grp", None),
    )
    return jax.shard_map(
        on_device, mesh=mesh, in_specs=in_specs, out_specs=out_specs, check_vma=False
    )
```
